32 devices in a mesh: dp: 8 (over y, x, core), chan: 4 (over z).
Axes of the slice: x: 2, y: 2, z: 4, core: 2. Of those that a mesh axis runs over, the one named last changes fastest.
Arguments:
- hidden_in: bfloat16 [8, 1024, 768], P('dp', None, 'chan'), may hold values from -6 to 6
- halves: int32 [8, 2], P('dp'), may hold values from 1 to 1024, as said below
- norm1_gain: float32 [768], P('chan'), may hold values from 0.25 to 1.75
- in_proj: bfloat16 [768, 3, 768], P(None, None, 'chan'), may hold values from -0.21875 to 0.21875
- short_taps: float32 [3, 3, 768], P(None, None, 'chan'), may hold values from -3 to 3
- cond_taps: float32 [3, 768], P(None, 'chan'), may hold values from -3 to 3
- filter_in: float32 [33, 64], replicated, may hold values from -2 to 2
- filter_bias: float32 [64], replicated, may hold values from -3.140625 to 3.140625
- filter_out: float32 [64, 768], P(None, 'chan'), may hold values from -0.75 to 0.75
- decay_rate: float32 [768], P('chan'), may hold values from 0.0009765625 to 0.05
- out_proj: bfloat16 [768, 768], P(None, 'chan'), may hold values from -0.21875 to 0.21875
- norm2_gain: float32 [768], P('chan'), may hold values from 0.25 to 1.75
- w_gate: bfloat16 [768, 3072], P(None, 'chan'), may hold values from -0.21875 to 0.21875
- w_up: bfloat16 [768, 3072], P(None, 'chan'), may hold values from -0.21875 to 0.21875
- w_down: bfloat16 [3072, 768], P('chan'), may hold values from -0.15625 to 0.15625
- out_grad: bfloat16 [8, 1024, 768], P('dp', None, 'chan'), may hold values from -6 to 6
Outputs:
- output: float32 [8, 1024, 768], P('dp', None, 'chan')
- input_grad: float32 [8, 1024, 768], P('dp', None, 'chan')
- norm1_gain_grad: float32 [768], P('chan')
- in_proj_grad: float32 [768, 3, 768], P(None, None, 'chan')
- short_taps_grad: float32 [3, 3, 768], P(None, None, 'chan')
- cond_taps_grad: float32 [3, 768], P(None, 'chan')
- filter_in_grad: float32 [33, 64], replicated
- filter_bias_grad: float32 [64], replicated
- filter_out_grad: float32 [64, 768], P(None, 'chan')
- decay_rate_grad: float32 [768], P('chan')
- out_proj_grad: float32 [768, 768], P(None, 'chan')
- norm2_gain_grad: float32 [768], P('chan')
- w_gate_grad: float32 [768, 3072], P(None, 'chan')
- w_up_grad: float32 [768, 3072], P(None, 'chan')
- w_down_grad: float32 [3072, 768], P('chan')
The draws below stay inside these ranges and needn't reach their ends.
Inputs may be any that keep to these rules, and one draw needn't show every extreme that they name: `halves`: column 0 is a row's split point, column 1 its valid length; the valid length is 512 or more, and 1024 in at least one row; the split point lies between a quarter and three quarters of the valid length.
All inputs are finite; a program needn't handle non-finite values.
Results may differ from the reference program's by a relative error of at most 0.012.
The reference program's roundings to bfloat16 on the way count: a program that leaves them out, or rounds other values in their place, can miss the bound.
Values may be sent and summed in bfloat16 or wider, within the bound.
A program may use at most 192 MiB of HBM per device.

```python
import math
import jax
import jax.numpy as jnp
from jax import lax

D = 768
FF = 3072
FH = 64
FEAT = 33
SEQ = 1024
ROWS_DEV = 1
ROWS = 8


def draw_halves(key, part):
    key = jax.random.fold_in(key, 11)
    key_valid, key_full, key_split = jax.random.split(key, 3)
    valid_len = jax.random.randint(key_valid, (ROWS,), SEQ // 2, SEQ + 1)
    full_row = jax.random.randint(key_full, (), 0, ROWS)
    valid_len = jnp.where(jnp.arange(ROWS) == full_row, SEQ, valid_len)
    offsets = jax.random.randint(key_split, (ROWS,), 0, 1 << 20) % (valid_len // 2)
    split_at = valid_len // 4 + offsets
    return jnp.stack([split_at, valid_len], axis=1).astype(jnp.int32)


def shard_levels(own_key, dims, cuts, low, high):
    def one(position, blocks):
        draws = jax.random.uniform(jax.random.fold_in(jax.random.fold_in(own_key, 6), position), (blocks,), jnp.float32, low / len(cuts), high / len(cuts))
        return jnp.repeat(jnp.exp(draws), dims[position] // blocks).reshape((-1,) + (1,) * (len(dims) - position - 1))

    level = one(*cuts[0])
    for cut in cuts[1:]:
        level = level * one(*cut)
    return level


def gaussian(own_key, shape, scale, most, shards=(), held_as=jnp.bfloat16):
    values = jax.random.normal(own_key, shape, jnp.float32) * scale
    if len(shards) > 0:
        values = shard_levels(own_key, shape, shards, -0.22, 0.18) * values
    return jnp.clip(values, min=-most, max=most).astype(held_as)


def setup_inputs(seed: int = 0) -> dict:
    seeds = jax.random.split(jax.random.key(seed), 17)
    hidden_in = gaussian(seeds[0], (ROWS, SEQ, D), 1.0, 6.0, ((0, 8), (2, 4)))
    halves = draw_halves(jax.random.fold_in(seeds[16], 71), 0)
    norm1_gain = jnp.clip(1.0 + 0.15 * jax.random.normal(seeds[2], (D,), jnp.float32), 0.25, 1.75)
    in_proj = gaussian(seeds[3], (D, 3, D), D ** -0.5, 0.21875, ((2, 4),))
    short_taps = gaussian(seeds[4], (3, 3, D), 0.6, 3.0, ((2, 4),), jnp.float32)
    cond_taps = gaussian(seeds[5], (3, D), 0.8, 3.0, ((1, 4),), jnp.float32)
    filter_in = gaussian(seeds[6], (FEAT, FH), (FEAT // 4) ** -0.5, 2.0, (), jnp.float32)
    filter_bias = jnp.clip(jax.random.uniform(seeds[7], (FH,), jnp.float32, -3.140625, 3.140625), -3.140625, 3.140625)
    filter_out = gaussian(seeds[8], (FH, D), FH ** -0.5, 0.75, ((1, 4),), jnp.float32)
    decay_rate = jnp.clip(jnp.exp(math.log(0.05) - 3.9357395 * jax.random.uniform(seeds[9], (D,), jnp.float32) ** shard_levels(seeds[9], (D,), ((0, 4),), -0.2, 0.2)), 0.0009765625, 0.05)
    out_proj = gaussian(seeds[10], (D, D), D ** -0.5, 0.21875, ((1, 4),))
    norm2_gain = jnp.clip(1.0 + 0.15 * jax.random.normal(seeds[11], (D,), jnp.float32), 0.25, 1.75)
    w_gate = gaussian(seeds[12], (D, FF), D ** -0.5, 0.21875, ((1, 4),))
    w_up = gaussian(seeds[13], (D, FF), D ** -0.5, 0.21875, ((1, 4),))
    w_down = gaussian(seeds[14], (FF, D), (FF // 2) ** -0.5, 0.15625, ((0, 4),))
    out_grad = gaussian(seeds[15], (ROWS, SEQ, D), 1.0, 6.0, ((0, 8), (2, 4)))
    return dict(hidden_in=hidden_in, halves=halves, norm1_gain=norm1_gain, in_proj=in_proj, short_taps=short_taps, cond_taps=cond_taps, filter_in=filter_in, filter_bias=filter_bias, filter_out=filter_out, decay_rate=decay_rate, out_proj=out_proj, norm2_gain=norm2_gain, w_gate=w_gate, w_up=w_up, w_down=w_down, out_grad=out_grad)


highest = lax.Precision.HIGHEST
norm_eps = 1e-05

@jax.custom_vjp
def low(v):
    return lax.optimization_barrier(v.astype(jnp.bfloat16)).astype(jnp.float32)

@jax.custom_vjp
def low_back(v):
    return v

def low_keep(v):
    return (low(v), None)

def low_pass(kept, grad):
    return (grad,)

def back_keep(v):
    return (v, None)

def back_low(kept, grad):
    return (low(grad),)
low.defvjp(low_keep, low_pass)
low_back.defvjp(back_keep, back_low)

def band_features(seq_len, feat_count):
    bands = (feat_count - 1) // 2
    positions = jnp.arange(seq_len, dtype=jnp.int32)
    orders = jnp.arange(1, bands + 1, dtype=jnp.int32)
    phases = (positions[:, None] * orders[None, :] % seq_len).astype(jnp.float32) * (2.0 * math.pi / seq_len)
    position_ramp = positions.astype(jnp.float32)[:, None] / seq_len
    return jnp.concatenate([position_ramp, jnp.sin(phases), jnp.cos(phases)], axis=1)

def delayed(values, tap_weights):
    seq_len = values.shape[1]
    padded = jnp.pad(values, ((0, 0), (2, 0)) + ((0, 0),) * (values.ndim - 2))
    return tap_weights[0] * padded[:, 2:] + tap_weights[1] * padded[:, 1:seq_len + 1] + tap_weights[2] * padded[:, :seq_len]

def filter_base(seq_len, filter_in, filter_bias, filter_out):
    features = band_features(seq_len, filter_in.shape[0])
    hidden_wave = jnp.sin(jnp.dot(features, filter_in, precision=highest) + filter_bias)
    return jnp.dot(hidden_wave, filter_out, precision=highest)

def layer_norm(values, scale_gain):
    centre = lax.optimization_barrier(jnp.mean(values, axis=-1, keepdims=True))
    spread = lax.optimization_barrier(jnp.mean(values * values, axis=-1, keepdims=True)) - centre * centre
    return (values - centre) * lax.rsqrt(spread + norm_eps) * scale_gain

def half_masks(halves, seq_len):
    positions = jnp.arange(seq_len, dtype=jnp.int32)[None, :]
    split_at = halves[:, 0:1]
    valid_len = halves[:, 1:2]
    first_half = (positions < split_at).astype(jnp.float32)[:, :, None]
    second_half = ((positions >= split_at) & (positions < valid_len)).astype(jnp.float32)[:, :, None]
    return (first_half + second_half, first_half, second_half)

def mixer_ref(projected, short_taps, cond_taps, filter_in, filter_bias, filter_out, decay_rate, first_half, second_half):
    seq_len = projected.shape[1]
    short_out = delayed(projected, short_taps)
    query_part = short_out[:, :, 0]
    key_part = short_out[:, :, 1]
    value_part = short_out[:, :, 2]
    conditioned = delayed(value_part, cond_taps)
    positions = jnp.arange(seq_len, dtype=jnp.float32)[:, None]
    kernel = (filter_base(seq_len, filter_in, filter_bias, filter_out)[None] + jnp.tanh(conditioned)) * jnp.exp(-decay_rate * positions)[None] / math.sqrt(seq_len)
    source = key_part * value_part
    kernel_hat = jnp.fft.rfft(kernel, n=2 * seq_len, axis=1)
    mixed_out = jnp.zeros_like(source)
    for half_mask in (first_half, second_half):
        spectrum = jnp.fft.rfft(source * half_mask, n=2 * seq_len, axis=1)
        mixed_out = mixed_out + jnp.fft.irfft(spectrum * kernel_hat, n=2 * seq_len, axis=1)[:, :seq_len] * half_mask
    return query_part * mixed_out

def block_forward(inputs, halves, norm1_gain, in_proj, short_taps, cond_taps, filter_in, filter_bias, filter_out, decay_rate, out_proj, norm2_gain, w_gate, w_up, w_down):
    valid_mask, first_half, second_half = half_masks(halves, inputs.shape[1])
    norm1_out = low(layer_norm(inputs, norm1_gain))
    projected = low_back(jnp.einsum('bld,djc->bljc', norm1_out, in_proj, precision=highest))
    mixer_out = mixer_ref(projected, short_taps, cond_taps, filter_in, filter_bias, filter_out, decay_rate, first_half, second_half)
    residual = inputs + low_back(jnp.einsum('bld,dc->blc', low(mixer_out), out_proj, precision=highest))
    norm2_out = low(layer_norm(residual, norm2_gain))
    gate_val = low_back(jnp.einsum('bld,df->blf', norm2_out, w_gate, precision=highest))
    up_val = low_back(jnp.einsum('bld,df->blf', norm2_out, w_up, precision=highest))
    hidden_mid = low(jax.nn.silu(gate_val) * up_val)
    mlp_out = jnp.einsum('blf,fd->bld', hidden_mid, w_down, precision=highest)
    return valid_mask * (residual + mlp_out)

def reference(hidden_in, halves, norm1_gain, in_proj, short_taps, cond_taps, filter_in, filter_bias, filter_out, decay_rate, out_proj, norm2_gain, w_gate, w_up, w_down, out_grad):
    weights = tuple((item.astype(jnp.float32) for item in (norm1_gain, in_proj, short_taps, cond_taps, filter_in, filter_bias, filter_out, decay_rate, out_proj, norm2_gain, w_gate, w_up, w_down)))
    row_total, seq_len, full_width = hidden_in.shape
    group_count = row_total // ROWS_DEV
    inputs = hidden_in.astype(jnp.float32).reshape(group_count, ROWS_DEV, seq_len, full_width)
    cotangents = out_grad.astype(jnp.float32).reshape(group_count, ROWS_DEV, seq_len, full_width)
    bounds = halves.reshape(group_count, ROWS_DEV, 2)

    def one_group(totals, pieces):
        row_block, row_bounds, cotangent = pieces

        def forward(block_in, *params):
            return block_forward(block_in, row_bounds, *params)
        result, pullback = jax.vjp(forward, row_block, *weights)
        gradients = pullback(cotangent)
        totals = tuple((running + added for running, added in zip(totals, gradients[1:])))
        return (totals, (result, gradients[0]))
    zero_sums = tuple((jnp.zeros_like(item) for item in weights))
    totals, (outputs, input_grads) = lax.scan(one_group, zero_sums, (inputs, bounds, cotangents))
    output = outputs.reshape(row_total, seq_len, full_width)
    input_grad = input_grads.reshape(row_total, seq_len, full_width)
    return (output, input_grad, totals[0], totals[1], totals[2], totals[3], totals[4], totals[5], totals[6], totals[7], totals[8], totals[9], totals[10], totals[11], totals[12])
```

```python
import math

import jax
import jax.numpy as jnp
import numpy as np
from jax import lax
from jax.sharding import PartitionSpec as P

highest = lax.Precision.HIGHEST
norm_eps = 1e-05
f32 = jnp.float32
bf16 = jnp.bfloat16


def band_features(seq_len, feat_count):
    bands = (feat_count - 1) // 2
    positions = np.arange(seq_len)
    orders = np.arange(1, bands + 1)
    phases = (orders[:, None] * positions[None, :] % seq_len) * (2.0 * math.pi / seq_len)
    ramp = positions[None, :] / seq_len
    return np.concatenate([ramp, np.sin(phases), np.cos(phases)], axis=0).astype(np.float32)


def wave_matrix(seq_len):
    period = 3 * seq_len // 2
    freq = period // 2
    phase = (np.arange(seq_len)[:, None] * (2 * np.arange(freq)[None, :] + 1)) % (2 * period)
    angle = phase * (math.pi / period)
    return np.concatenate([np.cos(angle), np.sin(angle)], axis=1)


def nn(a, b, precision=None):
    return lax.dot_general(a, b, (((1,), (0,)), ((), ())), precision=precision, preferred_element_type=f32)


def nt(a, b, precision=None):
    return lax.dot_general(a, b, (((1,), (1,)), ((), ())), precision=precision, preferred_element_type=f32)


def tn(a, b, precision=None):
    return lax.dot_general(a, b, (((0,), (0,)), ((), ())), precision=precision, preferred_element_type=f32)


def later(values, steps):
    if steps == 0:
        return values
    return jnp.pad(values, ((0, 0), (steps, 0)))[:, : values.shape[1]]


def sooner(values, steps):
    if steps == 0:
        return values
    return jnp.pad(values, ((0, 0), (0, steps)))[:, steps:]


def local(
    hidden_in, halves, norm1_gain, in_proj, short_taps, cond_taps, filter_in, filter_bias,
    filter_out, decay_rate, out_proj, norm2_gain, w_gate, w_up, w_down, out_grad,
):
    seq_len, own = hidden_in.shape[1], hidden_in.shape[2]
    ways = lax.axis_size("chan")
    width = own * ways
    me = lax.axis_index("chan")
    block = seq_len // ways
    lags = 3 * seq_len // 4
    freq = lags

    pos = jnp.arange(seq_len, dtype=jnp.int32)[None, :]
    half1 = (pos < halves[0, 0]).astype(f32)
    half2 = ((pos >= halves[0, 0]) & (pos < halves[0, 1])).astype(f32)
    valid = half1 + half2

    def gathered(v, axis=0):
        return lax.all_gather(v, "chan", axis=axis, tiled=True)

    x_own = hidden_in[0].T
    grad_own = (out_grad[0].T.astype(f32) * valid).astype(bf16)
    x_full = gathered(x_own).astype(f32)
    grad_full = gathered(grad_own)
    out_full = gathered(out_proj, axis=1)
    gains = gathered(jnp.stack([norm1_gain, norm2_gain], axis=1))
    gain1, gain2 = gains[:, 0:1], gains[:, 1:2]

    def normed(v):
        centre = jnp.mean(v, axis=0, keepdims=True)
        spread = jnp.mean(v * v, axis=0, keepdims=True) - centre * centre
        inverse = lax.rsqrt(spread + norm_eps)
        return (v - centre) * inverse, inverse

    n1, inv1 = normed(x_full)
    norm1_out = (n1 * gain1).astype(bf16)
    in_flat = in_proj.reshape(width, 3 * own)
    proj = tn(in_flat, norm1_out)

    feats = jnp.asarray(band_features(seq_len, filter_in.shape[0]))
    arg = tn(filter_in, feats, highest) + filter_bias[:, None]
    wave = jnp.sin(arg)
    base = tn(filter_out, wave, highest)
    decay = jnp.exp(-decay_rate[:, None] * pos.astype(f32)) * (1.0 / math.sqrt(seq_len))
    ramp = pos.astype(f32)

    table = jnp.asarray(wave_matrix(seq_len).astype(np.float32)).astype(bf16)

    def spectrum(v):
        return nn(v.astype(bf16), table[: v.shape[1]])

    def signal(re, im, length):
        both = jnp.concatenate([re, im], axis=1).astype(bf16)
        return nt(both, table[:length]) * (1.0 / freq)

    parts = [proj[j * own : (j + 1) * own] for j in range(3)]
    taps = [[short_taps[i, j][:, None] for i in range(3)] for j in range(3)]
    query, key, value = [sum(taps[j][i] * later(parts[j], i) for i in range(3)) for j in range(3)]
    ctaps = [cond_taps[i][:, None] for i in range(3)]
    cond = sum(ctaps[i] * later(value, i) for i in range(3))
    squash = jnp.tanh(cond)
    kern = (base + squash) * decay
    source = key * value
    k_hat = spectrum(kern[:, :lags])
    s_hat = [spectrum(source * h) for h in (half1, half2)]
    kr, ki = k_hat[:, :freq], k_hat[:, freq:]
    mixed = 0.0
    for h, s in zip((half1, half2), s_hat):
        sr, si = s[:, :freq], s[:, freq:]
        mixed = mixed + h * signal(kr * sr - ki * si, kr * si + ki * sr, seq_len)
    mixer_own = (query * mixed).astype(bf16)
    mixer_full = gathered(mixer_own)

    resid = x_full + tn(out_full, mixer_full)
    n2, inv2 = normed(resid)
    norm2_out = (n2 * gain2).astype(bf16)
    gate = tn(w_gate, norm2_out)
    up = tn(w_up, norm2_out)
    sig = jax.nn.sigmoid(gate)
    act = gate * sig
    mid = (act * up).astype(bf16)
    hid_grad = nn(w_down, grad_full)
    gate_grad = (hid_grad * up * sig * (1.0 + gate * (1.0 - sig))).astype(bf16)
    up_grad = (hid_grad * act).astype(bf16)
    terms = (nn(w_gate, gate_grad) + nn(w_up, up_grad)).astype(bf16)
    mlp = tn(w_down, mid).astype(bf16)
    w_down_grad = nt(mid, grad_full)
    w_gate_grad = nt(norm2_out, gate_grad)
    w_up_grad = nt(norm2_out, up_grad)

    resid_own = lax.dynamic_slice_in_dim(resid, me * own, own, 0)
    mlp_own = lax.psum_scatter(mlp, "chan", scatter_dimension=0, tiled=True).astype(f32)
    output = (valid * (resid_own + mlp_own)).T[None]

    def tok(v):
        return lax.dynamic_slice_in_dim(v, me * block, block, 1)

    def norm_back(up_g, gain, n, inv):
        q = up_g * gain
        return inv * (q - jnp.mean(q, axis=0, keepdims=True) - n * jnp.mean(q * n, axis=0, keepdims=True))

    terms_own = lax.psum_scatter(terms, "chan", scatter_dimension=1, tiled=True).astype(f32)
    n2_tok, inv2_tok = tok(n2), tok(inv2)
    gain2_part = jnp.sum(terms_own * n2_tok, axis=1)
    resid_grad = tok(grad_full).astype(f32) + norm_back(terms_own, gain2, n2_tok, inv2_tok)
    proj_grad = resid_grad.astype(bf16)
    mixer_grad = nn(out_full, proj_grad).astype(bf16)
    swapped = lax.all_to_all(
        jnp.stack([mixer_grad, proj_grad]), "chan", split_axis=1, concat_axis=2, tiled=True
    )
    mixer_grad, proj_grad_own = swapped[0].astype(f32), swapped[1]
    gain2_own = lax.psum_scatter(gain2_part, "chan", scatter_dimension=0, tiled=True)
    out_proj_grad = nt(mixer_full, proj_grad_own)

    query_grad = mixer_grad * mixed
    mixed_grad = mixer_grad * query
    source_grad = 0.0
    kg_re, kg_im = 0.0, 0.0
    for h, s in zip((half1, half2), s_hat):
        m = spectrum(mixed_grad * h)
        mr, mi = m[:, :freq], m[:, freq:]
        sr, si = s[:, :freq], s[:, freq:]
        source_grad = source_grad + h * signal(kr * mr + ki * mi, kr * mi - ki * mr, seq_len)
        kg_re = kg_re + sr * mr + si * mi
        kg_im = kg_im + sr * mi - si * mr
    kern_grad = signal(kg_re, kg_im, lags)
    kern_grad = jnp.pad(kern_grad, ((0, 0), (0, seq_len - lags)))
    rate_grad = -jnp.sum(kern_grad * kern * ramp, axis=1)
    base_grad = kern_grad * decay
    cond_grad = base_grad * (1.0 - squash * squash)
    ctap_grad = jnp.stack([jnp.sum(cond_grad * later(value, i), axis=1) for i in range(3)])
    key_grad = source_grad * value
    value_grad = source_grad * key + sum(ctaps[i] * sooner(cond_grad, i) for i in range(3))
    branch = (query_grad, key_grad, value_grad)
    stap_grad = jnp.stack(
        [jnp.stack([jnp.sum(branch[j] * later(parts[j], i), axis=1) for j in range(3)]) for i in range(3)]
    )
    low = jnp.concatenate(
        [sum(taps[j][i] * sooner(branch[j], i) for i in range(3)) for j in range(3)], axis=0
    ).astype(bf16)
    fout_grad = nt(wave, base_grad, highest)
    arg_grad = nn(filter_out, base_grad, highest) * jnp.cos(arg)
    fin_grad = nt(feats, arg_grad, highest)
    fbias_grad = jnp.sum(arg_grad, axis=1)

    in_grad = nt(norm1_out, low)
    terms1 = lax.psum_scatter(nn(in_flat, low).astype(bf16), "chan", scatter_dimension=0, tiled=True).astype(f32)
    gain1_own = norm1_gain[:, None]
    n1_own = lax.dynamic_slice_in_dim(n1, me * own, own, 0)
    q1 = terms1 * gain1_own
    m0, m1 = lax.psum((jnp.sum(q1, axis=0), jnp.sum(q1 * n1_own, axis=0)), "chan")
    input_grad = proj_grad_own.astype(f32) + inv1 * (q1 - m0 / width - n1_own * (m1 / width))
    gain1_grad = jnp.sum(terms1 * n1_own, axis=1)
    input_grad = input_grad.T[None]

    big = lax.psum((w_down_grad.astype(bf16), w_gate_grad.astype(bf16), w_up_grad.astype(bf16),
                    in_grad.astype(bf16), out_proj_grad.astype(bf16)), "dp")
    wdg, wgg, wug, ing, opg = [v.astype(f32) for v in big]
    g2, g1, st, ct, fo, rt = lax.psum((gain2_own, gain1_grad, stap_grad, ctap_grad, fout_grad, rate_grad), "dp")
    fi, fb = lax.psum((fin_grad, fbias_grad), ("dp", "chan"))
    return (output, input_grad, g1, ing.reshape(width, 3, own), st, ct, fi, fb, fo, rt, opg, g2, wgg, wug, wdg)


def solution(mesh):
    rows, cols = P("dp", None, "chan"), P(None, "chan")
    in_specs = (
        rows, P("dp", None), P("chan"), P(None, None, "chan"), P(None, None, "chan"), cols, P(), P(),
        cols, P("chan"), cols, P("chan"), cols, cols, P("chan", None), rows,
    )
    out_specs = (
        rows, rows, P("chan"), P(None, None, "chan"), P(None, None, "chan"), cols, P(), P(),
        cols, P("chan"), cols, P("chan"), cols, cols, P("chan", None),
    )
    return jax.shard_map(local, mesh=mesh, in_specs=in_specs, out_specs=out_specs, check_vma=False)
```

```python
import functools
import math

import jax
import jax.numpy as jnp
import numpy as np
from jax import lax
from jax.experimental import pallas as pl
from jax.experimental.pallas import tpu as pltpu
from jax.sharding import PartitionSpec as P

highest = lax.Precision.HIGHEST
norm_eps = 1e-05
f32 = jnp.float32
bf16 = jnp.bfloat16


def band_features(seq_len, feat_count):
    bands = (feat_count - 1) // 2
    positions = np.arange(seq_len)
    orders = np.arange(1, bands + 1)
    phases = (orders[:, None] * positions[None, :] % seq_len) * (2.0 * math.pi / seq_len)
    ramp = positions[None, :] / seq_len
    return np.concatenate([ramp, np.sin(phases), np.cos(phases)], axis=0).astype(np.float32)


def wave_matrix(seq_len):
    period = 3 * seq_len // 2
    freq = period // 2
    phase = (np.arange(seq_len)[:, None] * (2 * np.arange(freq)[None, :] + 1)) % (2 * period)
    angle = phase * (math.pi / period)
    return np.concatenate([np.cos(angle), np.sin(angle)], axis=1)


def nn(a, b, precision=None):
    return lax.dot_general(a, b, (((1,), (0,)), ((), ())), precision=precision, preferred_element_type=f32)


def nt(a, b, precision=None):
    return lax.dot_general(a, b, (((1,), (1,)), ((), ())), precision=precision, preferred_element_type=f32)


def tn(a, b, precision=None):
    return lax.dot_general(a, b, (((0,), (0,)), ((), ())), precision=precision, preferred_element_type=f32)


def later(values, steps):
    if steps == 0:
        return values
    return jnp.pad(values, ((0, 0), (steps, 0)))[:, : values.shape[1]]


def sooner(values, steps):
    if steps == 0:
        return values
    return jnp.pad(values, ((0, 0), (0, steps)))[:, steps:]


MESH = pl.DeviceIdType.MESH
lane_tile = 256
row_tile = 16


def flipped(index, bit):
    return index + (1 << bit) * (1 - 2 * ((index // (1 << bit)) % 2))


class Line:
    def __init__(self, view, send_sem, recv_sem, at, ways):
        self.view, self.send_sem, self.recv_sem, self.at, self.ways = view, send_sem, recv_sem, at, ways

    def copy(self, way, hop, part, shard):
        ref = self.view(shard, part)
        step = 1 - 2 * way
        return pltpu.make_async_remote_copy(
            src_ref=ref, dst_ref=ref, send_sem=self.send_sem.at[way, hop, part],
            recv_sem=self.recv_sem.at[way, hop, part],
            device_id={"chan": (self.at + step + self.ways) % self.ways}, device_id_type=MESH,
        )

    def sends(self, way, hop):
        if way == 0:
            return jnp.logical_and(self.at >= hop, self.at < self.ways - 1)
        return jnp.logical_and(self.at + hop <= self.ways - 1, self.at > 0)

    def gets(self, way, hop):
        if way == 0:
            return self.at >= hop + 1
        return self.at + hop + 1 <= self.ways - 1

    def start(self, way, hop, part):
        @pl.when(self.sends(way, hop))
        def _():
            self.copy(way, hop, part, self.at - hop * (1 - 2 * way)).start()

    def wait_recv(self, way, hop, part):
        @pl.when(self.gets(way, hop))
        def _():
            self.copy(way, hop, part, self.at - (hop + 1) * (1 - 2 * way)).wait_recv()

    def wait_send(self, way, hop, part):
        @pl.when(self.sends(way, hop))
        def _():
            self.copy(way, hop, part, self.at - hop * (1 - 2 * way)).wait_send()

    def relay(self, hop, part):
        for way in (0, 1):
            self.wait_recv(way, hop - 1, part)
            self.start(way, hop, part)


def front_kernel(
    cfg, x_hbm, g_hbm, mask_ref, cols_ref, gain_ref, fin_ref, in_hbm, outf_hbm, feat_ref, tab_hbm, inv_hbm,
    xf_out, gf_out, outt_out, proj_out, mixo_out, qkv_out, squash_out, kern_out, mixed_out, hat_out, arg_out,
    xf, gf, outt, proj, mixf, qkv, squash, kern, mixed, hat, arg,
    in_t, tab, inv, n1o, pieces, gains, gaincol, sig, prod,
    load_sem, line_send, line_recv, piece_send, piece_recv, gain_send, gain_recv, save_sem,
):
    ways, rows, seq, own, width, bits = (cfg[k] for k in ("ways", "rows", "seq", "own", "width", "bits"))
    lags = 3 * seq // 4
    freq = lags
    parts = seq // lane_tile
    z = lax.axis_index("chan")
    r = lax.axis_index("dp")
    group = r % (1 << bits)
    span = pl.ds(pl.multiple_of(z * own, row_tile), own)

    def load(index, src, dst):
        copy = pltpu.make_async_copy(src, dst, load_sem.at[index])
        copy.start()
        return copy

    own_rows = pieces.shape[2]
    loads = [
        load(0, x_hbm, xf.at[span]),
        load(1, g_hbm, gf.at[span]),
        load(2, outf_hbm.at[pl.ds(pl.multiple_of(group * own_rows, row_tile), own_rows)], pieces.at[group, z]),
        load(3, in_hbm, in_t),
        load(4, tab_hbm, tab),
        load(5, inv_hbm, inv),
    ]
    barrier = pltpu.get_barrier_semaphore()
    peers = [{"chan": (z + s) % ways} for s in range(1, ways)] + [{"dp": flipped(r, b)} for b in range(bits)]
    for peer in peers:
        pl.semaphore_signal(barrier, inc=1, device_id=peer, device_id_type=MESH)
    pl.semaphore_wait(barrier, len(peers))

    def cut(buf):
        def view(shard, part):
            return buf.at[
                pl.ds(pl.multiple_of(shard * own, row_tile), own),
                pl.ds(pl.multiple_of(part * lane_tile, lane_tile), lane_tile),
            ]
        return view

    in_line = Line(cut(xf), line_send.at[0], line_recv.at[0], z, ways)
    g_line = Line(cut(gf), line_send.at[1], line_recv.at[1], z, ways)

    loads[0].wait()

    def each_part(fn):
        def run(part, carry):
            fn(part)
            return carry
        lax.fori_loop(0, parts, run, 0)

    def send_own(line):
        def run(part):
            for way in (0, 1):
                line.start(way, 0, part)
        each_part(run)

    def direct(buf_view, send, recv, s, dst_z, src_z):
        return pltpu.make_async_remote_copy(
            src_ref=buf_view(src_z), dst_ref=buf_view(src_z), send_sem=send.at[s], recv_sem=recv.at[s],
            device_id={"chan": dst_z}, device_id_type=MESH,
        )

    gains[z] = gain_ref[...]
    loads[2].wait()
    for s in range(1, ways):
        direct(lambda at: gains.at[at], gain_send, gain_recv, s, (z + s) % ways, z).start()
        direct(lambda at: pieces.at[group, at], piece_send, piece_recv, s, (z + s) % ways, z).start()
    send_own(in_line)

    arg[...] = nn(fin_ref[...], feat_ref[...], highest)
    base_wave = jnp.sin(arg[...])
    kern[...] = nn(cols_ref[:, 64:128], base_wave, highest)

    for s in range(1, ways):
        direct(lambda at: gains.at[at], gain_send, gain_recv, s, (z + s) % ways, (z + ways - s) % ways).wait_recv()
        direct(lambda at: pieces.at[group, at], piece_send, piece_recv, s, (z + s) % ways, (z + ways - s) % ways).wait_recv()

    held = [group]
    slot = ways
    started = []
    for bit in reversed(range(bits)):
        batch = []
        for piece in held:
            def make(which, slot=slot, bit=bit):
                return pltpu.make_async_remote_copy(
                    src_ref=pieces.at[which], dst_ref=pieces.at[which], send_sem=piece_send.at[slot],
                    recv_sem=piece_recv.at[slot], device_id={"dp": flipped(r, bit)}, device_id_type=MESH,
                )
            make(piece).start()
            batch.append((make, piece))
            slot += 1
        started.append((bit, batch))
        if bit == bits - 1:
            eye = lax.broadcasted_iota(jnp.int32, (own, gains.shape[2]), 0) == lax.broadcasted_iota(
                jnp.int32, (own, gains.shape[2]), 1)
            for s in range(ways):
                for which in range(2):
                    row = gains[s, which : which + 1, :]
                    gaincol[s * own : (s + 1) * own, which : which + 1] = jnp.sum(
                        jnp.where(eye, row, 0.0), axis=1, keepdims=True)
        for make, piece in batch:
            make(flipped(piece, bit)).wait_recv()
        held = held + [flipped(piece, bit) for piece in held]

    loads[1].wait()
    loads[3].wait()

    def norm_part(part):
        for hop in range(1, ways - 1):
            in_line.relay(hop, part)
        for way in (0, 1):
            in_line.wait_recv(way, ways - 2, part)
        cols = pl.ds(pl.multiple_of(part * lane_tile, lane_tile), lane_tile)
        values = xf[:, cols].astype(f32)
        centre = jnp.sum(values, axis=0, keepdims=True) * (1.0 / width)
        spread = jnp.sum(values * values, axis=0, keepdims=True) * (1.0 / width) - centre * centre
        inverse = lax.rsqrt(spread + norm_eps)
        low = ((values - centre) * inverse * gaincol[:, 0:1]).astype(bf16)
        n1o[:, cols] = low
        proj[:, cols] = nn(in_t[...], low)

    each_part(norm_part)
    send_own(g_line)
    loads[4].wait()
    loads[5].wait()

    grain = math.gcd(own_rows, own)
    for s in range(ways):
        for row in range(0, own * width // 128, grain):
            piece, inner = divmod(row, own_rows)
            block, place = divmod(row, own)
            outt[s * own + place : s * own + place + grain, 128 * block : 128 * block + 128] = pieces[
                piece, s, inner : inner + grain, :]

    lane = lax.broadcasted_iota(jnp.int32, (row_tile, seq), 1)
    place = lane.astype(f32)
    half1, half2 = mask_ref[0:1, :], mask_ref[1:2, :]

    def back(values, steps):
        if steps == 0:
            return values
        return jnp.where(lane >= steps, pltpu.roll(values, steps, 1), 0.0)

    def mix_rows(i, carry):
        here = pl.ds(pl.multiple_of(i * row_tile, row_tile), row_tile)

        def at(j):
            return pl.ds(pl.multiple_of(j * own + i * row_tile, row_tile), row_tile)

        tap = cols_ref[here, :]
        outs = []
        for j in range(3):
            part = proj[at(j), :]
            total = sum(tap[:, 3 * k + j : 3 * k + j + 1] * back(part, k) for k in range(3))
            qkv[at(j), :] = total
            outs.append(total)
        cond = sum(tap[:, 9 + k : 10 + k] * back(outs[2], k) for k in range(3))
        bent = jnp.tanh(cond)
        squash[here, :] = bent
        decay = jnp.exp(-tap[:, 12:13] * place) * (1.0 / math.sqrt(seq))
        filt = (kern[here, :] + bent) * decay
        kern[here, :] = filt
        source = outs[1] * outs[2]
        sig[at(0), :] = jnp.where(lane < lags, filt, 0.0).astype(bf16)
        sig[at(1), :] = (source * half1).astype(bf16)
        sig[at(2), :] = (source * half2).astype(bf16)
        return carry

    lax.fori_loop(0, own // row_tile, mix_rows, 0)

    def freq_tile(j, carry):
        re_at = pl.ds(pl.multiple_of(j * lane_tile, lane_tile), lane_tile)
        im_at = pl.ds(pl.multiple_of(freq + j * lane_tile, lane_tile), lane_tile)
        re = nn(sig[...], tab[:, re_at])
        im = nn(sig[...], tab[:, im_at])
        hat[:, re_at] = re.astype(bf16)
        hat[:, im_at] = im.astype(bf16)
        kr, ki = re[:own], im[:own]
        for h in range(2):
            sr, si = re[own * (h + 1) : own * (h + 2)], im[own * (h + 1) : own * (h + 2)]
            prod[own * h : own * (h + 1), re_at] = (kr * sr - ki * si).astype(bf16)
            prod[own * h : own * (h + 1), im_at] = (kr * si + ki * sr).astype(bf16)
        return carry

    lax.fori_loop(0, freq // lane_tile, freq_tile, 0)

    def g_relay(hop):
        each_part(functools.partial(g_line.relay, hop))

    g_relay(1)

    def time_tile(j, carry):
        cols = pl.ds(pl.multiple_of(j * lane_tile, lane_tile), lane_tile)
        both = nn(prod[...], inv[:, cols])
        total = (both[:own] * mask_ref[0:1, cols] + both[own:] * mask_ref[1:2, cols]) * (1.0 / freq)
        mixed[:, cols] = total
        mixf[:, cols] = (qkv[0:own, cols] * total).astype(bf16)
        return carry

    lax.fori_loop(0, parts, time_tile, 0)
    for hop in range(2, ways - 1):
        g_relay(hop)

    def finish(part):
        for way in (0, 1):
            g_line.wait_recv(way, ways - 2, part)
            for hop in range(ways - 1):
                in_line.wait_send(way, hop, part)
                g_line.wait_send(way, hop, part)

    each_part(finish)
    for s in range(1, ways):
        direct(lambda at: gains.at[at], gain_send, gain_recv, s, (z + s) % ways, z).wait_send()
        direct(lambda at: pieces.at[group, at], piece_send, piece_recv, s, (z + s) % ways, z).wait_send()
    for bit, batch in started:
        for make, piece in batch:
            make(piece).wait_send()
    saves = []
    for k, (src, dst) in enumerate([
        (xf, xf_out), (gf, gf_out), (outt, outt_out), (proj, proj_out), (mixf, mixo_out), (qkv, qkv_out),
        (squash, squash_out), (kern, kern_out), (mixed, mixed_out), (hat, hat_out), (arg, arg_out),
    ]):
        copy = pltpu.make_async_copy(src, dst, save_sem.at[k])
        copy.start()
        saves.append(copy)
    for copy in saves:
        copy.wait()


def front(cfg, x_own, g_own, masks, cols, gain_rows, fin_t, in_t, out_flat, feats, tab, inv):
    ways, rows, seq, own, width, bits = (cfg[k] for k in ("ways", "rows", "seq", "own", "width", "bits"))
    period = 3 * seq // 2
    held = [
        ((width, seq), bf16), ((width, seq), bf16), ((width, width), bf16), ((3 * own, seq), f32), ((own, seq), bf16),
        ((3 * own, seq), f32), ((own, seq), f32), ((own, seq), f32), ((own, seq), f32), ((3 * own, period), bf16),
        ((64, seq), f32),
    ]
    here = pl.BlockSpec(memory_space=pltpu.VMEM)
    there = pl.BlockSpec(memory_space=pl.ANY)
    dma = pltpu.SemaphoreType.DMA
    parts = seq // lane_tile
    extra = [
        ((3 * own, width), bf16), ((seq, period), bf16), ((period, seq), bf16), ((width, seq), bf16),
        ((1 << bits, ways, own * width // 128 // (1 << bits), 128), bf16), ((ways, 8, 256), f32), ((width, 128), f32),
        ((3 * own, seq), bf16), ((2 * own, period), bf16),
    ]
    return pl.pallas_call(
        functools.partial(front_kernel, cfg),
        out_shape=[jax.ShapeDtypeStruct(s, t) for s, t in held],
        in_specs=[there, there, here, here, here, here, there, there, here, there, there],
        out_specs=[there] * len(held),
        scratch_shapes=[pltpu.VMEM(s, t) for s, t in held + extra] + [
            dma((8,)), dma((2, 2, ways - 1, parts)), dma((2, 2, ways - 1, parts)),
            dma((ways + (1 << bits),)), dma((ways + (1 << bits),)), dma((ways,)), dma((ways,)), dma((16,)),
        ],
        compiler_params=pltpu.CompilerParams(collective_id=0, has_side_effects=True, vmem_limit_bytes=56 << 20),
    )(x_own, g_own, masks, cols, gain_rows, fin_t, in_t, out_flat, feats, tab, inv)

def local(
    hidden_in, halves, norm1_gain, in_proj, short_taps, cond_taps, filter_in, filter_bias,
    filter_out, decay_rate, out_proj, norm2_gain, w_gate, w_up, w_down, out_grad,
):
    seq_len, own = hidden_in.shape[1], hidden_in.shape[2]
    ways = lax.axis_size("chan")
    width = own * ways
    me = lax.axis_index("chan")
    block = seq_len // ways
    lags = 3 * seq_len // 4
    freq = lags

    pos = jnp.arange(seq_len, dtype=jnp.int32)[None, :]
    half1 = (pos < halves[0, 0]).astype(f32)
    half2 = ((pos >= halves[0, 0]) & (pos < halves[0, 1])).astype(f32)
    valid = half1 + half2

    def gathered(v, axis=0):
        return lax.all_gather(v, "chan", axis=axis, tiled=True)

    rows = lax.axis_size("dp")
    cfg = dict(ways=ways, rows=rows, seq=seq_len, own=own, width=width, bits=min(3, rows.bit_length() - 1))
    x_own = hidden_in[0].T
    grad_own = (out_grad[0].T.astype(f32) * valid).astype(bf16)
    masks = jnp.pad(jnp.concatenate([half1, half2, valid], axis=0), ((0, 5), (0, 0)))
    small = jnp.concatenate([short_taps.reshape(9, own), cond_taps, decay_rate[None], jnp.zeros((51, own), f32), filter_out])
    cols = small.T
    gain_rows = jnp.pad(jnp.stack([norm1_gain, norm2_gain]), ((0, 6), (0, 256 - own)))
    feat_np = band_features(seq_len, filter_in.shape[0])
    count = feat_np.shape[0]
    feat_np = np.concatenate([feat_np, np.ones((1, seq_len), np.float32), np.zeros((63 - count, seq_len), np.float32)])
    feats = jnp.asarray(feat_np)
    fin_t = jnp.pad(jnp.concatenate([filter_in, filter_bias[None]]), ((0, 63 - count), (0, 0))).T
    in_flat = in_proj.reshape(width, 3 * own)
    out_flat = out_proj.T.reshape(own, width // 128, 128).transpose(1, 0, 2).reshape(-1, 128)
    table_np = wave_matrix(seq_len).astype(np.float32)
    table = jnp.asarray(table_np).astype(bf16)
    inv_table = jnp.asarray(table_np.T).astype(bf16)
    (xf, grad_full, out_t, proj, mixer_own, qkv, squash, kern, mixed, hat, arg) = front(
        cfg, x_own, grad_own, masks, cols, gain_rows, fin_t, in_flat.T, out_flat, feats, table, inv_table)
    x_full = xf.astype(f32)
    out_full = out_t.T
    gains = gathered(jnp.stack([norm1_gain, norm2_gain], axis=1))
    gain1, gain2 = gains[:, 0:1], gains[:, 1:2]

    def normed(v):
        centre = jnp.mean(v, axis=0, keepdims=True)
        spread = jnp.mean(v * v, axis=0, keepdims=True) - centre * centre
        inverse = lax.rsqrt(spread + norm_eps)
        return (v - centre) * inverse, inverse

    n1, inv1 = normed(x_full)
    norm1_out = (n1 * gain1).astype(bf16)
    wave = jnp.sin(arg)
    decay = jnp.exp(-decay_rate[:, None] * pos.astype(f32)) * (1.0 / math.sqrt(seq_len))
    ramp = pos.astype(f32)


    def spectrum(v):
        return nn(v.astype(bf16), table[: v.shape[1]])

    def signal(re, im, length):
        both = jnp.concatenate([re, im], axis=1).astype(bf16)
        return nt(both, table[:length]) * (1.0 / freq)

    parts = [proj[j * own : (j + 1) * own] for j in range(3)]
    taps = [[short_taps[i, j][:, None] for i in range(3)] for j in range(3)]
    query, key, value = [qkv[j * own : (j + 1) * own] for j in range(3)]
    ctaps = [cond_taps[i][:, None] for i in range(3)]
    hats = [hat[j * own : (j + 1) * own].astype(f32) for j in range(3)]
    kr, ki = hats[0][:, :freq], hats[0][:, freq:]
    s_hat = hats[1:]
    mixer_full = gathered(mixer_own)

    resid = x_full + tn(out_full, mixer_full)
    n2, inv2 = normed(resid)
    norm2_out = (n2 * gain2).astype(bf16)
    gate = tn(w_gate, norm2_out)
    up = tn(w_up, norm2_out)
    sig = jax.nn.sigmoid(gate)
    act = gate * sig
    mid = (act * up).astype(bf16)
    hid_grad = nn(w_down, grad_full)
    gate_grad = (hid_grad * up * sig * (1.0 + gate * (1.0 - sig))).astype(bf16)
    up_grad = (hid_grad * act).astype(bf16)
    terms = (nn(w_gate, gate_grad) + nn(w_up, up_grad)).astype(bf16)
    mlp = tn(w_down, mid).astype(bf16)
    w_down_grad = nt(mid, grad_full)
    w_gate_grad = nt(norm2_out, gate_grad)
    w_up_grad = nt(norm2_out, up_grad)

    resid_own = lax.dynamic_slice_in_dim(resid, me * own, own, 0)
    mlp_own = lax.psum_scatter(mlp, "chan", scatter_dimension=0, tiled=True).astype(f32)
    output = (valid * (resid_own + mlp_own)).T[None]

    def tok(v):
        return lax.dynamic_slice_in_dim(v, me * block, block, 1)

    def norm_back(up_g, gain, n, inv):
        q = up_g * gain
        return inv * (q - jnp.mean(q, axis=0, keepdims=True) - n * jnp.mean(q * n, axis=0, keepdims=True))

    terms_own = lax.psum_scatter(terms, "chan", scatter_dimension=1, tiled=True).astype(f32)
    n2_tok, inv2_tok = tok(n2), tok(inv2)
    gain2_part = jnp.sum(terms_own * n2_tok, axis=1)
    resid_grad = tok(grad_full).astype(f32) + norm_back(terms_own, gain2, n2_tok, inv2_tok)
    proj_grad = resid_grad.astype(bf16)
    mixer_grad = nn(out_full, proj_grad).astype(bf16)
    swapped = lax.all_to_all(
        jnp.stack([mixer_grad, proj_grad]), "chan", split_axis=1, concat_axis=2, tiled=True
    )
    mixer_grad, proj_grad_own = swapped[0].astype(f32), swapped[1]
    gain2_own = lax.psum_scatter(gain2_part, "chan", scatter_dimension=0, tiled=True)
    out_proj_grad = nt(mixer_full, proj_grad_own)

    query_grad = mixer_grad * mixed
    mixed_grad = mixer_grad * query
    source_grad = 0.0
    kg_re, kg_im = 0.0, 0.0
    for h, s in zip((half1, half2), s_hat):
        m = spectrum(mixed_grad * h)
        mr, mi = m[:, :freq], m[:, freq:]
        sr, si = s[:, :freq], s[:, freq:]
        source_grad = source_grad + h * signal(kr * mr + ki * mi, kr * mi - ki * mr, seq_len)
        kg_re = kg_re + sr * mr + si * mi
        kg_im = kg_im + sr * mi - si * mr
    kern_grad = signal(kg_re, kg_im, lags)
    kern_grad = jnp.pad(kern_grad, ((0, 0), (0, seq_len - lags)))
    rate_grad = -jnp.sum(kern_grad * kern * ramp, axis=1)
    base_grad = kern_grad * decay
    cond_grad = base_grad * (1.0 - squash * squash)
    ctap_grad = jnp.stack([jnp.sum(cond_grad * later(value, i), axis=1) for i in range(3)])
    key_grad = source_grad * value
    value_grad = source_grad * key + sum(ctaps[i] * sooner(cond_grad, i) for i in range(3))
    branch = (query_grad, key_grad, value_grad)
    stap_grad = jnp.stack(
        [jnp.stack([jnp.sum(branch[j] * later(parts[j], i), axis=1) for j in range(3)]) for i in range(3)]
    )
    low = jnp.concatenate(
        [sum(taps[j][i] * sooner(branch[j], i) for i in range(3)) for j in range(3)], axis=0
    ).astype(bf16)
    fout_grad = nt(wave, base_grad, highest)
    arg_grad = nn(filter_out, base_grad, highest) * jnp.cos(arg)
    both = nt(feats, arg_grad, highest)
    fin_grad, fbias_grad = both[:count], both[count]

    in_grad = nt(norm1_out, low)
    terms1 = lax.psum_scatter(nn(in_flat, low).astype(bf16), "chan", scatter_dimension=0, tiled=True).astype(f32)
    gain1_own = norm1_gain[:, None]
    n1_own = lax.dynamic_slice_in_dim(n1, me * own, own, 0)
    q1 = terms1 * gain1_own
    m0, m1 = lax.psum((jnp.sum(q1, axis=0), jnp.sum(q1 * n1_own, axis=0)), "chan")
    input_grad = proj_grad_own.astype(f32) + inv1 * (q1 - m0 / width - n1_own * (m1 / width))
    gain1_grad = jnp.sum(terms1 * n1_own, axis=1)
    input_grad = input_grad.T[None]

    big = lax.psum((w_down_grad.astype(bf16), w_gate_grad.astype(bf16), w_up_grad.astype(bf16),
                    in_grad.astype(bf16), out_proj_grad.astype(bf16)), "dp")
    wdg, wgg, wug, ing, opg = [v.astype(f32) for v in big]
    g2, g1, st, ct, fo, rt = lax.psum((gain2_own, gain1_grad, stap_grad, ctap_grad, fout_grad, rate_grad), "dp")
    fi, fb = lax.psum((fin_grad, fbias_grad), ("dp", "chan"))
    return (output, input_grad, g1, ing.reshape(width, 3, own), st, ct, fi, fb, fo, rt, opg, g2, wgg, wug, wdg)


def solution(mesh):
    rows, cols = P("dp", None, "chan"), P(None, "chan")
    in_specs = (
        rows, P("dp", None), P("chan"), P(None, None, "chan"), P(None, None, "chan"), cols, P(), P(),
        cols, P("chan"), cols, P("chan"), cols, cols, P("chan", None), rows,
    )
    out_specs = (
        rows, rows, P("chan"), P(None, None, "chan"), P(None, None, "chan"), cols, P(), P(),
        cols, P("chan"), cols, P("chan"), cols, cols, P("chan", None),
    )
    return jax.shard_map(local, mesh=mesh, in_specs=in_specs, out_specs=out_specs, check_vma=False)
```

```python
import functools
import math

import jax
import jax.numpy as jnp
import numpy as np
from jax import lax
from jax.experimental import pallas as pl
from jax.experimental.pallas import tpu as pltpu
from jax.sharding import PartitionSpec as P

highest = lax.Precision.HIGHEST
norm_eps = 1e-05
f32 = jnp.float32
bf16 = jnp.bfloat16


def band_features(seq_len, feat_count):
    bands = (feat_count - 1) // 2
    positions = np.arange(seq_len)
    orders = np.arange(1, bands + 1)
    phases = (orders[:, None] * positions[None, :] % seq_len) * (2.0 * math.pi / seq_len)
    ramp = positions[None, :] / seq_len
    return np.concatenate([ramp, np.sin(phases), np.cos(phases)], axis=0).astype(np.float32)


def wave_matrix(seq_len):
    period = 3 * seq_len // 2
    freq = period // 2
    phase = (np.arange(seq_len)[:, None] * (2 * np.arange(freq)[None, :] + 1)) % (2 * period)
    angle = phase * (math.pi / period)
    return np.concatenate([np.cos(angle), np.sin(angle)], axis=1)


def nn(a, b, precision=None):
    return lax.dot_general(a, b, (((1,), (0,)), ((), ())), precision=precision, preferred_element_type=f32)


def nt(a, b, precision=None):
    return lax.dot_general(a, b, (((1,), (1,)), ((), ())), precision=precision, preferred_element_type=f32)


def tn(a, b, precision=None):
    return lax.dot_general(a, b, (((0,), (0,)), ((), ())), precision=precision, preferred_element_type=f32)


MESH = pl.DeviceIdType.MESH
lane_tile = 256
row_tile = 16


def flipped(index, bit):
    return index + (1 << bit) * (1 - 2 * ((index // (1 << bit)) % 2))


class Line:
    def __init__(self, view, send_sem, recv_sem, at, ways):
        self.view, self.send_sem, self.recv_sem, self.at, self.ways = view, send_sem, recv_sem, at, ways

    def copy(self, way, hop, part, shard):
        ref = self.view(shard, part)
        step = 1 - 2 * way
        return pltpu.make_async_remote_copy(
            src_ref=ref, dst_ref=ref, send_sem=self.send_sem.at[way, hop, part],
            recv_sem=self.recv_sem.at[way, hop, part],
            device_id={"chan": (self.at + step + self.ways) % self.ways}, device_id_type=MESH,
        )

    def sends(self, way, hop):
        if way == 0:
            return jnp.logical_and(self.at >= hop, self.at < self.ways - 1)
        return jnp.logical_and(self.at + hop <= self.ways - 1, self.at > 0)

    def gets(self, way, hop):
        if way == 0:
            return self.at >= hop + 1
        return self.at + hop + 1 <= self.ways - 1

    def order(self, way, index):
        return index if way == 0 else self.ways - 1 - index

    def far_side(self):
        return (2 * self.at) // self.ways

    def send_own(self, wanted=True):
        for index in range(self.ways):
            for way in (0, 1):
                @pl.when(jnp.logical_and(self.sends(way, 0), wanted))
                def _():
                    self.copy(way, 0, self.order(way, index), self.at).start()

    def relay(self, way, index, wanted, hops=None):
        part, step = self.order(way, index), 1 - 2 * way
        for hop in range(1, self.ways - 1) if hops is None else hops:
            @pl.when(jnp.logical_and(self.sends(way, hop), wanted))
            def _():
                self.copy(way, hop - 1, part, self.at - hop * step).wait_recv()
                self.copy(way, hop, part, self.at - hop * step).start()

    def short_way(self, index):
        for way in (0, 1):
            self.relay(way, index, self.far_side() == way)

    def long_way(self, index, hops=None):
        for way in (0, 1):
            self.relay(way, index, self.far_side() != way, hops)

    def take(self, index):
        for way in (0, 1):
            for hop in range(self.ways - 1):
                last = self.gets(way, hop)
                if hop + 1 < self.ways - 1:
                    last = jnp.logical_and(last, jnp.logical_not(self.sends(way, hop + 1)))

                @pl.when(last)
                def _():
                    self.copy(way, hop, self.order(way, index), self.at - (hop + 1) * (1 - 2 * way)).wait_recv()

    def drain(self):
        for way in (0, 1):
            for hop in range(self.ways - 1):
                for part in range(self.ways):
                    @pl.when(self.sends(way, hop))
                    def _():
                        self.copy(way, hop, part, self.at - hop * (1 - 2 * way)).wait_send()


class LineSum:
    def __init__(self, mine, inbox, send_sem, recv_sem, at, ways, subs):
        self.mine, self.inbox, self.send_sem, self.recv_sem = mine, inbox, send_sem, recv_sem
        self.at, self.ways, self.subs = at, ways, subs

    def dest(self, way, k):
        return self.ways - 1 - k if way == 0 else k

    def sends(self, way, k):
        return self.dest(way, k) > self.at if way == 0 else self.dest(way, k) < self.at

    def gets(self, way, k):
        dest = self.dest(way, k)
        if way == 0:
            return jnp.logical_and(dest >= self.at, self.at > 0)
        return jnp.logical_and(dest <= self.at, self.at < self.ways - 1)

    def copy(self, way, k, sub):
        step = 1 - 2 * way
        return pltpu.make_async_remote_copy(
            src_ref=self.mine(self.dest(way, k), sub), dst_ref=self.inbox(way, k, sub),
            send_sem=self.send_sem.at[way, k, sub], recv_sem=self.recv_sem.at[way, k, sub],
            device_id={"chan": (self.at + step + self.ways) % self.ways}, device_id_type=MESH,
        )

    def first(self, k, sub):
        for way in (0, 1):
            @pl.when(jnp.logical_and(self.sends(way, k), jnp.logical_not(self.gets(way, k))))
            def _():
                self.copy(way, k, sub[way]).start()

    def onward(self, way, k, sub, wanted):
        @pl.when(jnp.logical_and(jnp.logical_and(self.sends(way, k), self.gets(way, k)), wanted))
        def _():
            self.copy(way, k, sub).wait_recv()
            mine, inbox = self.mine(self.dest(way, k), sub), self.inbox(way, k, sub)
            mine[...] = (mine[...].astype(f32) + inbox[...].astype(f32)).astype(bf16)
            self.copy(way, k, sub).start()

    def near(self, k, sub):
        for way in (0, 1):
            self.onward(way, k, sub[way], (2 * self.at) // self.ways == way)

    def far(self, k, sub):
        for way in (0, 1):
            self.onward(way, k, sub[way], (2 * self.at) // self.ways != way)

    def take(self, way, sub, total):
        k = self.ways - 1 - self.at if way == 0 else self.at

        @pl.when(self.at > 0 if way == 0 else self.at < self.ways - 1)
        def _():
            self.copy(way, k, sub).wait_recv()
            total[...] += self.inbox(way, k, sub)[...].astype(f32)

    def drain(self):
        for way in (0, 1):
            for k in range(self.ways):
                for sub in range(self.subs):
                    @pl.when(self.sends(way, k))
                    def _():
                        self.copy(way, k, sub).wait_send()


class RowSum:
    tile = 96

    def __init__(self, buf, result, box, extra_box, send_sem, recv_sem, r, total_bits):
        self.buf, self.result, self.box, self.extra_box = buf, result, box, extra_box
        self.send_sem, self.recv_sem = send_sem, recv_sem
        self.total_bits, self.r = total_bits, r
        height = buf.shape[0]
        core = r % 2
        steps = [1, 2 + 2 * core, 4 - 2 * core]
        self.levels = []
        base, size = 0, height
        inbox_at = 0
        for step in steps:
            size = size // 2
            bit = (r // step) % 2
            keep, give = base + bit * size, base + (1 - bit) * size
            self.levels.append((r + step * (1 - 2 * bit), keep, give, size, inbox_at))
            base = keep
            inbox_at += size

    def rows(self, at, size, buf=None):
        return (self.buf if buf is None else buf).at[pl.ds(pl.multiple_of(at, 32), size)]

    def halve(self, level):
        partner, keep, give, size, inbox_at = self.levels[level]
        return pltpu.make_async_remote_copy(
            src_ref=self.rows(give, size), dst_ref=self.box.at[pl.ds(inbox_at, size)],
            send_sem=self.send_sem.at[level], recv_sem=self.recv_sem.at[level],
            device_id={"dp": partner}, device_id_type=MESH,
        )

    def double(self, level, arriving=False):
        partner, keep, give, size, inbox_at = self.levels[level]
        part = self.rows(give if arriving else keep, size, self.result)
        return pltpu.make_async_remote_copy(
            src_ref=part, dst_ref=part, send_sem=self.send_sem.at[3 + level], recv_sem=self.recv_sem.at[3 + level],
            device_id={"dp": partner}, device_id_type=MESH,
        )

    def add(self, level, target=None):
        partner, keep, give, size, inbox_at = self.levels[level]
        target = self.buf if target is None else target
        self.halve(level).wait_recv()

        def run(i, carry):
            at = pl.ds(pl.multiple_of(keep + i * self.tile, 32), self.tile)
            there = pl.ds(pl.multiple_of(inbox_at + i * self.tile, 32), self.tile)
            target[at, :] = (self.buf[at, :].astype(f32) + self.box[there, :].astype(f32)).astype(bf16)
            return carry

        lax.fori_loop(0, size // self.tile, run, 0)

    def extra(self):
        partner, keep, give, size, inbox_at = self.levels[2]
        for bit in range(3, self.total_bits):
            copy = pltpu.make_async_remote_copy(
                src_ref=self.rows(keep, size, self.result), dst_ref=self.extra_box.at[bit - 3], send_sem=self.send_sem.at[3 + bit],
                recv_sem=self.recv_sem.at[3 + bit], device_id={"dp": flipped(self.r, bit)}, device_id_type=MESH,
            )
            copy.start()
            copy.wait()
            at = pl.ds(pl.multiple_of(keep, 32), size)
            self.result[at, :] = (self.result[at, :].astype(f32) + self.extra_box[bit - 3].astype(f32)).astype(bf16)

    def tasks(self, done):
        def second():
            self.add(0)
            self.halve(1).start()

        def third():
            self.add(1)
            self.halve(2).start()

        def turn():
            self.add(2, self.result)
            self.extra()
            self.double(2).start()

        def wider():
            self.double(2, True).wait_recv()
            self.double(1).start()

        def widest():
            self.double(1, True).wait_recv()
            self.double(0).start()

        def last():
            self.double(0, True).wait_recv()
            done()

        return [self.halve(0).start, second, third, turn, wider, widest, last]

    def drain(self):
        for level in range(3):
            self.halve(level).wait_send()
            self.double(level).wait_send()


def layer_kernel(
    cfg,
    x_hbm, g_hbm, outp_hbm, in_hbm, tab_hbm, wg_hbm, wu_hbm, wd_hbm, halves_ref, gain1_ref, gain2_ref, short_ref, cond_ref,
    rate_ref, fin_ref, fbias_ref, fout_ref, feat_ref,
    out_hbm, igrad_hbm, big_hbm, proj_hbm, small_hbm, zsum_hbm, *scratch,
):
    ways, seq, own, width, hidden, bits, all_bits = cfg
    (
        xf, gf, outt, proj, mixf, query, kv, squash, kern, mixed, hat, arg, in_t, tab, n1o, masks, cols, prow, frow,
        pieces, gains, gaincol, stat1, sig, prod, weights, n2o, mid, gg, ug, tbuf, tin, mbuf, ein,
        gb, rb, rbx, rb2, rbx2, n2own, inv2, rres, resown, pgb, mgb, mgf, pgo, sgr, kgr, sm, smbox, zbox, mom, gsum,
        load_sem, line_send, line_recv, piece_send, piece_recv, gain_send, gain_recv, save_sem,
        fs_send, fs_recv, es_send, es_recv, hs_send, hs_recv, sw_send, sw_recv,
        ar_send, ar_recv, sm_send, sm_recv, z_send, z_recv, mom_send, mom_recv,
    ) = scratch
    lags = 3 * seq // 4
    freq = lags
    block = seq // ways
    z = lax.axis_index("chan")
    r = lax.axis_index("dp")
    side = (2 * z) // ways
    inner = ((z + ways - 1) // ways) * ((2 * ways - 2 - z) // ways)
    group = r % (1 << bits)

    wd, wg, wu = (weights.at[pl.ds(at, size)] for at, size in ((0, hidden), (hidden, width), (hidden + width, width)))

    def own_rows(at):
        return pl.ds(pl.multiple_of(at * own, row_tile), own)

    def token(at):
        return pl.ds(pl.multiple_of(at * block, block), block)

    span = own_rows(z)
    saves = []

    def load(index, src, dst):
        copy = pltpu.make_async_copy(src, dst, load_sem.at[index])
        copy.start()
        return copy

    def save(src, dst):
        copy = pltpu.make_async_copy(src, dst, save_sem.at[len(saves)])
        copy.start()
        saves.append(copy)

    grain = 48
    per_piece = pieces.shape[2] // grain
    x_load = load(0, x_hbm, xf.at[span])
    g_load = load(1, g_hbm, gf.at[span])
    in_load = load(2, in_hbm, in_t)

    def piece_from(i):
        at = group * per_piece + i
        return outp_hbm.at[
            pl.ds(pl.multiple_of((at % (own // grain)) * grain, row_tile), grain),
            pl.ds(pl.multiple_of((at // (own // grain)) * 128, 128), 128)]

    piece_loads = [load(8 + i, piece_from(i), pieces.at[group, z, pl.ds(i * grain, grain)]) for i in range(per_piece)]
    tab_load = load(3, tab_hbm, tab)
    weight_loads = [load(4, wg_hbm, wg), load(5, wu_hbm, wu), load(6, wd_hbm, wd)]
    barrier = pltpu.get_barrier_semaphore()
    peers = [{"chan": (z + s) % ways} for s in range(1, ways)] + [{"dp": flipped(r, b)} for b in range(all_bits)]
    for peer in peers:
        pl.semaphore_signal(barrier, inc=1, device_id=peer, device_id_type=MESH)
    pl.semaphore_wait(barrier, len(peers))

    def cut(buf):
        return lambda shard, part: buf.at[own_rows(shard), token(part)]

    in_line, g_line, mix_line = (
        Line(cut(buf), line_send.at[i], line_recv.at[i], z, ways) for i, buf in enumerate((xf, gf, mixf)))

    class Direct:
        def __init__(self, view_src, view_dst, send, recv):
            self.view_src, self.view_dst, self.send, self.recv = view_src, view_dst, send, recv

        def copy(self, s, arriving):
            there = (z + s) % ways
            src = (z + ways - s) % ways
            dst = self.view_dst(src if arriving else z)
            return pltpu.make_async_remote_copy(
                src_ref=dst if arriving else self.view_src(there), dst_ref=dst, send_sem=self.send.at[s],
                recv_sem=self.recv.at[s], device_id={"chan": there}, device_id_type=MESH,
            )

        def start(self, wanted=None):
            for s in range(1, ways):
                if wanted is None:
                    self.copy(s, False).start()
                else:
                    @pl.when(wanted((z + s) % ways))
                    def _():
                        self.copy(s, False).start()

        def wait_recv(self):
            for s in range(1, ways):
                self.copy(s, True).wait_recv()

        def drain(self):
            for s in range(1, ways):
                self.copy(s, False).wait_send()

    gain_msg = Direct(lambda to: gains.at[z], lambda at: gains.at[at], gain_send, gain_recv)
    piece_msg = Direct(lambda to: pieces.at[group, z], lambda at: pieces.at[group, at], piece_send, piece_recv)

    gains[z] = jnp.zeros(gains.shape[1:], f32)
    gains[z, 0:1, 0:own] = gain1_ref[...]
    gains[z, 1:2, 0:own] = gain2_ref[...]
    gain_msg.start()
    x_load.wait()
    in_line.send_own()

    def inside(at):
        return jnp.logical_and(at > 0, at < ways - 1)

    def early(there):
        return jnp.logical_or(inside(there), inner == 0)

    for copy in piece_loads:
        copy.wait()
    piece_msg.start(early)

    line_at = lax.broadcasted_iota(jnp.int32, (1, seq), 1)
    split, valid = halves_ref[0, 0], halves_ref[0, 1]
    masks[0:1, :] = jnp.where(line_at < split, 1.0, 0.0)
    masks[1:2, :] = jnp.where(jnp.logical_and(line_at >= split, line_at < valid), 1.0, 0.0)
    masks[2:3, :] = masks[0:1, :] + masks[1:2, :]
    prow[...] = jnp.zeros(prow.shape, f32)
    for i in range(3):
        for j in range(3):
            prow[3 * i + j : 3 * i + j + 1, 0:own] = short_ref[i, j : j + 1, :]
    prow[9:12, 0:own] = cond_ref[...]
    prow[12:13, 0:own] = rate_ref[...]
    prow[64:128, 0:own] = fout_ref[...]
    cols[...] = prow[...].T[0:own, :]
    frow[...] = jnp.zeros(frow.shape, f32)
    frow[0 : fin_ref.shape[0], :] = fin_ref[...]
    frow[fin_ref.shape[0] : fin_ref.shape[0] + 1, :] = fbias_ref[...]
    g_load.wait()
    gf[span, :] = (gf[span, :].astype(f32) * masks[2:3, :]).astype(bf16)

    arg[...] = tn(frow[...], feat_ref[...], highest)
    kern[...] = nn(cols[:, 64:128], jnp.sin(arg[...]), highest)

    gain_msg.wait_recv()
    eye = lax.broadcasted_iota(jnp.int32, (own, gains.shape[2]), 0) == lax.broadcasted_iota(
        jnp.int32, (own, gains.shape[2]), 1)
    for s in range(ways):
        for which in range(2):
            row = gains[s, which : which + 1, :]
            gaincol[s * own : (s + 1) * own, which : which + 1] = jnp.sum(jnp.where(eye, row, 0.0), axis=1, keepdims=True)
    in_load.wait()

    def moments(values):
        centre = jnp.sum(values, axis=0, keepdims=True) * (1.0 / width)
        spread = jnp.sum(values * values, axis=0, keepdims=True) * (1.0 / width) - centre * centre
        return centre, lax.rsqrt(spread + norm_eps)

    def in_order(index):
        return side * index + (1 - side) * (ways - 1 - index)

    def norm1(q):
        at = token(q)
        values = xf[:, at].astype(f32)
        centre, inverse = moments(values)
        stat1[0:1, at] = centre
        stat1[1:2, at] = inverse
        low = ((values - centre) * inverse * gaincol[:, 0:1]).astype(bf16)
        n1o[:, at] = low
        proj[:, at] = nn(in_t[...], low)

    for index in range(ways):
        in_line.short_way(index)
        if index < 2:
            in_line.long_way(index)
    for index in range(ways):
        if index + 2 < ways:
            in_line.long_way(index + 2)
        in_line.take(index)
        norm1(in_order(index))
    g_line.send_own(inner == 0)

    piece_sends = []

    def piece_step(bit, held, slot):
        batch = []
        for i, piece in enumerate(held):
            def make(which, slot=slot + i):
                return pltpu.make_async_remote_copy(
                    src_ref=pieces.at[which], dst_ref=pieces.at[which], send_sem=piece_send.at[slot],
                    recv_sem=piece_recv.at[slot], device_id={"dp": flipped(r, bit)}, device_id_type=MESH,
                )
            make(piece).start()
            batch.append((make, piece))
            piece_sends.append((make, piece))

        def finish():
            for make, piece in batch:
                make(flipped(piece, bit)).wait_recv()
        return finish, held + [flipped(piece, bit) for piece in held], slot + len(held)

    tab_load.wait()

    lane = lax.broadcasted_iota(jnp.int32, (row_tile, seq), 1)
    place = lane.astype(f32)
    half1, half2 = masks[0:1, :], masks[1:2, :]

    def back(values, steps):
        if steps == 0:
            return values
        return jnp.where(lane >= steps, pltpu.roll(values, steps, 1), 0.0)

    def ahead(values, steps):
        if steps == 0:
            return values
        return jnp.where(lane < seq - steps, pltpu.roll(values, seq - steps, 1), 0.0)

    def row_at(j, i):
        return pl.ds(pl.multiple_of(j * own + i * row_tile, row_tile), row_tile)

    def decay_of(tap):
        return jnp.exp(-tap[:, 12:13] * place) * (1.0 / math.sqrt(seq))

    def mix_rows(i, carry):
        here = row_at(0, i)
        tap = cols[here, :]
        outs = []
        for j in range(3):
            part = proj[row_at(j, i), :]
            outs.append(sum(tap[:, 3 * k + j : 3 * k + j + 1] * back(part, k) for k in range(3)))
        query[here, :] = outs[0]
        kv[here, :] = outs[1]
        kv[row_at(1, i), :] = outs[2]
        cond = sum(tap[:, 9 + k : 10 + k] * back(outs[2], k) for k in range(3))
        bent = jnp.tanh(cond)
        squash[here, :] = bent
        filt = (kern[here, :] + bent) * decay_of(tap)
        kern[here, :] = filt
        source = outs[1] * outs[2]
        sig[row_at(0, i), :] = jnp.where(lane < lags, filt, 0.0).astype(bf16)
        sig[row_at(1, i), :] = (source * half1).astype(bf16)
        sig[row_at(2, i), :] = (source * half2).astype(bf16)
        return carry

    lax.fori_loop(0, own // row_tile, mix_rows, 0)
    def freq_at(j):
        return (pl.ds(pl.multiple_of(j * lane_tile, lane_tile), lane_tile),
                pl.ds(pl.multiple_of(freq + j * lane_tile, lane_tile), lane_tile))

    def freq_tile(j, carry):
        re_at, im_at = freq_at(j)
        re = nn(sig[...], tab[:, re_at])
        im = nn(sig[...], tab[:, im_at])
        hat[:, re_at] = re.astype(bf16)
        hat[:, im_at] = im.astype(bf16)
        kr, ki = re[:own], im[:own]
        for h in range(2):
            sr, si = re[own * (h + 1) : own * (h + 2)], im[own * (h + 1) : own * (h + 2)]
            prod[own * h : own * (h + 1), re_at] = (kr * sr - ki * si).astype(bf16)
            prod[own * h : own * (h + 1), im_at] = (kr * si + ki * sr).astype(bf16)
        return carry

    lax.fori_loop(0, freq // lane_tile, freq_tile, 0)
    g_line.send_own(inner == 1)
    piece_msg.start(lambda there: jnp.logical_not(early(there)))

    def time_tile(j, carry):
        at = token(j)
        both = nt(prod[0 : 2 * own, :], tab[at, :])
        total = (both[:own] * masks[0:1, at] + both[own:] * masks[1:2, at]) * (1.0 / freq)
        mixed[:, at] = total
        mixf[span, at] = (query[:, at] * total).astype(bf16)
        return carry

    lax.fori_loop(0, ways, time_tile, 0)

    mix_line.send_own()
    piece_msg.wait_recv()
    held, slot = [group], ways
    for bit in reversed(range(bits)):
        finish, held, slot = piece_step(bit, held, slot)
        if bit == bits - 1:
            for index in range(ways):
                g_line.short_way(index)
        finish()
    next_hops, last_hops = range(1, 2), range(2, ways - 1)
    mix_line.long_way(0, next_hops)
    mix_line.short_way(0)
    mix_line.long_way(0, last_hops)
    for s in range(ways):
        for block_at in range(own * width // 128 // grain):
            piece, inside_at = divmod(block_at, per_piece)
            column, down = divmod(block_at, own // grain)
            outt[s * own + down * grain : s * own + (down + 1) * grain, 128 * column : 128 * column + 128] = pieces[
                piece, s, inside_at * grain : (inside_at + 1) * grain, :]
    for copy in weight_loads:
        copy.wait()
    g_line.long_way(0)
    mix_line.short_way(1)
    mix_line.long_way(1)
    g_line.long_way(1)
    for index in range(2, ways):
        mix_line.short_way(index)

    half_block = block // 2

    def half_token(at, sub):
        return pl.ds(pl.multiple_of(at * block + sub * half_block, half_block), half_block)

    f_sum = LineSum(
        lambda dest, sub: tbuf.at[:, half_token(dest, sub)],
        lambda way, k, sub: tin.at[way, k, :, pl.ds(sub * half_block, half_block)],
        fs_send, fs_recv, z, ways, 2)
    e_sum = LineSum(
        lambda dest, sub: mbuf.at[own_rows(dest), token(sub)],
        lambda way, k, sub: ein.at[way, k, :, token(sub)],
        es_send, es_recv, z, ways, ways)

    def by_end(index):
        return (ways - 1 - index, index)

    halves_of = [(sub, sub) for sub in range(2)]
    plain_order = [(sub, sub) for sub in range(ways)]

    def tiles(count, fn):
        def run(j, carry):
            fn(pl.ds(pl.multiple_of(j * lane_tile, lane_tile), lane_tile))
            return carry
        lax.fori_loop(0, count // lane_tile, run, 0)

    def forward(q):
        at = token(q)
        rres[...] = xf[:, at].astype(f32) + nn(outt[...], mixf[:, at])
        resown[:, at] = rres[span, :]
        centre, inverse = moments(rres[...])
        n2o[:, at] = ((rres[...] - centre) * inverse * gaincol[:, 1:2]).astype(bf16)

        @pl.when(q == z)
        def _():
            n2own[...] = (rres[...] - centre) * inverse
            inv2[0:1, :] = inverse

        def hidden_tile(fs):
            low = n2o[:, at]
            gate = tn(wg[:, fs], low)
            up = tn(wu[:, fs], low)
            bent = jax.nn.sigmoid(gate)
            act = gate * bent
            mid[fs, at] = (act * up).astype(bf16)
            gg[fs, at] = (up * bent * (1.0 + gate * (1.0 - bent))).astype(bf16)
            ug[fs, at] = act.astype(bf16)

        tiles(hidden, hidden_tile)

        def mlp_tile(ds):
            mbuf[ds, at] = tn(wd[:, ds], mid[:, at]).astype(bf16)

        tiles(width, mlp_tile)

    def backward(q):
        at = token(q)

        def back_tile(fs):
            grad = nn(wd[fs, :], gf[:, at])
            gg[fs, at] = (grad * gg[fs, at].astype(f32)).astype(bf16)
            ug[fs, at] = (grad * ug[fs, at].astype(f32)).astype(bf16)

        tiles(hidden, back_tile)

        def term_tile(ds):
            tbuf[ds, at] = (nn(wg[ds, :], gg[:, at]) + nn(wu[ds, :], ug[:, at])).astype(bf16)

        tiles(width, term_tile)

    def turn_of(index):
        if index == ways - 2:
            return index + inner
        if index == ways - 1:
            return index - inner
        return index

    for index in range(ways):
        if 0 < index < ways - 1:
            mix_line.long_way(index + 1)
            g_line.long_way(index + 1)
        q = in_order(turn_of(index))
        mix_line.take(index)
        forward(q)
        if index == 0:
            for k in range(ways - 1):
                e_sum.first(k, by_end(0))
        if index == 2:
            f_sum.near(0, halves_of[1])
        if index == 3:
            f_sum.far(0, halves_of[1])
            f_sum.near(1, halves_of[0])
        g_line.take(index)
        backward(q)
        if index < ways - 1:
            for sub in halves_of:
                f_sum.first(index, sub)
        if index == 1:
            f_sum.near(0, halves_of[0])
        if index == 2:
            f_sum.far(0, halves_of[0])
    f_sum.near(1, halves_of[1])
    for k in range(ways - 1):
        e_sum.first(k, by_end(1))

    def weight_grad(lhs, rhs, place_at):
        def run(j, carry):
            at = pl.ds(pl.multiple_of(j * lane_tile, lane_tile), lane_tile)
            gb[pl.ds(pl.multiple_of(place_at + j * lane_tile, lane_tile), lane_tile), :] = nt(
                lhs[at, :], rhs[...]).astype(bf16)
            return carry
        lax.fori_loop(0, lhs.shape[0] // lane_tile, run, 0)

    def weight_grads():
        weight_grad(mid, gf, 0)
        weight_grad(n2o, gg, hidden)
        weight_grad(n2o, ug, hidden + width)

    pl.when(inner == 1)(weight_grads)
    big = RowSum(gb, weights, rb, rbx, ar_send.at[0], ar_recv.at[0], r, all_bits)
    big_tasks = big.tasks(lambda: save(weights, big_hbm))

    rres[...] = tbuf[:, token(z)].astype(f32)
    for sub in range(2):
        for way in (0, 1):
            f_sum.take(way, sub, rres.at[:, pl.ds(sub * half_block, half_block)])
    upstream = rres[...] * gaincol[:, 1:2]
    normed = n2own[...]
    plain = jnp.sum(upstream, axis=0, keepdims=True) * (1.0 / width)
    cross = jnp.sum(upstream * normed, axis=0, keepdims=True) * (1.0 / width)
    pgb[...] = (gf[:, token(z)].astype(f32) + inv2[0:1, :] * (upstream - plain - normed * cross)).astype(bf16)
    mgb[...] = tn(outt[...], pgb[...]).astype(bf16)
    swap_mix = Direct(lambda to: mgb.at[own_rows(to)], lambda at: mgf.at[:, token(at)], sw_send.at[0], sw_recv.at[0])
    swap_proj = Direct(lambda to: pgb.at[own_rows(to)], lambda at: pgo.at[:, token(at)], sw_send.at[1], sw_recv.at[1])
    swap_mix.start()
    swap_proj.start()
    mgf[:, token(z)] = mgb[span, :]
    pgo[:, token(z)] = pgb[span, :]
    ones = jnp.ones((8, block), bf16)
    gsum[ways] = nt(ones, (rres[...] * normed).astype(bf16))

    for index in range(2, ways):
        for k in range(ways - 1):
            e_sum.first(k, by_end(index))
    pl.when(inner == 0)(weight_grads)
    big_tasks.pop(0)()
    swap_mix.wait_recv()

    def grad_rows(i, carry):
        here = row_at(0, i)
        down = mgf[here, :].astype(f32) * query[here, :]
        sig[row_at(0, i), :] = (down * half1).astype(bf16)
        sig[row_at(1, i), :] = (down * half2).astype(bf16)
        return carry

    lax.fori_loop(0, own // row_tile, grad_rows, 0)

    def grad_freq(j, carry):
        re_at, im_at = freq_at(j)
        re = nn(sig[0 : 2 * own, :], tab[:, re_at])
        im = nn(sig[0 : 2 * own, :], tab[:, im_at])
        hr, hi = hat[:, re_at].astype(f32), hat[:, im_at].astype(f32)
        kr, ki = hr[:own], hi[:own]
        kg_re, kg_im = 0.0, 0.0
        for h in range(2):
            mr, mi = re[own * h : own * (h + 1)], im[own * h : own * (h + 1)]
            sr, si = hr[own * (h + 1) : own * (h + 2)], hi[own * (h + 1) : own * (h + 2)]
            prod[own * h : own * (h + 1), re_at] = (kr * mr + ki * mi).astype(bf16)
            prod[own * h : own * (h + 1), im_at] = (kr * mi - ki * mr).astype(bf16)
            kg_re = kg_re + sr * mr + si * mi
            kg_im = kg_im + sr * mi - si * mr
        prod[2 * own : 3 * own, re_at] = kg_re.astype(bf16)
        prod[2 * own : 3 * own, im_at] = kg_im.astype(bf16)
        return carry

    lax.fori_loop(0, freq // lane_tile, grad_freq, 0)
    big_tasks.pop(0)()

    def grad_time(j, carry):
        at = token(j)
        all3 = nt(prod[...], tab[at, :])
        sgr[:, at] = (all3[:own] * masks[0:1, at] + all3[own : 2 * own] * masks[1:2, at]) * (1.0 / freq)
        kgr[:, at] = all3[2 * own :] * (1.0 / freq)
        return carry

    lax.fori_loop(0, ways, grad_time, 0)

    def chain_rows(i, carry):
        here = row_at(0, i)
        tap = cols[here, :]
        stat = jnp.zeros((row_tile, 128), f32)
        column = lax.broadcasted_iota(jnp.int32, (row_tile, 128), 1)

        def note(stat, index, values):
            return jnp.where(column == index, jnp.sum(values, axis=1, keepdims=True), stat)

        key, value = kv[here, :], kv[row_at(1, i), :]
        kgrad = jnp.where(lane < lags, kgr[here, :], 0.0)
        base_grad = kgrad * decay_of(tap)
        kgr[here, :] = base_grad
        stat = note(stat, 12, -kgrad * kern[here, :] * place)
        bent = squash[here, :]
        cond_grad = base_grad * (1.0 - bent * bent)
        sgrad = sgr[here, :]
        value_grad = sgrad * key
        for k in range(3):
            moved = ahead(cond_grad, k)
            stat = note(stat, 9 + k, moved * value)
            value_grad = value_grad + tap[:, 9 + k : 10 + k] * moved
        branch = (mgf[here, :].astype(f32) * mixed[here, :], sgrad * value, value_grad)
        for j in range(3):
            part = proj[row_at(j, i), :]
            total = 0.0
            for k in range(3):
                moved = ahead(branch[j], k)
                stat = note(stat, 3 * k + j, moved * part)
                total = total + tap[:, 3 * k + j : 3 * k + j + 1] * moved
            sig[row_at(j, i), :] = total.astype(bf16)
        sm[here, :] = stat
        return carry

    lax.fori_loop(0, own // row_tile, chain_rows, 0)

    h_sum = LineSum(
        lambda dest, sub: tbuf.at[own_rows(dest), token(sub)],
        lambda way, k, sub: tin.at[way, k, own_rows(sub), :],
        hs_send, hs_recv, z, ways, ways)
    f_sum.drain()
    mom_msg = Direct(lambda to: mom.at[z], lambda at: mom.at[at], mom_send, mom_recv)

    def in_back(tile):
        at = token(tile)
        rres[...] = tn(in_t[...], sig[:, at])
        tbuf[:, at] = rres[...].astype(bf16)
        h_sum.first(0, plain_order[tile])
        normed = (xf[:, at].astype(f32) - stat1[0:1, at]) * stat1[1:2, at]
        upstream = rres[...] * gaincol[:, 0:1]
        mom[z, 0:1, at] = jnp.sum(upstream, axis=0, keepdims=True)
        mom[z, 1:2, at] = jnp.sum(upstream * normed, axis=0, keepdims=True)
        gsum[tile] = nt(ones, (rres[...] * normed).astype(bf16))

    gb2 = gg.at[0 : 4 * own, 0:width]
    sum2 = mid.at[0 : 4 * own, 0:width]

    def proj_grad(lhs, rhs, place_at):
        gb2[place_at : place_at + lhs.shape[0], :] = nt(lhs[...], rhs[...]).astype(bf16)

    two = RowSum(gb2, sum2, rb2, rbx2, ar_send.at[1], ar_recv.at[1], r, all_bits)
    two_tasks = two.tasks(lambda: save(sum2, proj_hbm))

    def small_copy(b):
        return pltpu.make_async_remote_copy(
            src_ref=sm, dst_ref=smbox.at[b], send_sem=sm_send.at[b], recv_sem=sm_recv.at[b],
            device_id={"dp": flipped(r, b)}, device_id_type=MESH,
        )

    def small_step(b):
        small_copy(b).wait()
        sm[...] += smbox[b]
        if b + 1 < all_bits:
            small_copy(b + 1).start()

    def near(summer, k, index):
        summer.near(k, by_end(index) if summer is e_sum else plain_order[index])

    def far(summer, k, index):
        summer.far(k, by_end(index) if summer is e_sum else plain_order[index])

    total = rres.at[0:own, :]

    def output_part(tile):
        at = token(tile)
        total[...] = mbuf[span, at].astype(f32)
        for way in (0, 1):
            e_sum.take(way, tile, total)
        resown[:, at] = (resown[:, at] + total[...]) * masks[2:3, at]
        save(resown.at[:, at], out_hbm.at[:, at])

    def input_part(tile):
        at = token(tile)
        total[...] = tbuf[span, at].astype(f32)
        for way in (0, 1):
            h_sum.take(way, tile, total)
        sums = sum(mom[s, :, at] for s in range(ways)) * (1.0 / width)
        inverse = stat1[1:2, at]
        normed = (xf[span, at].astype(f32) - stat1[0:1, at]) * inverse
        upstream = total[...] * gaincol[span, 0:1]
        sgr[:, at] = pgo[:, at].astype(f32) + inverse * (upstream - sums[0:1, :] - normed * sums[1:2, :])
        save(sgr.at[:, at], igrad_hbm.at[:, at])

    for index in range(ways):
        near(e_sum, 0, index)
    in_back(0)
    in_back(1)
    swap_proj.wait_recv()
    proj_grad(sig, n1o, 0)
    proj_grad(pgo, mixf, 3 * own)
    two_tasks.pop(0)()
    near(h_sum, 0, 0)
    in_back(2)
    near(h_sum, 0, 1)
    in_back(3)
    for k in range(1, ways - 1):
        for tile in range(ways):
            h_sum.first(k, plain_order[tile])
    mom_msg.start()
    for index in range(ways):
        near(e_sum, 1, index)
    for index in range(ways):
        far(e_sum, 0, index)
    near(h_sum, 0, 2)
    two_tasks.pop(0)()
    far(h_sum, 0, 0)
    big_tasks.pop(0)()

    wave_grad = tn(cols[:, 64:128], kgr[...], highest) * jnp.cos(arg[...])
    sm[0:own, 64:128] = nt(kgr[...], jnp.sin(arg[...]), highest)
    near(h_sum, 0, 3)
    far(h_sum, 0, 1)
    sm[own : own + 64, 0:64] = nt(feat_ref[...], wave_grad, highest)
    sm[own : own + 64, 64:128] = jnp.zeros((64, 64), f32)
    sm[own + 64 :, :] = jnp.zeros((16, 128), f32)
    for b in range(width // 128):
        lanes = slice(128 * b, 128 * b + 128)
        sm[own + 64 + b : own + 65 + b, :] = sum(gsum[tile, 0:1, lanes] for tile in range(ways))
        sm[own + 72 + b : own + 73 + b, :] = gsum[ways, 0:1, lanes]
    small_copy(0).start()
    far(h_sum, 0, 2)
    two_tasks.pop(0)()
    near(h_sum, 1, 0)
    far(h_sum, 0, 3)
    small_step(0)
    near(h_sum, 1, 1)
    big_tasks.pop(0)()
    for tile in range(ways):
        output_part(tile)
    near(h_sum, 1, 2)
    two_tasks.pop(0)()
    small_step(1)
    near(h_sum, 1, 3)
    two_tasks.pop(0)()
    big_tasks.pop(0)()
    for b in range(2, all_bits):
        small_step(b)
    z_msg = Direct(lambda to: zbox.at[z], lambda at: zbox.at[at], z_send, z_recv)
    zbox[z] = sm[own:, :]
    z_msg.start()
    save(sm, small_hbm)
    mom_msg.wait_recv()
    input_part(0)
    two_tasks.pop(0)()
    input_part(1)
    big_tasks.pop(0)()
    two_tasks.pop(0)()
    input_part(2)
    big_tasks.pop(0)()
    z_msg.wait_recv()
    zsum = zbox[0]
    for s in range(1, ways):
        zsum = zsum + zbox[s]
    zout = kern.at[0 : zsum.shape[0], 0:128]
    zout[...] = zsum
    save(zout, zsum_hbm)
    input_part(3)

    for line in (in_line, g_line, mix_line, e_sum, h_sum, gain_msg, piece_msg, swap_mix, swap_proj, mom_msg, z_msg, big, two):
        line.drain()
    for make, piece in piece_sends:
        make(piece).wait_send()
    for copy in saves:
        copy.wait()


def layer(cfg, x_own, g_own, out_t, in_t, table, w_gate, w_up, w_down, halves, gain1, gain2, short_taps, cond_taps, rates,
          filter_in, filter_bias, filter_out, feats):
    ways, seq, own, width, hidden, bits, all_bits = cfg
    period = 3 * seq // 2
    block = seq // ways
    big_rows = hidden + 2 * width
    assert hidden == width
    held = dict(
        xf=((width, seq), bf16), gf=((width, seq), bf16), outt=((width, width), bf16), proj=((3 * own, seq), f32),
        mixf=((width, seq), bf16), query=((own, seq), f32), kv=((2 * own, seq), f32), squash=((own, seq), f32), kern=((own, seq), f32),
        mixed=((own, seq), f32), hat=((3 * own, period), bf16), arg=((64, seq), f32), in_t=((3 * own, width), bf16),
        tab=((seq, period), bf16), n1o=((width, seq), bf16), masks=((8, seq), f32), cols=((own, 128), f32),
        prow=((128, 256), f32), frow=((64, 64), f32),
        pieces=((1 << bits, ways, own * width // 128 // (1 << bits), 128), bf16), gains=((ways, 8, 256), f32),
        gaincol=((width, 128), f32), stat1=((8, seq), f32), sig=((3 * own, seq), bf16), prod=((3 * own, period), bf16),
        weights=((big_rows, width), bf16), n2o=((width, seq), bf16),
        mid=((hidden, seq), bf16), gg=((hidden, seq), bf16), ug=((hidden, seq), bf16), tbuf=((width, seq), bf16),
        tin=((2, ways - 1, width, block), bf16), mbuf=((width, seq), bf16), ein=((2, ways - 1, own, seq), bf16),
        gb=((big_rows, width), bf16), rb=((big_rows * 7 // 8, width), bf16),
        rbx=((max(all_bits - 3, 1), big_rows // 8 if all_bits > 3 else 16, width), bf16),
        rb2=((4 * own * 7 // 8, width), bf16),
        rbx2=((max(all_bits - 3, 1), 4 * own // 8 if all_bits > 3 else 16, width), bf16),
        n2own=((width, block), f32), inv2=((8, block), f32), rres=((width, block), f32), resown=((own, seq), f32),
        pgb=((width, block), bf16), mgb=((width, block), bf16), mgf=((own, seq), bf16), pgo=((own, seq), bf16),
        sgr=((own, seq), f32), kgr=((own, seq), f32), sm=((own + 80, 128), f32),
        smbox=((all_bits, own + 80, 128), f32), zbox=((ways, 80, 128), f32),
        mom=((ways, 8, seq), f32), gsum=((ways + 1, 8, width), f32),
    )
    hops = (3, 2, ways - 1, ways)
    sems = dict(
        load_sem=(16,), line_send=hops, line_recv=hops, piece_send=(ways + (1 << bits),), piece_recv=(ways + (1 << bits),),
        gain_send=(ways,), gain_recv=(ways,), save_sem=(24,), fs_send=(2, ways, 2), fs_recv=(2, ways, 2),
        es_send=(2, ways, ways), es_recv=(2, ways, ways), hs_send=(2, ways, ways), hs_recv=(2, ways, ways),
        sw_send=(2, ways), sw_recv=(2, ways), ar_send=(2, 3 + max(all_bits, 3)), ar_recv=(2, 3 + max(all_bits, 3)),
        sm_send=(all_bits,), sm_recv=(all_bits,), z_send=(ways,), z_recv=(ways,), mom_send=(ways,), mom_recv=(ways,),
    )
    here = pl.BlockSpec(memory_space=pltpu.VMEM)
    there = pl.BlockSpec(memory_space=pl.ANY)
    outs = [
        ((own, seq), f32), ((own, seq), f32), ((big_rows, width), bf16), ((4 * own, width), bf16),
        ((own + 80, 128), f32), ((80, 128), f32),
    ]
    return pl.pallas_call(
        functools.partial(layer_kernel, cfg),
        out_shape=[jax.ShapeDtypeStruct(s, t) for s, t in outs],
        in_specs=[there] * 8 + [pl.BlockSpec(memory_space=pltpu.SMEM)] + [here] * 9,
        out_specs=[there] * len(outs),
        scratch_shapes=[pltpu.VMEM(s, t) for s, t in held.values()] + [
            pltpu.SemaphoreType.DMA(s) for s in sems.values()],
        compiler_params=pltpu.CompilerParams(collective_id=0, has_side_effects=True, vmem_limit_bytes=64 << 20),
    )(x_own, g_own, out_t, in_t, table, w_gate, w_up, w_down, halves, gain1, gain2, short_taps, cond_taps, rates,
      filter_in, filter_bias, filter_out, feats)


def local(
    hidden_in, halves, norm1_gain, in_proj, short_taps, cond_taps, filter_in, filter_bias,
    filter_out, decay_rate, out_proj, norm2_gain, w_gate, w_up, w_down, out_grad,
):
    seq, own = hidden_in.shape[1], hidden_in.shape[2]
    ways, rows = lax.axis_size("chan"), lax.axis_size("dp")
    width, hidden = own * ways, w_gate.shape[1]
    z = lax.axis_index("chan")
    all_bits = rows.bit_length() - 1
    cfg = (ways, seq, own, width, hidden, 3, all_bits)
    count = filter_in.shape[0]
    feat_np = np.concatenate([
        band_features(seq, count), np.ones((1, seq), np.float32), np.zeros((63 - count, seq), np.float32)])
    table = jnp.asarray(wave_matrix(seq).astype(np.float32)).astype(bf16)

    output, input_grad, big, two, small, zsum = layer(
        cfg, hidden_in[0].T, out_grad[0].T, out_proj.T, in_proj.transpose(1, 2, 0).reshape(3 * own, width), table,
        w_gate, w_up, w_down, halves, norm1_gain[None], norm2_gain[None], short_taps, cond_taps, decay_rate[None],
        filter_in, filter_bias[None], filter_out, jnp.asarray(feat_np))

    stats = small[:own].T
    gain_sums = zsum[64:].reshape(2, 8 * 128)
    mine = lax.dynamic_slice_in_dim(gain_sums, z * own, own, 1)
    in_grad = two[: 3 * own].astype(f32).reshape(3, own, width).transpose(2, 0, 1)
    out_grad_sum = two[3 * own :].astype(f32).T
    return (
        output.T[None], input_grad.T[None], mine[0], in_grad, stats[:9].reshape(3, 3, own),
        stats[9:12], zsum[:count, :64], zsum[count, :64], stats[64:128], stats[12], out_grad_sum, mine[1],
        big[hidden : hidden + width].astype(f32), big[hidden + width :].astype(f32), big[:hidden].astype(f32),
    )


def solution(mesh):
    rows, cols = P("dp", None, "chan"), P(None, "chan")
    in_specs = (
        rows, P("dp", None), P("chan"), P(None, None, "chan"), P(None, None, "chan"), cols, P(), P(),
        cols, P("chan"), cols, P("chan"), cols, cols, P("chan", None), rows,
    )
    out_specs = (
        rows, rows, P("chan"), P(None, None, "chan"), P(None, None, "chan"), cols, P(), P(),
        cols, P("chan"), cols, P("chan"), cols, cols, P("chan", None),
    )
    return jax.shard_map(local, mesh=mesh, in_specs=in_specs, out_specs=out_specs, check_vma=False)
```

```python
import functools
import math

import jax
import jax.numpy as jnp
import numpy as np
from jax import lax
from jax.experimental import pallas as pl
from jax.experimental.pallas import tpu as pltpu
from jax.sharding import PartitionSpec as P

highest = lax.Precision.HIGHEST
norm_eps = 1e-05
f32 = jnp.float32
bf16 = jnp.bfloat16


def band_features(seq_len, feat_count):
    bands = (feat_count - 1) // 2
    positions = np.arange(seq_len)
    orders = np.arange(1, bands + 1)
    phases = (orders[:, None] * positions[None, :] % seq_len) * (2.0 * math.pi / seq_len)
    ramp = positions[None, :] / seq_len
    return np.concatenate([ramp, np.sin(phases), np.cos(phases)], axis=0).astype(np.float32)


def wave_matrix(seq_len):
    period = 3 * seq_len // 2
    freq = period // 2
    phase = (np.arange(seq_len)[:, None] * (2 * np.arange(freq)[None, :] + 1)) % (2 * period)
    angle = phase * (math.pi / period)
    return np.concatenate([np.cos(angle), np.sin(angle)], axis=1)


def nn(a, b, precision=None):
    return lax.dot_general(a, b, (((1,), (0,)), ((), ())), precision=precision, preferred_element_type=f32)


def nt(a, b, precision=None):
    return lax.dot_general(a, b, (((1,), (1,)), ((), ())), precision=precision, preferred_element_type=f32)


def tn(a, b, precision=None):
    return lax.dot_general(a, b, (((0,), (0,)), ((), ())), precision=precision, preferred_element_type=f32)


MESH = pl.DeviceIdType.MESH
lane_tile = 256
row_tile = 16


def flipped(index, bit):
    return index + (1 << bit) * (1 - 2 * ((index // (1 << bit)) % 2))


def both(first, second):
    if second is True:
        return first
    return second if first is True else jnp.logical_and(first, second)


class Line:
    def __init__(self, view, send_sem, recv_sem, at, ways):
        self.view, self.send_sem, self.recv_sem, self.at, self.ways = view, send_sem, recv_sem, at, ways
        self.pending, self.arrived = {}, set()

    def copy(self, way, hop, part, shard):
        ref = self.view(shard, part)
        step = 1 - 2 * way
        return pltpu.make_async_remote_copy(
            src_ref=ref, dst_ref=ref, send_sem=self.send_sem.at[way, hop, part],
            recv_sem=self.recv_sem.at[way, hop, part],
            device_id={"chan": (self.at + step + self.ways) % self.ways}, device_id_type=MESH,
        )

    def sends(self, way, hop):
        if way == 0:
            return jnp.logical_and(self.at >= hop, self.at < self.ways - 1)
        return jnp.logical_and(self.at + hop <= self.ways - 1, self.at > 0)

    def gets(self, way, hop):
        if way == 0:
            return self.at >= hop + 1
        return self.at + hop + 1 <= self.ways - 1

    def order(self, way, index):
        return index if way == 0 else self.ways - 1 - index

    def far_side(self):
        return (2 * self.at) // self.ways

    def launch(self, hop, way, index, wanted, wait_first):
        part, step = self.order(way, index), 1 - 2 * way

        @pl.when(both(self.sends(way, hop), wanted()))
        def _():
            if wait_first:
                self.copy(way, hop - 1, part, self.at - hop * step).wait_recv()
            self.copy(way, hop, part, self.at - hop * step).start()

        def left(also):
            @pl.when(both(both(self.sends(way, hop), wanted()), also))
            def _():
                self.copy(way, hop, part, self.at - hop * step).wait_send()

        self.pending.setdefault((hop, way, index), []).append(left)

    def settle(self, hops, indices, wanted=True):
        for key in [k for k in self.pending if k[0] in hops and k[2] in indices]:
            before = self.pending.pop(key)
            for left in before:
                left(wanted)
            if wanted is not True:
                self.pending[key] = [
                    lambda also, left=left: left(both(jnp.logical_not(wanted), also)) for left in before]

    def send_own(self, indices, wanted, inward=None):
        for index in indices:
            for way in (0, 1):
                def ok(way=way):
                    if inward is None:
                        return wanted
                    facing = self.far_side() == way
                    return both(wanted, facing if inward else jnp.logical_not(facing))
                self.launch(0, way, index, ok, False)

    def relay(self, way, index, wanted, hops=None, wait_first=True):
        for hop in range(1, self.ways - 1) if hops is None else hops:
            self.launch(hop, way, index, wanted, wait_first)

    def short_way(self, index):
        for way in (0, 1):
            self.relay(way, index, lambda way=way: self.far_side() == way)

    def long_way(self, index, hops=None):
        for way in (0, 1):
            self.relay(way, index, lambda way=way: self.far_side() != way, hops, index not in self.arrived)

    def arrive(self, index):
        self.arrived.add(index)
        for way in (0, 1):
            for hop in range(1, self.ways - 1):
                @pl.when(jnp.logical_and(self.sends(way, hop), self.far_side() != way))
                def _():
                    self.copy(way, hop - 1, self.order(way, index), self.at - hop * (1 - 2 * way)).wait_recv()

    def take(self, index):
        for way in (0, 1):
            for hop in range(self.ways - 1):
                last = self.gets(way, hop)
                if hop + 1 < self.ways - 1:
                    last = jnp.logical_and(last, jnp.logical_not(self.sends(way, hop + 1)))

                @pl.when(last)
                def _():
                    self.copy(way, hop, self.order(way, index), self.at - (hop + 1) * (1 - 2 * way)).wait_recv()

    def drain(self):
        self.settle(range(self.ways), range(self.ways))


class LineSum:
    def __init__(self, mine, inbox, send_sem, recv_sem, at, ways, subs):
        self.mine, self.inbox, self.send_sem, self.recv_sem = mine, inbox, send_sem, recv_sem
        self.at, self.ways, self.subs = at, ways, subs
        self.pending = {}

    def dest(self, way, k):
        return self.ways - 1 - k if way == 0 else k

    def sends(self, way, k):
        return self.dest(way, k) > self.at if way == 0 else self.dest(way, k) < self.at

    def gets(self, way, k):
        dest = self.dest(way, k)
        if way == 0:
            return jnp.logical_and(dest >= self.at, self.at > 0)
        return jnp.logical_and(dest <= self.at, self.at < self.ways - 1)

    def copy(self, way, k, sub):
        step = 1 - 2 * way
        return pltpu.make_async_remote_copy(
            src_ref=self.mine(self.dest(way, k), sub), dst_ref=self.inbox(way, k, sub),
            send_sem=self.send_sem.at[way, k, sub], recv_sem=self.recv_sem.at[way, k, sub],
            device_id={"chan": (self.at + step + self.ways) % self.ways}, device_id_type=MESH,
        )

    def first(self, k, sub, noted=True):
        for way in (0, 1):
            def starts(way=way):
                return jnp.logical_and(self.sends(way, k), jnp.logical_not(self.gets(way, k)))

            @pl.when(starts())
            def _():
                self.copy(way, k, sub[way]).start()
            if noted:
                self.note(way, k, sub[way], starts)

    def note_first(self, k, sub):
        for way in (0, 1):
            self.note(way, k, sub[way], lambda way=way: jnp.logical_and(
                self.sends(way, k), jnp.logical_not(self.gets(way, k))))

    def note(self, way, k, sub, going):
        def left(also):
            @pl.when(both(going(), also))
            def _():
                self.copy(way, k, sub).wait_send()
        self.pending.setdefault(k, []).append(left)

    def settle(self, k, wanted=True):
        before = self.pending.pop(k, [])
        for left in before:
            left(wanted)
        if wanted is not True:
            self.pending[k] = [
                lambda also, left=left: left(both(jnp.logical_not(wanted), also)) for left in before]

    def onward(self, way, k, sub, wanted):
        def going():
            return both(jnp.logical_and(self.sends(way, k), self.gets(way, k)), wanted())

        self.note(way, k, sub, going)

        @pl.when(going())
        def _():
            self.copy(way, k, sub).wait_recv()
            mine, inbox = self.mine(self.dest(way, k), sub), self.inbox(way, k, sub)
            mine[...] = (mine[...].astype(f32) + inbox[...].astype(f32)).astype(bf16)
            self.copy(way, k, sub).start()

    def near(self, k, sub):
        for way in (0, 1):
            self.onward(way, k, sub[way], lambda way=way: (2 * self.at) // self.ways == way)

    def far(self, k, sub):
        for way in (0, 1):
            self.onward(way, k, sub[way], lambda way=way: (2 * self.at) // self.ways != way)

    def take(self, way, sub, total):
        k = self.ways - 1 - self.at if way == 0 else self.at

        @pl.when(self.at > 0 if way == 0 else self.at < self.ways - 1)
        def _():
            self.copy(way, k, sub).wait_recv()
            total[...] += self.inbox(way, k, sub)[...].astype(f32)

    def drain(self):
        for k in list(self.pending):
            self.settle(k)


class RowSum:
    tile = 48

    def __init__(self, buf, result, box, extra_box, send_sem, recv_sem, r, total_bits):
        self.buf, self.result, self.box, self.extra_box = buf, result, box, extra_box
        self.send_sem, self.recv_sem = send_sem, recv_sem
        self.total_bits, self.r = total_bits, r
        height = buf.shape[0]
        core = r % 2
        steps = [1, 2 + 2 * core, 4 - 2 * core]
        self.levels = []
        base, size = 0, height
        inbox_at = 0
        for step in steps:
            size = size // 2
            bit = (r // step) % 2
            keep, give = base + bit * size, base + (1 - bit) * size
            self.levels.append((r + step * (1 - 2 * bit), keep, give, size, inbox_at))
            base = keep
            inbox_at += size

    def rows(self, at, size, buf=None):
        return (self.buf if buf is None else buf).at[pl.ds(pl.multiple_of(at, 16), size)]

    def halve(self, level):
        partner, keep, give, size, inbox_at = self.levels[level]
        return pltpu.make_async_remote_copy(
            src_ref=self.rows(give, size), dst_ref=self.box.at[pl.ds(inbox_at, size)],
            send_sem=self.send_sem.at[level], recv_sem=self.recv_sem.at[level],
            device_id={"dp": partner}, device_id_type=MESH,
        )

    def double(self, level, arriving=False):
        partner, keep, give, size, inbox_at = self.levels[level]
        part = self.rows(give if arriving else keep, size, self.result)
        return pltpu.make_async_remote_copy(
            src_ref=part, dst_ref=part, send_sem=self.send_sem.at[3 + level], recv_sem=self.recv_sem.at[3 + level],
            device_id={"dp": partner}, device_id_type=MESH,
        )

    def add(self, level, target=None):
        partner, keep, give, size, inbox_at = self.levels[level]
        target = self.buf if target is None else target
        self.halve(level).wait_recv()

        def run(i, carry):
            at = pl.ds(pl.multiple_of(keep + i * self.tile, 16), self.tile)
            there = pl.ds(pl.multiple_of(inbox_at + i * self.tile, 16), self.tile)
            target[at, :] = (self.buf[at, :].astype(f32) + self.box[there, :].astype(f32)).astype(bf16)
            return carry

        lax.fori_loop(0, size // self.tile, run, 0)

    def extra(self):
        partner, keep, give, size, inbox_at = self.levels[2]
        for bit in range(3, self.total_bits):
            copy = pltpu.make_async_remote_copy(
                src_ref=self.rows(keep, size, self.result), dst_ref=self.extra_box.at[bit - 3], send_sem=self.send_sem.at[3 + bit],
                recv_sem=self.recv_sem.at[3 + bit], device_id={"dp": flipped(self.r, bit)}, device_id_type=MESH,
            )
            copy.start()
            copy.wait()
            at = pl.ds(pl.multiple_of(keep, 16), size)
            self.result[at, :] = (self.result[at, :].astype(f32) + self.extra_box[bit - 3].astype(f32)).astype(bf16)

    def tasks(self):
        def second():
            self.add(0)
            self.halve(1).start()

        def third():
            self.add(1)
            self.halve(2).start()

        def turn():
            self.add(2, self.result)
            self.extra()
            self.double(2).start()

        def wider():
            self.double(2, True).wait_recv()
            self.double(1).start()

        def widest():
            self.double(1, True).wait_recv()
            self.double(0).start()

        def last():
            self.double(0, True).wait_recv()

        return [self.halve(0).start, second, third, turn, wider, widest, last]

    def drain(self):
        for level in range(3):
            self.halve(level).wait_send()
            self.double(level).wait_send()


def layer_kernel(
    cfg,
    x_hbm, g_hbm, outp_hbm, in_hbm, tab_hbm, wg_hbm, wu_hbm, wd_hbm, halves_ref, gain1_ref, gain2_ref, short_ref, cond_ref,
    rate_ref, fin_ref, fbias_ref, fout_ref, feat_ref,
    out_hbm, igrad_hbm, big_hbm, proj_hbm, small_hbm, zsum_hbm, *scratch,
):
    ways, seq, own, width, hidden, bits, all_bits = cfg
    (
        xf, gf, outt, proj, mixf, query, kv, squash, kern, mixed, hat, arg, in_t, tab, n1o, masks, cols, prow, frow,
        pieces, gains, gaincol, stat1, sig, prod, weights, n2o, mid, gg, ug, tbuf, tin, mbuf, ein,
        gb, rb, rbx, rb2, rbx2, n2own, inv2, rres, resown, pgb, mgb, mgf, pgo, sgr, kgr, sm, smbox, zbox, mom, gsum,
        load_sem, line_send, line_recv, piece_send, piece_recv, gain_send, gain_recv, save_sem,
        fs_send, fs_recv, es_send, es_recv, hs_send, hs_recv, sw_send, sw_recv,
        ar_send, ar_recv, sm_send, sm_recv, z_send, z_recv, mom_send, mom_recv,
    ) = scratch
    lags = 3 * seq // 4
    freq = lags
    block = seq // ways
    z = lax.axis_index("chan")
    r = lax.axis_index("dp")
    side = (2 * z) // ways
    inner = ((z + ways - 1) // ways) * ((2 * ways - 2 - z) // ways)
    group = r % (1 << bits)

    wd, wg, wu = (weights.at[pl.ds(at, size)] for at, size in ((0, hidden), (hidden, width), (hidden + width, width)))

    def own_rows(at):
        return pl.ds(pl.multiple_of(at * own, row_tile), own)

    def token(at):
        return pl.ds(pl.multiple_of(at * block, block), block)

    span = own_rows(z)
    saves = []

    def load(index, src, dst):
        copy = pltpu.make_async_copy(src, dst, load_sem.at[index])
        copy.start()
        return copy

    def save(src, dst):
        copy = pltpu.make_async_copy(src, dst, save_sem.at[len(saves)])
        copy.start()
        saves.append(copy)

    grain = 48
    per_piece = pieces.shape[2] // grain
    x_load = load(0, x_hbm, xf.at[span])
    g_load = load(1, g_hbm, gf.at[span])
    in_load = load(2, in_hbm, in_t)

    def piece_from(i):
        at = group * per_piece + i
        return outp_hbm.at[
            pl.ds(pl.multiple_of((at % (own // grain)) * grain, row_tile), grain),
            pl.ds(pl.multiple_of((at // (own // grain)) * 128, 128), 128)]

    piece_loads = [load(8 + i, piece_from(i), pieces.at[group, z, pl.ds(i * grain, grain)]) for i in range(per_piece)]
    tab_load = load(3, tab_hbm, tab)
    weight_loads = [load(4, wg_hbm, wg), load(5, wu_hbm, wu), load(6, wd_hbm, wd)]
    barrier = pltpu.get_barrier_semaphore()
    peers = [{"chan": (z + s) % ways} for s in range(1, ways)] + [{"dp": flipped(r, b)} for b in range(all_bits)]
    for peer in peers:
        pl.semaphore_signal(barrier, inc=1, device_id=peer, device_id_type=MESH)
    pl.semaphore_wait(barrier, len(peers))

    def cut(buf):
        return lambda shard, part: buf.at[own_rows(shard), token(part)]

    in_line, g_line, mix_line = (
        Line(cut(buf), line_send.at[i], line_recv.at[i], z, ways) for i, buf in enumerate((xf, gf, mixf)))

    class Direct:
        def __init__(self, view_src, view_dst, send, recv):
            self.view_src, self.view_dst, self.send, self.recv = view_src, view_dst, send, recv

        def copy(self, s, arriving):
            there = (z + s) % ways
            src = (z + ways - s) % ways
            dst = self.view_dst(src if arriving else z)
            return pltpu.make_async_remote_copy(
                src_ref=dst if arriving else self.view_src(there), dst_ref=dst, send_sem=self.send.at[s],
                recv_sem=self.recv.at[s], device_id={"chan": there}, device_id_type=MESH,
            )

        def start(self, wanted=None):
            for s in range(1, ways):
                if wanted is None:
                    self.copy(s, False).start()
                else:
                    @pl.when(wanted((z + s) % ways))
                    def _():
                        self.copy(s, False).start()

        def wait_recv(self):
            for s in range(1, ways):
                self.copy(s, True).wait_recv()

        def drain(self):
            for s in range(1, ways):
                self.copy(s, False).wait_send()

    gain_msg = Direct(lambda to: gains.at[z], lambda at: gains.at[at], gain_send, gain_recv)
    piece_msg = Direct(lambda to: pieces.at[group, z], lambda at: pieces.at[group, at], piece_send, piece_recv)

    gains[z] = jnp.zeros(gains.shape[1:], f32)
    gains[z, 0:1, 0:own] = gain1_ref[...]
    gains[z, 1:2, 0:own] = gain2_ref[...]
    gain_msg.start()
    x_load.wait()
    every, outer, middle = range(ways), inner == 0, inner == 1
    first_two, last_two = range(ways // 2), range(ways // 2, ways)
    next_hops, last_hops = range(1, 2), range(2, ways - 1)
    in_line.send_own(first_two, True)
    in_line.send_own(last_two, middle)

    def inside(at):
        return jnp.logical_and(at > 0, at < ways - 1)

    def early(there):
        return jnp.logical_or(inside(there), inner == 0)

    for copy in piece_loads:
        copy.wait()
    piece_msg.start(early)

    def clear(j, carry):
        gb[pl.ds(pl.multiple_of(j * 96, 96), 96), :] = jnp.zeros((96, width), bf16)
        return carry

    lax.fori_loop(0, gb.shape[0] // 96, clear, 0)

    line_at = lax.broadcasted_iota(jnp.int32, (1, seq), 1)
    split, valid = halves_ref[0, 0], halves_ref[0, 1]
    masks[0:1, :] = jnp.where(line_at < split, 1.0, 0.0)
    masks[1:2, :] = jnp.where(jnp.logical_and(line_at >= split, line_at < valid), 1.0, 0.0)
    masks[2:3, :] = masks[0:1, :] + masks[1:2, :]
    prow[...] = jnp.zeros(prow.shape, f32)
    for i in range(3):
        for j in range(3):
            prow[3 * i + j : 3 * i + j + 1, 0:own] = short_ref[i, j : j + 1, :]
    prow[9:12, 0:own] = cond_ref[...]
    prow[12:13, 0:own] = rate_ref[...]
    prow[64:128, 0:own] = fout_ref[...]
    cols[...] = prow[...].T[0:own, :]
    frow[...] = jnp.zeros(frow.shape, f32)
    frow[0 : fin_ref.shape[0], :] = fin_ref[...]
    frow[fin_ref.shape[0] : fin_ref.shape[0] + 1, :] = fbias_ref[...]
    g_load.wait()
    gf[span, :] = (gf[span, :].astype(f32) * masks[2:3, :]).astype(bf16)

    arg[...] = tn(frow[...], feat_ref[...], highest)
    kern[...] = nn(cols[:, 64:128], jnp.sin(arg[...]), highest)

    in_line.settle([0], first_two)
    in_line.send_own(last_two, outer)
    gain_msg.wait_recv()
    eye = lax.broadcasted_iota(jnp.int32, (own, gains.shape[2]), 0) == lax.broadcasted_iota(
        jnp.int32, (own, gains.shape[2]), 1)
    for s in range(ways):
        for which in range(2):
            row = gains[s, which : which + 1, :]
            gaincol[s * own : (s + 1) * own, which : which + 1] = jnp.sum(jnp.where(eye, row, 0.0), axis=1, keepdims=True)
    in_load.wait()

    def moments(values):
        centre = jnp.sum(values, axis=0, keepdims=True) * (1.0 / width)
        spread = jnp.sum(values * values, axis=0, keepdims=True) * (1.0 / width) - centre * centre
        return centre, lax.rsqrt(spread + norm_eps)

    def in_order(index):
        return side * index + (1 - side) * (ways - 1 - index)

    def norm1(q):
        at = token(q)
        values = xf[:, at].astype(f32)
        centre, inverse = moments(values)
        stat1[0:1, at] = centre
        stat1[1:2, at] = inverse
        low = ((values - centre) * inverse * gaincol[:, 0:1]).astype(bf16)
        n1o[:, at] = low
        proj[:, at] = nn(in_t[...], low)

    for index in first_two:
        in_line.short_way(index)
    for index in every:
        in_line.long_way(index, next_hops)
    for index in last_two:
        in_line.short_way(index)
    in_line.settle([0], last_two)
    g_line.send_own(every, outer)
    for index in first_two:
        in_line.long_way(index, last_hops)
    g_line.send_own(every, middle, inward=True)
    for index in last_two:
        in_line.long_way(index, last_hops)

    def norm_turn(index, carry):
        in_line.take(index)
        norm1(in_order(index))
        return carry

    lax.fori_loop(0, ways, norm_turn, 0)
    piece_msg.start(lambda there: jnp.logical_not(early(there)))
    for index in every:
        g_line.short_way(index)

    piece_sends = []

    def piece_step(bit, held, slot):
        batch = []
        for i, piece in enumerate(held):
            def make(which, slot=slot + i):
                return pltpu.make_async_remote_copy(
                    src_ref=pieces.at[which], dst_ref=pieces.at[which], send_sem=piece_send.at[slot],
                    recv_sem=piece_recv.at[slot], device_id={"dp": flipped(r, bit)}, device_id_type=MESH,
                )
            make(piece).start()
            batch.append((make, piece))
            piece_sends.append((make, piece))

        def finish():
            for make, piece in batch:
                make(flipped(piece, bit)).wait_recv()
        return finish, held + [flipped(piece, bit) for piece in held], slot + len(held)

    tab_load.wait()

    half1, half2 = masks[0:1, :], masks[1:2, :]

    def back(values, steps):
        if steps == 0:
            return values
        return jnp.where(lane2 >= steps, pltpu.roll(values, steps, 1), 0.0)

    def row_at(j, i):
        return pl.ds(pl.multiple_of(j * own + i * row_tile, row_tile), row_tile)

    tall = 2 * row_tile
    lane2 = lax.broadcasted_iota(jnp.int32, (tall, seq), 1)
    place2 = lane2.astype(f32)

    def mix_rows(i, carry):
        here, here1, here2 = (pl.ds(pl.multiple_of(j * own + i * tall, tall), tall) for j in range(3))
        tap = cols[here, :]
        outs = []
        for j in range(3):
            part = proj[(here, here1, here2)[j], :]
            outs.append(sum(tap[:, 3 * k + j : 3 * k + j + 1] * back(part, k) for k in range(3)))
        query[here, :] = outs[0]
        kv[here, :] = outs[1]
        kv[here1, :] = outs[2]
        cond = sum(tap[:, 9 + k : 10 + k] * back(outs[2], k) for k in range(3))
        bent = jnp.tanh(cond)
        squash[here, :] = bent
        filt = (kern[here, :] + bent) * (jnp.exp(-tap[:, 12:13] * place2) * (1.0 / math.sqrt(seq)))
        kern[here, :] = filt
        source = outs[1] * outs[2]
        sig[here, :] = jnp.where(lane2 < lags, filt, 0.0).astype(bf16)
        sig[here1, :] = (source * half1).astype(bf16)
        sig[here2, :] = (source * half2).astype(bf16)
        return carry

    lax.fori_loop(0, own // tall, mix_rows, 0)
    g_line.send_own(first_two, middle, inward=False)
    piece_msg.wait_recv()
    bit_list = list(reversed(range(bits)))
    finish, held, slot = piece_step(bit_list[0], [group], ways)

    def freq_at(j):
        return (pl.ds(pl.multiple_of(j * lane_tile, lane_tile), lane_tile),
                pl.ds(pl.multiple_of(freq + j * lane_tile, lane_tile), lane_tile))

    def freq_tile(j, carry):
        re_at, im_at = freq_at(j)
        re = nn(sig[...], tab[:, re_at])
        im = nn(sig[...], tab[:, im_at])
        hat[:, re_at] = re.astype(bf16)
        hat[:, im_at] = im.astype(bf16)
        kr, ki = re[:own], im[:own]
        for h in range(2):
            sr, si = re[own * (h + 1) : own * (h + 2)], im[own * (h + 1) : own * (h + 2)]
            prod[own * h : own * (h + 1), re_at] = (kr * sr - ki * si).astype(bf16)
            prod[own * h : own * (h + 1), im_at] = (kr * si + ki * sr).astype(bf16)
        return carry

    lax.fori_loop(0, freq // lane_tile, freq_tile, 0)

    def time_tile(j, carry):
        at = token(j)
        both = nt(prod[0 : 2 * own, :], tab[at, :])
        total = (both[:own] * masks[0:1, at] + both[own:] * masks[1:2, at]) * (1.0 / freq)
        mixed[:, at] = total
        mixf[span, at] = (query[:, at] * total).astype(bf16)
        return carry

    def time_turn(index, carry):
        time_tile(side * (ways - 1 - index) + (1 - side) * index, 0)
        for early_index in first_two:
            @pl.when(index == early_index)
            def _():
                mix_line.send_own([early_index], True, inward=True)
        return carry

    lax.fori_loop(0, ways, time_turn, 0)
    mix_line.send_own(first_two, middle, inward=False)
    finish()
    finish, held, slot = piece_step(bit_list[1], held, slot)
    for index in first_two:
        g_line.long_way(index)
    mix_line.settle([0], first_two, outer)
    mix_line.send_own(last_two, outer)
    finish()
    finish, held, slot = piece_step(bit_list[2], held, slot)
    finish()
    for s in range(ways):
        for block_at in range(own * width // 128 // grain):
            piece, inside_at = divmod(block_at, per_piece)
            column, down = divmod(block_at, own // grain)
            outt[s * own + down * grain : s * own + (down + 1) * grain, 128 * column : 128 * column + 128] = pieces[
                piece, s, inside_at * grain : (inside_at + 1) * grain, :]
    for copy in weight_loads:
        copy.wait()

    def pass_set(index):
        for line in (g_line, mix_line):
            line.send_own([index], middle, inward=False)
            line.long_way(index)

    mix_line.long_way(0, next_hops)
    for index in first_two:
        mix_line.short_way(index)
    mix_line.long_way(0, last_hops)
    mix_line.send_own(last_two, middle, inward=True)
    for index in last_two:
        mix_line.short_way(index)

    half_block = block // 2

    def half_token(at, sub):
        return pl.ds(pl.multiple_of(at * block + sub * half_block, half_block), half_block)

    f_sum = LineSum(
        lambda dest, sub: tbuf.at[:, half_token(dest, sub)],
        lambda way, k, sub: tin.at[way, k, :, pl.ds(sub * half_block, half_block)],
        fs_send, fs_recv, z, ways, 2)
    e_sum = LineSum(
        lambda dest, sub: mbuf.at[own_rows(dest), token(sub)],
        lambda way, k, sub: ein.at[way, k, :, token(sub)],
        es_send, es_recv, z, ways, ways)

    def by_end(index):
        return (ways - 1 - index, index)

    halves_of = [(sub, sub) for sub in range(2)]
    plain_order = [(sub, sub) for sub in range(ways)]

    def tiles(count, fn):
        def run(j, carry):
            fn(pl.ds(pl.multiple_of(j * lane_tile, lane_tile), lane_tile))
            return carry
        lax.fori_loop(0, count // lane_tile, run, 0)

    def forward(q):
        at = token(q)
        def resid_tile(ds):
            rres[ds, :] = xf[ds, at].astype(f32) + nn(outt[ds, :], mixf[:, at])

        tiles(width, resid_tile)
        resown[:, at] = rres[span, :]
        centre, inverse = moments(rres[...])
        n2o[:, at] = ((rres[...] - centre) * inverse * gaincol[:, 1:2]).astype(bf16)

        @pl.when(q == z)
        def _():
            n2own[...] = (rres[...] - centre) * inverse
            inv2[0:1, :] = inverse

        def hidden_tile(fs):
            low = n2o[:, at]
            gate = tn(wg[:, fs], low)
            up = tn(wu[:, fs], low)
            bent = jax.nn.sigmoid(gate)
            act = gate * bent
            mid[fs, at] = (act * up).astype(bf16)
            gg[fs, at] = (up * bent * (1.0 + gate * (1.0 - bent))).astype(bf16)
            ug[fs, at] = act.astype(bf16)

        tiles(hidden, hidden_tile)

        def mlp_tile(ds):
            mbuf[ds, at] = tn(wd[:, ds], mid[:, at]).astype(bf16)

        tiles(width, mlp_tile)

    def backward(q):
        at = token(q)

        def back_tile(fs):
            grad = nn(wd[fs, :], gf[:, at])
            gg[fs, at] = (grad * gg[fs, at].astype(f32)).astype(bf16)
            ug[fs, at] = (grad * ug[fs, at].astype(f32)).astype(bf16)

        tiles(hidden, back_tile)

        def term_tile(ds):
            tbuf[ds, at] = (nn(wg[ds, :], gg[:, at]) + nn(wu[ds, :], ug[:, at])).astype(bf16)

        tiles(width, term_tile)

    def turn_tokens(index):
        late = index // (ways - 2)
        return in_order(index + inner * late * (1 - 2 * (index - (ways - 2))))

    def weight_grads(turn, carry):
        at = token(turn_tokens(turn))
        for lhs, rhs, place_at in ((mid, gf, 0), (n2o, gg, hidden), (n2o, ug, hidden + width)):
            def run(j, carry):
                rows_at = pl.ds(pl.multiple_of(j * lane_tile, lane_tile), lane_tile)
                to = pl.ds(pl.multiple_of(place_at + j * lane_tile, lane_tile), lane_tile)
                gb[to, :] = (nt(lhs[rows_at, at], rhs[:, at]) + gb[to, :].astype(f32)).astype(bf16)
                return carry
            lax.fori_loop(0, lhs.shape[0] // lane_tile, run, 0)
        return carry

    big_rows = hidden + 2 * width

    def feed_forward_turn(index, carry):
        def at_turn(which):
            return pl.when(index == which)

        q = turn_tokens(index)
        mix_line.take(index)

        @at_turn(ways - 1)
        def _():
            for early_index in first_two:
                for k in range(ways - 2):
                    e_sum.first(k, by_end(early_index))

        forward(q)
        for which in every:
            @at_turn(which)
            def _():
                if which == 0:
                    mix_line.long_way(1)
                elif which + 1 < ways:
                    for line in (g_line, mix_line):
                        line.settle(range(ways - 1), range(which + 1))
                    pass_set(which + 1)
                if which == ways - 3:
                    g_line.arrive(ways - 1)
                    mix_line.arrive(ways - 1)
                if which == ways - 2:
                    for sub in halves_of:
                        f_sum.near(0, sub)
        g_line.take(index)
        backward(q)
        for which in every:
            @at_turn(which)
            def _():
                if which < ways - 1:
                    for sub in halves_of:
                        f_sum.first(which, sub)
                if which == ways - 1:
                    for sub in halves_of:
                        f_sum.near(1, sub)
                    for sub in halves_of:
                        f_sum.far(0, sub)
        seen = (index + ways - 1) // ways
        behind = seen * (1 - (index + ways - 2) // ways)
        lax.fori_loop(index - behind * index, seen * (index + 1), weight_grads, 0)
        return carry

    lax.fori_loop(0, ways, feed_forward_turn, 0)

    first_rows = big_rows // 2
    big_parts = []
    for i, at in enumerate((0, first_rows)):
        def cut_rows(buf, at=at, size=first_rows):
            return buf.at[pl.ds(at, size)]
        big = RowSum(
            cut_rows(gb), cut_rows(weights), cut_rows(rb, at * 7 // 8, first_rows * 7 // 8),
            rbx.at[:, pl.ds(i * (rbx.shape[1] // 2), rbx.shape[1] // 2)], ar_send.at[i], ar_recv.at[i], r, all_bits)
        big.halve(0).start()
        big_parts.append(big)
    big_left = [[big.tasks()[1:] for big in big_parts] for _ in range(2)]

    def big_step(inside_line):
        steps = [left.pop(0) for left in big_left[inside_line]]

        @pl.when(inner == inside_line)
        def _():
            for step in steps:
                step()

    rres[...] = tbuf[:, token(z)].astype(f32)
    for sub in range(2):
        for way in (0, 1):
            f_sum.take(way, sub, rres.at[:, pl.ds(sub * half_block, half_block)])
    upstream = rres[...] * gaincol[:, 1:2]
    normed = n2own[...]
    plain = jnp.sum(upstream, axis=0, keepdims=True) * (1.0 / width)
    cross = jnp.sum(upstream * normed, axis=0, keepdims=True) * (1.0 / width)
    pgb[...] = (gf[:, token(z)].astype(f32) + inv2[0:1, :] * (upstream - plain - normed * cross)).astype(bf16)
    def mix_grad_tile(ds):
        mgb[ds, :] = tn(outt[:, ds], pgb[...]).astype(bf16)

    tiles(width, mix_grad_tile)
    swap_mix = Direct(lambda to: mgb.at[own_rows(to)], lambda at: mgf.at[:, token(at)], sw_send.at[0], sw_recv.at[0])
    swap_proj = Direct(lambda to: pgb.at[own_rows(to)], lambda at: pgo.at[:, token(at)], sw_send.at[1], sw_recv.at[1])
    swap_mix.start()
    mgf[:, token(z)] = mgb[span, :]
    pgo[:, token(z)] = pgb[span, :]
    ones = jnp.ones((8, block), bf16)
    gsum[ways] = nt(ones, (rres[...] * normed).astype(bf16))

    big_step(0)
    big_step(1)
    swap_mix.wait_recv()
    swap_proj.start()
    for k in range(ways - 2):
        e_sum.first(k, by_end(2))
    for index in first_two:
        for k in range(ways - 2):
            e_sum.near(k, by_end(index))

    def grad_rows(i, carry):
        here = row_at(0, i)
        down = mgf[here, :].astype(f32) * query[here, :]
        sig[row_at(0, i), :] = (down * half1).astype(bf16)
        sig[row_at(1, i), :] = (down * half2).astype(bf16)
        return carry

    lax.fori_loop(0, own // row_tile, grad_rows, 0)

    def grad_freq(j, carry):
        re_at, im_at = freq_at(j)
        re = nn(sig[0 : 2 * own, :], tab[:, re_at])
        im = nn(sig[0 : 2 * own, :], tab[:, im_at])
        hr, hi = hat[:, re_at].astype(f32), hat[:, im_at].astype(f32)
        kr, ki = hr[:own], hi[:own]
        kg_re, kg_im = 0.0, 0.0
        for h in range(2):
            mr, mi = re[own * h : own * (h + 1)], im[own * h : own * (h + 1)]
            sr, si = hr[own * (h + 1) : own * (h + 2)], hi[own * (h + 1) : own * (h + 2)]
            prod[own * h : own * (h + 1), re_at] = (kr * mr + ki * mi).astype(bf16)
            prod[own * h : own * (h + 1), im_at] = (kr * mi - ki * mr).astype(bf16)
            kg_re = kg_re + sr * mr + si * mi
            kg_im = kg_im + sr * mi - si * mr
        prod[2 * own : 3 * own, re_at] = kg_re.astype(bf16)
        prod[2 * own : 3 * own, im_at] = kg_im.astype(bf16)
        return carry

    lax.fori_loop(0, freq // lane_tile, grad_freq, 0)
    big_step(1)

    def grad_time(j, carry):
        at = token(j)
        all3 = nt(prod[...], tab[at, :])
        sgr[:, at] = (all3[:own] * masks[0:1, at] + all3[own : 2 * own] * masks[1:2, at]) * (1.0 / freq)
        kgr[:, at] = all3[2 * own :] * (1.0 / freq)
        return carry

    lax.fori_loop(0, ways, grad_time, 0)

    def sum_slot(index, at, size):
        if index < seq // 128:
            return query.at[pl.ds(at, size), 128 * index : 128 * index + 128]
        index = index - seq // 128
        return n2own.at[pl.ds(own * (index % ways) + at, size), 128 * (index // ways) : 128 * (index // ways) + 128]

    def ahead2(values, steps):
        if steps == 0:
            return values
        return jnp.where(lane2 < seq - steps, pltpu.roll(values, seq - steps, 1), 0.0)

    def chain_rows(i, carry):
        at = pl.multiple_of(i * tall, tall)
        here, here1, here2 = (pl.ds(pl.multiple_of(j * own + i * tall, tall), tall) for j in range(3))
        tap = cols[here, :]

        def note(index, values):
            sum_slot(index, at, tall)[...] = sum(values[:, 128 * b : 128 * b + 128] for b in range(seq // 128))

        key, value = kv[here, :], kv[here1, :]
        kgrad = jnp.where(lane2 < lags, kgr[here, :], 0.0)
        base_grad = kgrad * (jnp.exp(-tap[:, 12:13] * place2) * (1.0 / math.sqrt(seq)))
        kgr[here, :] = base_grad
        note(12, -kgrad * kern[here, :] * place2)
        bent = squash[here, :]
        cond_grad = base_grad * (1.0 - bent * bent)
        sgrad = sgr[here, :]
        value_grad = sgrad * key
        for k in range(3):
            moved = ahead2(cond_grad, k)
            note(9 + k, moved * value)
            value_grad = value_grad + tap[:, 9 + k : 10 + k] * moved
        branch = (mgf[here, :].astype(f32) * mixed[here, :], sgrad * value, value_grad)
        for j, rows_at in enumerate((here, here1, here2)):
            part = proj[rows_at, :]
            total = 0.0
            for k in range(3):
                moved = ahead2(branch[j], k)
                note(3 * k + j, moved * part)
                total = total + tap[:, 3 * k + j : 3 * k + j + 1] * moved
            sig[rows_at, :] = total.astype(bf16)
        return carry

    lax.fori_loop(0, own // tall, chain_rows, 0)
    big_step(0)
    big_step(1)

    def finish_sums():
        ones_square = jnp.ones((128, 128), f32)

        def run(i, carry):
            at = pl.multiple_of(i * 64, 64)
            column = lax.broadcasted_iota(jnp.int32, (64, 128), 1)
            stat = jnp.zeros((64, 128), f32)
            for index in range(13):
                stat = jnp.where(column == index, nn(sum_slot(index, at, 64)[...], ones_square, highest), stat)
            sm[pl.ds(at, 64), :] = stat
            return carry

        lax.fori_loop(0, own // 64, run, 0)


    h_sum = LineSum(
        lambda dest, sub: tbuf.at[own_rows(dest), token(sub)],
        lambda way, k, sub: tin.at[way, k, own_rows(sub), :],
        hs_send, hs_recv, z, ways, ways)
    f_sum.drain()
    mom_msg = Direct(lambda to: mom.at[z], lambda at: mom.at[at], mom_send, mom_recv)

    def in_back(tile):
        at = token(tile)
        rres[...] = tn(in_t[...], sig[:, at])
        tbuf[:, at] = rres[...].astype(bf16)
        h_sum.first(0, (tile, tile), False)
        normed = (xf[:, at].astype(f32) - stat1[0:1, at]) * stat1[1:2, at]
        upstream = rres[...] * gaincol[:, 0:1]
        mom[z, 0:1, at] = jnp.sum(upstream, axis=0, keepdims=True)
        mom[z, 1:2, at] = jnp.sum(upstream * normed, axis=0, keepdims=True)
        gsum[tile] = nt(ones, (rres[...] * normed).astype(bf16))

    gb2 = gg.at[0 : 4 * own, 0:width]
    sum2 = mid.at[0 : 4 * own, 0:width]

    def proj_grad(lhs, rhs, place_at):
        def run(j, carry):
            gb2[pl.ds(pl.multiple_of(place_at + j * own, row_tile), own), :] = nt(
                lhs[pl.ds(pl.multiple_of(j * own, row_tile), own), :], rhs[...]).astype(bf16)
            return carry

        lax.fori_loop(0, lhs.shape[0] // own, run, 0)

    two = RowSum(gb2, sum2, rb2, rbx2, ar_send.at[2], ar_recv.at[2], r, all_bits)
    two_tasks = two.tasks()

    def small_copy(b):
        return pltpu.make_async_remote_copy(
            src_ref=sm, dst_ref=smbox.at[b], send_sem=sm_send.at[b], recv_sem=sm_recv.at[b],
            device_id={"dp": flipped(r, b)}, device_id_type=MESH,
        )

    def small_step(b):
        small_copy(b).wait()
        sm[...] += smbox[b]
        if b + 1 < all_bits:
            small_copy(b + 1).start()

    def near(summer, k, index):
        summer.near(k, by_end(index) if summer is e_sum else plain_order[index])

    def far(summer, k, index):
        summer.far(k, by_end(index) if summer is e_sum else plain_order[index])

    total = rres.at[0:own, :]

    def output_part(tile):
        at = token(tile)
        total[...] = mbuf[span, at].astype(f32)
        for way in (0, 1):
            e_sum.take(way, tile, total)
        resown[:, at] = (resown[:, at] + total[...]) * masks[2:3, at]

    def input_part(tile):
        at = token(tile)
        total[...] = tbuf[span, at].astype(f32)
        for way in (0, 1):
            h_sum.take(way, tile, total)
        sums = sum(mom[s, :, at] for s in range(ways)) * (1.0 / width)
        inverse = stat1[1:2, at]
        normed = (xf[span, at].astype(f32) - stat1[0:1, at]) * inverse
        upstream = total[...] * gaincol[span, 0:1]
        sgr[:, at] = pgo[:, at].astype(f32) + inverse * (upstream - sums[0:1, :] - normed * sums[1:2, :])
        save(sgr.at[:, at], igrad_hbm.at[:, at])

    def in_turn(tile, carry):
        in_back(tile)
        return carry

    lax.fori_loop(0, ways, in_turn, 0)
    for index in every:
        h_sum.note_first(0, plain_order[index])
    mom_msg.start()
    swap_proj.wait_recv()
    proj_grad(sig, n1o, 0)
    proj_grad(pgo, mixf, 3 * own)
    two_tasks.pop(0)()
    for index in every:
        h_sum.first(1, plain_order[index])
    for index in first_two:
        far(e_sum, 0, index)
    for k in range(ways - 2):
        near(e_sum, k, 2)
    big_step(0)
    big_step(1)

    wave_grad = tn(cols[:, 64:128], kgr[...], highest) * jnp.cos(arg[...])
    finish_sums()
    for index in every:
        near(h_sum, 0, index)
    sm[0:own, 64:128] = nt(kgr[...], jnp.sin(arg[...]), highest)
    sm[own : own + 64, 0:64] = nt(feat_ref[...], wave_grad, highest)
    sm[own : own + 64, 64:128] = jnp.zeros((64, 64), f32)
    sm[own + 64 :, :] = jnp.zeros((16, 128), f32)
    for b in range(width // 128):
        lanes = slice(128 * b, 128 * b + 128)
        sm[own + 64 + b : own + 65 + b, :] = sum(gsum[tile, 0:1, lanes] for tile in range(ways))
        sm[own + 72 + b : own + 73 + b, :] = gsum[ways, 0:1, lanes]
    small_copy(0).start()
    two_tasks.pop(0)()
    small_step(0)
    for k in range(ways - 2):
        e_sum.first(k, by_end(3))
    for index in every:
        far(h_sum, 0, index)
    small_step(1)
    for index in every:
        h_sum.first(2, plain_order[index])
    for index in every:
        near(h_sum, 1, index)
    two_tasks.pop(0)()
    big_step(0)
    for index in every:
        e_sum.first(ways - 2, by_end(index))
    far(e_sum, 0, 2)
    big_step(1)
    for b in range(2, all_bits):
        small_step(b)
    z_msg = Direct(lambda to: zbox.at[z], lambda at: zbox.at[at], z_send, z_recv)
    zbox[z] = sm[own:, :]
    z_msg.start()
    save(sm, small_hbm)
    two_tasks.pop(0)()
    for k in range(ways - 2):
        near(e_sum, k, 3)
    two_tasks.pop(0)()
    big_step(0)
    two_tasks.pop(0)()
    far(e_sum, 0, 3)
    big_step(1)
    big_step(0)
    save(weights, big_hbm)
    mom_msg.wait_recv()
    input_part(0)
    input_part(1)
    two_tasks.pop(0)()
    save(sum2, proj_hbm)
    input_part(2)
    z_msg.wait_recv()
    zsum = zbox[0]
    for s in range(1, ways):
        zsum = zsum + zbox[s]
    zout = kern.at[0 : zsum.shape[0], 0:128]
    zout[...] = zsum
    save(zout, zsum_hbm)
    input_part(3)
    def output_turn(tile, carry):
        output_part(tile)
        return carry

    lax.fori_loop(0, ways, output_turn, 0)
    save(resown, out_hbm)

    for line in (in_line, g_line, mix_line, e_sum, h_sum, gain_msg, piece_msg, swap_mix, swap_proj, mom_msg, z_msg, big_parts[0], big_parts[1], two):
        line.drain()
    for make, piece in piece_sends:
        make(piece).wait_send()
    for copy in saves:
        copy.wait()


def layer(cfg, x_own, g_own, out_t, in_t, table, w_gate, w_up, w_down, halves, gain1, gain2, short_taps, cond_taps, rates,
          filter_in, filter_bias, filter_out, feats):
    ways, seq, own, width, hidden, bits, all_bits = cfg
    period = 3 * seq // 2
    block = seq // ways
    big_rows = hidden + 2 * width
    assert hidden == width
    held = dict(
        xf=((width, seq), bf16), gf=((width, seq), bf16), outt=((width, width), bf16), proj=((3 * own, seq), f32),
        mixf=((width, seq), bf16), query=((own, seq), f32), kv=((2 * own, seq), f32), squash=((own, seq), f32), kern=((own, seq), f32),
        mixed=((own, seq), f32), hat=((3 * own, period), bf16), arg=((64, seq), f32), in_t=((3 * own, width), bf16),
        tab=((seq, period), bf16), n1o=((width, seq), bf16), masks=((8, seq), f32), cols=((own, 128), f32),
        prow=((128, 256), f32), frow=((64, 64), f32),
        pieces=((1 << bits, ways, own * width // 128 // (1 << bits), 128), bf16), gains=((ways, 8, 256), f32),
        gaincol=((width, 128), f32), stat1=((8, seq), f32), sig=((3 * own, seq), bf16), prod=((3 * own, period), bf16),
        weights=((big_rows, width), bf16), n2o=((width, seq), bf16),
        mid=((hidden, seq), bf16), gg=((hidden, seq), bf16), ug=((hidden, seq), bf16), tbuf=((width, seq), bf16),
        tin=((2, ways - 1, width, block), bf16), mbuf=((width, seq), bf16), ein=((2, ways - 1, own, seq), bf16),
        gb=((big_rows, width), bf16), rb=((big_rows * 7 // 8, width), bf16),
        rbx=((max(all_bits - 3, 1), big_rows // 8 if all_bits > 3 else 32, width), bf16),
        rb2=((4 * own * 7 // 8, width), bf16),
        rbx2=((max(all_bits - 3, 1), 4 * own // 8 if all_bits > 3 else 16, width), bf16),
        n2own=((width, block), f32), inv2=((8, block), f32), rres=((width, block), f32), resown=((own, seq), f32),
        pgb=((width, block), bf16), mgb=((width, block), bf16), mgf=((own, seq), bf16), pgo=((own, seq), bf16),
        sgr=((own, seq), f32), kgr=((own, seq), f32), sm=((own + 80, 128), f32),
        smbox=((all_bits, own + 80, 128), f32), zbox=((ways, 80, 128), f32),
        mom=((ways, 8, seq), f32), gsum=((ways + 1, 8, width), f32),
    )
    hops = (3, 2, ways - 1, ways)
    sems = dict(
        load_sem=(16,), line_send=hops, line_recv=hops, piece_send=(ways + (1 << bits),), piece_recv=(ways + (1 << bits),),
        gain_send=(ways,), gain_recv=(ways,), save_sem=(24,), fs_send=(2, ways, 2), fs_recv=(2, ways, 2),
        es_send=(2, ways, ways), es_recv=(2, ways, ways), hs_send=(2, ways, ways), hs_recv=(2, ways, ways),
        sw_send=(2, ways), sw_recv=(2, ways), ar_send=(3, 3 + max(all_bits, 3)), ar_recv=(3, 3 + max(all_bits, 3)),
        sm_send=(all_bits,), sm_recv=(all_bits,), z_send=(ways,), z_recv=(ways,), mom_send=(ways,), mom_recv=(ways,),
    )
    here = pl.BlockSpec(memory_space=pltpu.VMEM)
    there = pl.BlockSpec(memory_space=pl.ANY)
    outs = [
        ((own, seq), f32), ((own, seq), f32), ((big_rows, width), bf16), ((4 * own, width), bf16),
        ((own + 80, 128), f32), ((80, 128), f32),
    ]
    return pl.pallas_call(
        functools.partial(layer_kernel, cfg),
        out_shape=[jax.ShapeDtypeStruct(s, t) for s, t in outs],
        in_specs=[there] * 8 + [pl.BlockSpec(memory_space=pltpu.SMEM)] + [here] * 9,
        out_specs=[there] * len(outs),
        scratch_shapes=[pltpu.VMEM(s, t) for s, t in held.values()] + [
            pltpu.SemaphoreType.DMA(s) for s in sems.values()],
        compiler_params=pltpu.CompilerParams(collective_id=0, has_side_effects=True, vmem_limit_bytes=64 << 20),
    )(x_own, g_own, out_t, in_t, table, w_gate, w_up, w_down, halves, gain1, gain2, short_taps, cond_taps, rates,
      filter_in, filter_bias, filter_out, feats)


def widen_kernel(
    cfg, count, out_in, igrad_in, big_in, two_in, small_ref, zsum_ref,
    out_hbm, igrad_hbm, wd_hbm, wg_hbm, wu_hbm, in_hbm, outp_hbm, gain1_ref, gain2_ref, short_ref, cond_ref, rate_ref,
    fin_ref, fbias_ref, fout_ref, low, wide, through, in_sem, out_sem, copy_sem,
):
    ways, seq, own, width, hidden, bits, all_bits = cfg
    step = own
    sources = [(big_in, at) for at in range(0, hidden + 2 * width, step)] + [(two_in, at) for at in range(0, 4 * own, step)]
    targets = [
        (ref, at) for ref, size in ((wd_hbm, hidden), (wg_hbm, width), (wu_hbm, width), (in_hbm, 3 * own), (outp_hbm, own))
        for at in range(0, size, step)]
    loads = [
        pltpu.make_async_copy(src.at[pl.ds(at, step)], low.at[i], in_sem.at[i]) for i, (src, at) in enumerate(sources)]
    for copy in loads:
        copy.start()
    ins = [pltpu.make_async_copy(src, through.at[i], copy_sem.at[i]) for i, src in enumerate((out_in, igrad_in))]
    for copy in ins:
        copy.start()
    moves = []
    stats = small_ref[0:own, :].T
    for i in range(3):
        for j in range(3):
            short_ref[i, j : j + 1, :] = stats[3 * i + j : 3 * i + j + 1, :]
    cond_ref[...] = stats[9:12, :]
    rate_ref[...] = stats[12:13, :]
    fout_ref[...] = stats[64:128, :]
    fin_ref[...] = zsum_ref[0:count, 0:64]
    fbias_ref[...] = zsum_ref[count : count + 1, 0:64]
    shift = (width - own * lax.axis_index("chan")) % width
    for first, ref in ((64, gain1_ref), (72, gain2_ref)):
        row = jnp.concatenate([zsum_ref[first + b : first + b + 1, :] for b in range(width // 128)], axis=1)
        ref[...] = pltpu.roll(jnp.broadcast_to(row, (8, width)), shift, 1)[0:1, 0:own]
    for i, ref in enumerate((out_hbm, igrad_hbm)):
        ins[i].wait()
        copy = pltpu.make_async_copy(through.at[i], ref, copy_sem.at[2 + i])
        copy.start()
        moves.append(copy)
    for i, (ref, at) in enumerate(targets):
        loads[i].wait()
        wide[i] = low[i].astype(f32)
        copy = pltpu.make_async_copy(wide.at[i], ref.at[pl.ds(at, step)], out_sem.at[i])
        copy.start()
        moves.append(copy)
    for copy in moves:
        copy.wait()


def widen(cfg, count, output, input_grad, big, two, small, zsum):
    ways, seq, own, width, hidden, bits, all_bits = cfg
    here = pl.BlockSpec(memory_space=pltpu.VMEM)
    there = pl.BlockSpec(memory_space=pl.ANY)
    far = [(own, seq), (own, seq), (hidden, width), (width, hidden), (width, hidden), (3 * own, width), (own, width)]
    near = [(1, own), (1, own), (3, 3, own), (3, own), (1, own), (count, 64), (1, 64), (64, own)]
    steps = (hidden + 2 * width + 4 * own) // own
    dma = pltpu.SemaphoreType.DMA
    return pl.pallas_call(
        functools.partial(widen_kernel, cfg, count),
        out_shape=[jax.ShapeDtypeStruct(shape, f32) for shape in far + near],
        in_specs=[there] * 4 + [here] * 2,
        out_specs=[there] * len(far) + [here] * len(near),
        scratch_shapes=[
            pltpu.VMEM((steps, own, width), bf16), pltpu.VMEM((steps, own, width), f32),
            pltpu.VMEM((2, own, seq), f32), dma((steps,)), dma((steps,)), dma((4,))],
        compiler_params=pltpu.CompilerParams(vmem_limit_bytes=64 << 20),
    )(output, input_grad, big, two, small, zsum)


def local(
    hidden_in, halves, norm1_gain, in_proj, short_taps, cond_taps, filter_in, filter_bias,
    filter_out, decay_rate, out_proj, norm2_gain, w_gate, w_up, w_down, out_grad,
):
    seq, own = hidden_in.shape[1], hidden_in.shape[2]
    ways, rows = lax.axis_size("chan"), lax.axis_size("dp")
    width, hidden = own * ways, w_gate.shape[1]
    z = lax.axis_index("chan")
    all_bits = rows.bit_length() - 1
    cfg = (ways, seq, own, width, hidden, 3, all_bits)
    count = filter_in.shape[0]
    feat_np = np.concatenate([
        band_features(seq, count), np.ones((1, seq), np.float32), np.zeros((63 - count, seq), np.float32)])
    table = jnp.asarray(wave_matrix(seq).astype(np.float32)).astype(bf16)

    output, input_grad, big, two, small, zsum = layer(
        cfg, hidden_in[0].T, out_grad[0].T, out_proj.T, in_proj.transpose(1, 2, 0).reshape(3 * own, width), table,
        w_gate, w_up, w_down, halves, norm1_gain[None], norm2_gain[None], short_taps, cond_taps, decay_rate[None],
        filter_in, filter_bias[None], filter_out, jnp.asarray(feat_np))

    (output, input_grad, wd_sum, wg_sum, wu_sum, in_sum, out_sum, gain1, gain2, short, cond, rates, fin, fbias, fout) = widen(
        cfg, count, output, input_grad, big, two, small, zsum)
    return (
        output.T[None], input_grad.T[None], gain1[0], in_sum.reshape(3, own, width).transpose(2, 0, 1), short, cond, fin,
        fbias[0], fout, rates[0], out_sum.T, gain2[0], wg_sum, wu_sum, wd_sum,
    )


def solution(mesh):
    rows, cols = P("dp", None, "chan"), P(None, "chan")
    in_specs = (
        rows, P("dp", None), P("chan"), P(None, None, "chan"), P(None, None, "chan"), cols, P(), P(),
        cols, P("chan"), cols, P("chan"), cols, cols, P("chan", None), rows,
    )
    out_specs = (
        rows, rows, P("chan"), P(None, None, "chan"), P(None, None, "chan"), cols, P(), P(),
        cols, P("chan"), cols, P("chan"), cols, cols, P("chan", None),
    )
    return jax.shard_map(local, mesh=mesh, in_specs=in_specs, out_specs=out_specs, check_vma=False)
```

```python
import functools
import math

import jax
import jax.numpy as jnp
import numpy as np
from jax import lax
from jax.experimental import pallas as pl
from jax.experimental.pallas import tpu as pltpu
from jax.sharding import PartitionSpec as P

highest = lax.Precision.HIGHEST
norm_eps = 1e-05
f32 = jnp.float32
bf16 = jnp.bfloat16


def band_features(seq_len, feat_count):
    bands = (feat_count - 1) // 2
    positions = np.arange(seq_len)
    orders = np.arange(1, bands + 1)
    phases = (orders[:, None] * positions[None, :] % seq_len) * (2.0 * math.pi / seq_len)
    ramp = positions[None, :] / seq_len
    return np.concatenate([ramp, np.sin(phases), np.cos(phases)], axis=0).astype(np.float32)


def wave_matrix(seq_len):
    period = 3 * seq_len // 2
    freq = period // 2
    phase = (np.arange(seq_len)[:, None] * (2 * np.arange(freq)[None, :] + 1)) % (2 * period)
    angle = phase * (math.pi / period)
    return np.concatenate([np.cos(angle), np.sin(angle)], axis=1)


def nn(a, b, precision=None):
    return lax.dot_general(a, b, (((1,), (0,)), ((), ())), precision=precision, preferred_element_type=f32)


def nt(a, b, precision=None):
    return lax.dot_general(a, b, (((1,), (1,)), ((), ())), precision=precision, preferred_element_type=f32)


def tn(a, b, precision=None):
    return lax.dot_general(a, b, (((0,), (0,)), ((), ())), precision=precision, preferred_element_type=f32)


MESH = pl.DeviceIdType.MESH
lane_tile = 256
row_tile = 16


def flipped(index, bit):
    return index + (1 << bit) * (1 - 2 * ((index // (1 << bit)) % 2))


def both(first, second):
    if second is True:
        return first
    return second if first is True else jnp.logical_and(first, second)


class Line:
    def __init__(self, view, send_sem, recv_sem, at, ways):
        self.view, self.send_sem, self.recv_sem, self.at, self.ways = view, send_sem, recv_sem, at, ways
        self.pending, self.arrived = {}, set()

    def copy(self, way, hop, part, shard):
        ref = self.view(shard, part)
        step = 1 - 2 * way
        return pltpu.make_async_remote_copy(
            src_ref=ref, dst_ref=ref, send_sem=self.send_sem.at[way, hop, part],
            recv_sem=self.recv_sem.at[way, hop, part],
            device_id={"chan": (self.at + step + self.ways) % self.ways}, device_id_type=MESH,
        )

    def sends(self, way, hop):
        if way == 0:
            return jnp.logical_and(self.at >= hop, self.at < self.ways - 1)
        return jnp.logical_and(self.at + hop <= self.ways - 1, self.at > 0)

    def gets(self, way, hop):
        if way == 0:
            return self.at >= hop + 1
        return self.at + hop + 1 <= self.ways - 1

    def order(self, way, index):
        return index if way == 0 else self.ways - 1 - index

    def far_side(self):
        return (2 * self.at) // self.ways

    def launch(self, hop, way, index, wanted, wait_first):
        part, step = self.order(way, index), 1 - 2 * way

        @pl.when(both(self.sends(way, hop), wanted()))
        def _():
            if wait_first:
                self.copy(way, hop - 1, part, self.at - hop * step).wait_recv()
            self.copy(way, hop, part, self.at - hop * step).start()

        def left(also):
            @pl.when(both(both(self.sends(way, hop), wanted()), also))
            def _():
                self.copy(way, hop, part, self.at - hop * step).wait_send()

        self.pending.setdefault((hop, way, index), []).append(left)

    def settle(self, hops, indices, wanted=True):
        for key in [k for k in self.pending if k[0] in hops and k[2] in indices]:
            before = self.pending.pop(key)
            for left in before:
                left(wanted)
            if wanted is not True:
                self.pending[key] = [
                    lambda also, left=left: left(both(jnp.logical_not(wanted), also)) for left in before]

    def send_own(self, indices, wanted, inward=None):
        for index in indices:
            for way in (0, 1):
                def ok(way=way):
                    if inward is None:
                        return wanted
                    facing = self.far_side() == way
                    return both(wanted, facing if inward else jnp.logical_not(facing))
                self.launch(0, way, index, ok, False)

    def relay(self, way, index, wanted, hops=None, wait_first=True):
        for hop in range(1, self.ways - 1) if hops is None else hops:
            self.launch(hop, way, index, wanted, wait_first)

    def short_way(self, index):
        for way in (0, 1):
            self.relay(way, index, lambda way=way: self.far_side() == way)

    def long_way(self, index, hops=None):
        for way in (0, 1):
            self.relay(way, index, lambda way=way: self.far_side() != way, hops, index not in self.arrived)

    def arrive(self, index):
        self.arrived.add(index)
        for way in (0, 1):
            for hop in range(1, self.ways - 1):
                @pl.when(jnp.logical_and(self.sends(way, hop), self.far_side() != way))
                def _():
                    self.copy(way, hop - 1, self.order(way, index), self.at - hop * (1 - 2 * way)).wait_recv()

    def take(self, index):
        for way in (0, 1):
            for hop in range(self.ways - 1):
                last = self.gets(way, hop)
                if hop + 1 < self.ways - 1:
                    last = jnp.logical_and(last, jnp.logical_not(self.sends(way, hop + 1)))

                @pl.when(last)
                def _():
                    self.copy(way, hop, self.order(way, index), self.at - (hop + 1) * (1 - 2 * way)).wait_recv()

    def drain(self):
        self.settle(range(self.ways), range(self.ways))


class LineSum:
    def __init__(self, mine, inbox, send_sem, recv_sem, at, ways, subs):
        self.mine, self.inbox, self.send_sem, self.recv_sem = mine, inbox, send_sem, recv_sem
        self.at, self.ways, self.subs = at, ways, subs
        self.pending = {}

    def dest(self, way, k):
        return self.ways - 1 - k if way == 0 else k

    def sends(self, way, k):
        return self.dest(way, k) > self.at if way == 0 else self.dest(way, k) < self.at

    def gets(self, way, k):
        dest = self.dest(way, k)
        if way == 0:
            return jnp.logical_and(dest >= self.at, self.at > 0)
        return jnp.logical_and(dest <= self.at, self.at < self.ways - 1)

    def copy(self, way, k, sub):
        step = 1 - 2 * way
        return pltpu.make_async_remote_copy(
            src_ref=self.mine(self.dest(way, k), sub), dst_ref=self.inbox(way, k, sub),
            send_sem=self.send_sem.at[way, k, sub], recv_sem=self.recv_sem.at[way, k, sub],
            device_id={"chan": (self.at + step + self.ways) % self.ways}, device_id_type=MESH,
        )

    def first(self, k, sub, noted=True):
        for way in (0, 1):
            def starts(way=way):
                return jnp.logical_and(self.sends(way, k), jnp.logical_not(self.gets(way, k)))

            @pl.when(starts())
            def _():
                self.copy(way, k, sub[way]).start()
            if noted:
                self.note(way, k, sub[way], starts)

    def note_first(self, k, sub):
        for way in (0, 1):
            self.note(way, k, sub[way], lambda way=way: jnp.logical_and(
                self.sends(way, k), jnp.logical_not(self.gets(way, k))))

    def note(self, way, k, sub, going):
        def left(also):
            @pl.when(both(going(), also))
            def _():
                self.copy(way, k, sub).wait_send()
        self.pending.setdefault(k, []).append(left)

    def settle(self, k, wanted=True):
        before = self.pending.pop(k, [])
        for left in before:
            left(wanted)
        if wanted is not True:
            self.pending[k] = [
                lambda also, left=left: left(both(jnp.logical_not(wanted), also)) for left in before]

    def onward(self, way, k, sub, wanted):
        def going():
            return both(jnp.logical_and(self.sends(way, k), self.gets(way, k)), wanted())

        self.note(way, k, sub, going)

        @pl.when(going())
        def _():
            self.copy(way, k, sub).wait_recv()
            mine, inbox = self.mine(self.dest(way, k), sub), self.inbox(way, k, sub)
            mine[...] = (mine[...].astype(f32) + inbox[...].astype(f32)).astype(bf16)
            self.copy(way, k, sub).start()

    def near(self, k, sub):
        for way in (0, 1):
            self.onward(way, k, sub[way], lambda way=way: (2 * self.at) // self.ways == way)

    def far(self, k, sub):
        for way in (0, 1):
            self.onward(way, k, sub[way], lambda way=way: (2 * self.at) // self.ways != way)

    def take(self, way, sub, total):
        k = self.ways - 1 - self.at if way == 0 else self.at

        @pl.when(self.at > 0 if way == 0 else self.at < self.ways - 1)
        def _():
            self.copy(way, k, sub).wait_recv()
            total[...] += self.inbox(way, k, sub)[...].astype(f32)

    def drain(self):
        for k in list(self.pending):
            self.settle(k)


class RowSum:
    tile = 48

    def __init__(self, buf, result, box, extra_box, send_sem, recv_sem, r, total_bits):
        self.buf, self.result, self.box, self.extra_box = buf, result, box, extra_box
        self.send_sem, self.recv_sem = send_sem, recv_sem
        self.total_bits, self.r = total_bits, r
        height = buf.shape[0]
        core = r % 2
        steps = [1, 2 + 2 * core, 4 - 2 * core]
        self.levels = []
        base, size = 0, height
        inbox_at = 0
        for step in steps:
            size = size // 2
            bit = (r // step) % 2
            keep, give = base + bit * size, base + (1 - bit) * size
            self.levels.append((r + step * (1 - 2 * bit), keep, give, size, inbox_at))
            base = keep
            inbox_at += size

    def rows(self, at, size, buf=None):
        return (self.buf if buf is None else buf).at[pl.ds(pl.multiple_of(at, 16), size)]

    def halve(self, level):
        partner, keep, give, size, inbox_at = self.levels[level]
        return pltpu.make_async_remote_copy(
            src_ref=self.rows(give, size), dst_ref=self.box.at[pl.ds(inbox_at, size)],
            send_sem=self.send_sem.at[level], recv_sem=self.recv_sem.at[level],
            device_id={"dp": partner}, device_id_type=MESH,
        )

    def double(self, level, arriving=False):
        partner, keep, give, size, inbox_at = self.levels[level]
        part = self.rows(give if arriving else keep, size, self.result)
        return pltpu.make_async_remote_copy(
            src_ref=part, dst_ref=part, send_sem=self.send_sem.at[3 + level], recv_sem=self.recv_sem.at[3 + level],
            device_id={"dp": partner}, device_id_type=MESH,
        )

    def add(self, level, target=None):
        partner, keep, give, size, inbox_at = self.levels[level]
        target = self.buf if target is None else target
        self.halve(level).wait_recv()

        def run(i, carry):
            at = pl.ds(pl.multiple_of(keep + i * self.tile, 16), self.tile)
            there = pl.ds(pl.multiple_of(inbox_at + i * self.tile, 16), self.tile)
            target[at, :] = (self.buf[at, :].astype(f32) + self.box[there, :].astype(f32)).astype(bf16)
            return carry

        lax.fori_loop(0, size // self.tile, run, 0)

    def extra(self):
        partner, keep, give, size, inbox_at = self.levels[2]
        for bit in range(3, self.total_bits):
            copy = pltpu.make_async_remote_copy(
                src_ref=self.rows(keep, size, self.result), dst_ref=self.extra_box.at[bit - 3], send_sem=self.send_sem.at[3 + bit],
                recv_sem=self.recv_sem.at[3 + bit], device_id={"dp": flipped(self.r, bit)}, device_id_type=MESH,
            )
            copy.start()
            copy.wait()
            at = pl.ds(pl.multiple_of(keep, 16), size)
            self.result[at, :] = (self.result[at, :].astype(f32) + self.extra_box[bit - 3].astype(f32)).astype(bf16)

    def tasks(self):
        def second():
            self.add(0)
            self.halve(1).start()

        def third():
            self.add(1)
            self.halve(2).start()

        def turn():
            self.add(2, self.result)
            self.extra()
            self.double(2).start()

        def wider():
            self.double(2, True).wait_recv()
            self.double(1).start()

        def widest():
            self.double(1, True).wait_recv()
            self.double(0).start()

        def last():
            self.double(0, True).wait_recv()

        return [self.halve(0).start, second, third, turn, wider, widest, last]

    def drain(self):
        for level in range(3):
            self.halve(level).wait_send()
            self.double(level).wait_send()


def layer_kernel(
    cfg,
    x_hbm, g_hbm, outp_hbm, in_hbm, tab_hbm, wg_hbm, wu_hbm, wd_hbm, halves_ref, gain1_ref, gain2_ref, short_ref, cond_ref,
    rate_ref, fin_ref, fbias_ref, fout_ref, feat_ref,
    out_hbm, igrad_hbm, big_hbm, proj_hbm, small_hbm, *scratch,
):
    ways, seq, own, width, hidden, bits, all_bits = cfg
    (
        xf, gf, outt, proj, mixf, query, kv, squash, kern, mixed, hat, arg, in_t, tab, n1o, masks, cols, prow, frow,
        pieces, gains, gaincol, stat1, sig, prod, weights, n2o, mid, gg, ug, tbuf, tin, mbuf, ein,
        gb, rb, rbx, rb2, rbx2, n2own, inv2, rres, resown, pgb, mgb, mgf, pgo, sgr, kgr, sm, smbox, zbox, mom, gsum,
        load_sem, line_send, line_recv, piece_send, piece_recv, gain_send, gain_recv, save_sem,
        fs_send, fs_recv, es_send, es_recv, hs_send, hs_recv, sw_send, sw_recv,
        pace_sem, ar_send, ar_recv, sm_send, sm_recv, z_send, z_recv, mom_send, mom_recv,
    ) = scratch
    lags = 3 * seq // 4
    freq = lags
    block = seq // ways
    z = lax.axis_index("chan")
    r = lax.axis_index("dp")
    side = (2 * z) // ways
    inner = ((z + ways - 1) // ways) * ((2 * ways - 2 - z) // ways)
    group = r % (1 << bits)

    wd, wg, wu = (weights.at[pl.ds(at, size)] for at, size in ((0, hidden), (hidden, width), (hidden + width, width)))

    def own_rows(at):
        return pl.ds(pl.multiple_of(at * own, row_tile), own)

    def token(at):
        return pl.ds(pl.multiple_of(at * block, block), block)

    span = own_rows(z)
    saves = []

    def load(index, src, dst):
        copy = pltpu.make_async_copy(src, dst, load_sem.at[index])
        copy.start()
        return copy

    def save(src, dst):
        copy = pltpu.make_async_copy(src, dst, save_sem.at[len(saves)])
        copy.start()
        saves.append(copy)

    grain = 48
    per_piece = pieces.shape[2] // grain
    x_load = load(0, x_hbm, xf.at[span])
    g_load = load(1, g_hbm, gf.at[span])
    in_load = load(2, in_hbm, in_t)

    def piece_from(i):
        at = group * per_piece + i
        return outp_hbm.at[
            pl.ds(pl.multiple_of((at % (own // grain)) * grain, row_tile), grain),
            pl.ds(pl.multiple_of((at // (own // grain)) * 128, 128), 128)]

    piece_loads = [load(8 + i, piece_from(i), pieces.at[group, z, pl.ds(i * grain, grain)]) for i in range(per_piece)]
    tab_load = load(3, tab_hbm, tab)
    weight_loads = [load(4, wg_hbm, wg), load(5, wu_hbm, wu), load(6, wd_hbm, wd)]
    barrier = pltpu.get_barrier_semaphore()
    peers = [{"chan": (z + s) % ways} for s in range(1, ways)] + [{"dp": flipped(r, b)} for b in range(all_bits)]
    for peer in peers:
        pl.semaphore_signal(barrier, inc=1, device_id=peer, device_id_type=MESH)
    pl.semaphore_wait(barrier, len(peers))

    def cut(buf):
        return lambda shard, part: buf.at[own_rows(shard), token(part)]

    in_line, g_line, mix_line = (
        Line(cut(buf), line_send.at[i], line_recv.at[i], z, ways) for i, buf in enumerate((xf, gf, mixf)))

    class Direct:
        def __init__(self, view_src, view_dst, send, recv):
            self.view_src, self.view_dst, self.send, self.recv = view_src, view_dst, send, recv

        def copy(self, s, arriving):
            there = (z + s) % ways
            src = (z + ways - s) % ways
            dst = self.view_dst(src if arriving else z)
            return pltpu.make_async_remote_copy(
                src_ref=dst if arriving else self.view_src(there), dst_ref=dst, send_sem=self.send.at[s],
                recv_sem=self.recv.at[s], device_id={"chan": there}, device_id_type=MESH,
            )

        def start(self, wanted=None):
            for s in range(1, ways):
                if wanted is None:
                    self.copy(s, False).start()
                else:
                    @pl.when(wanted((z + s) % ways))
                    def _():
                        self.copy(s, False).start()

        def wait_recv(self):
            for s in range(1, ways):
                self.copy(s, True).wait_recv()

        def drain(self):
            for s in range(1, ways):
                self.copy(s, False).wait_send()

    gain_msg = Direct(lambda to: gains.at[z], lambda at: gains.at[at], gain_send, gain_recv)
    piece_msg = Direct(lambda to: pieces.at[group, z], lambda at: pieces.at[group, at], piece_send, piece_recv)

    gains[z] = jnp.zeros(gains.shape[1:], f32)
    gains[z, 0:1, 0:own] = gain1_ref[...]
    gains[z, 1:2, 0:own] = gain2_ref[...]
    gain_msg.start()
    x_load.wait()
    every, outer, middle = range(ways), inner == 0, inner == 1
    first_two, last_two = range(ways // 2), range(ways // 2, ways)
    next_hops, last_hops = range(1, 2), range(2, ways - 1)
    in_line.send_own(first_two, True)
    in_line.send_own(last_two, middle)

    def inside(at):
        return jnp.logical_and(at > 0, at < ways - 1)

    def early(there):
        return jnp.logical_or(inside(there), inner == 0)

    for copy in piece_loads:
        copy.wait()
    piece_msg.start(early)

    def clear(j, carry):
        gb[pl.ds(pl.multiple_of(j * 96, 96), 96), :] = jnp.zeros((96, width), bf16)
        return carry

    lax.fori_loop(0, gb.shape[0] // 96, clear, 0)

    line_at = lax.broadcasted_iota(jnp.int32, (1, seq), 1)
    split, valid = halves_ref[0, 0], halves_ref[0, 1]
    masks[0:1, :] = jnp.where(line_at < split, 1.0, 0.0)
    masks[1:2, :] = jnp.where(jnp.logical_and(line_at >= split, line_at < valid), 1.0, 0.0)
    masks[2:3, :] = masks[0:1, :] + masks[1:2, :]
    prow[...] = jnp.zeros(prow.shape, f32)
    for i in range(3):
        for j in range(3):
            prow[3 * i + j : 3 * i + j + 1, 0:own] = short_ref[i, j : j + 1, :]
    prow[9:12, 0:own] = cond_ref[...]
    prow[12:13, 0:own] = rate_ref[...]
    prow[64:128, 0:own] = fout_ref[...]
    cols[...] = prow[...].T[0:own, :]
    frow[...] = jnp.zeros(frow.shape, f32)
    frow[0 : fin_ref.shape[0], :] = fin_ref[...]
    frow[fin_ref.shape[0] : fin_ref.shape[0] + 1, :] = fbias_ref[...]
    g_load.wait()
    gf[span, :] = (gf[span, :].astype(f32) * masks[2:3, :]).astype(bf16)

    arg[...] = tn(frow[...], feat_ref[...], highest)
    kern[...] = nn(cols[:, 64:128], jnp.sin(arg[...]), highest)

    in_line.settle([0], first_two)
    in_line.send_own(last_two, outer)
    gain_msg.wait_recv()
    eye = lax.broadcasted_iota(jnp.int32, (own, gains.shape[2]), 0) == lax.broadcasted_iota(
        jnp.int32, (own, gains.shape[2]), 1)
    for s in range(ways):
        for which in range(2):
            row = gains[s, which : which + 1, :]
            gaincol[s * own : (s + 1) * own, which : which + 1] = jnp.sum(jnp.where(eye, row, 0.0), axis=1, keepdims=True)
    in_load.wait()

    def moments(values):
        centre = jnp.sum(values, axis=0, keepdims=True) * (1.0 / width)
        spread = jnp.sum(values * values, axis=0, keepdims=True) * (1.0 / width) - centre * centre
        return centre, lax.rsqrt(spread + norm_eps)

    def in_order(index):
        return side * index + (1 - side) * (ways - 1 - index)

    def norm1(q):
        at = token(q)
        values = xf[:, at].astype(f32)
        centre, inverse = moments(values)
        stat1[0:1, at] = centre
        stat1[1:2, at] = inverse
        low = ((values - centre) * inverse * gaincol[:, 0:1]).astype(bf16)
        n1o[:, at] = low
        proj[:, at] = nn(in_t[...], low)

    for index in first_two:
        in_line.short_way(index)
    for index in every:
        in_line.long_way(index, next_hops)
    for index in last_two:
        in_line.short_way(index)
    in_line.settle([0], last_two)
    g_line.send_own(every, outer)
    for index in first_two:
        in_line.long_way(index, last_hops)
    g_line.send_own(every, middle, inward=True)
    for index in last_two:
        in_line.long_way(index, last_hops)

    def norm_turn(index, carry):
        in_line.take(index)
        norm1(in_order(index))
        return carry

    lax.fori_loop(0, ways, norm_turn, 0)
    piece_msg.start(lambda there: jnp.logical_not(early(there)))
    for index in every:
        g_line.short_way(index)

    piece_sends = []

    def piece_step(bit, held, slot):
        batch = []
        for i, piece in enumerate(held):
            def make(which, slot=slot + i):
                return pltpu.make_async_remote_copy(
                    src_ref=pieces.at[which], dst_ref=pieces.at[which], send_sem=piece_send.at[slot],
                    recv_sem=piece_recv.at[slot], device_id={"dp": flipped(r, bit)}, device_id_type=MESH,
                )
            make(piece).start()
            batch.append((make, piece))
            piece_sends.append((make, piece))

        def finish():
            for make, piece in batch:
                make(flipped(piece, bit)).wait_recv()
        return finish, held + [flipped(piece, bit) for piece in held], slot + len(held)

    tab_load.wait()

    half1, half2 = masks[0:1, :], masks[1:2, :]

    def back(values, steps):
        if steps == 0:
            return values
        return jnp.where(lane2 >= steps, pltpu.roll(values, steps, 1), 0.0)

    def row_at(j, i):
        return pl.ds(pl.multiple_of(j * own + i * row_tile, row_tile), row_tile)

    tall = 2 * row_tile
    lane2 = lax.broadcasted_iota(jnp.int32, (tall, seq), 1)
    place2 = lane2.astype(f32)

    def mix_rows(i, carry):
        here, here1, here2 = (pl.ds(pl.multiple_of(j * own + i * tall, tall), tall) for j in range(3))
        tap = cols[here, :]
        outs = []
        for j in range(3):
            part = proj[(here, here1, here2)[j], :]
            outs.append(sum(tap[:, 3 * k + j : 3 * k + j + 1] * back(part, k) for k in range(3)))
        query[here, :] = outs[0]
        kv[here, :] = outs[1]
        kv[here1, :] = outs[2]
        cond = sum(tap[:, 9 + k : 10 + k] * back(outs[2], k) for k in range(3))
        bent = jnp.tanh(cond)
        squash[here, :] = bent
        filt = (kern[here, :] + bent) * (jnp.exp(-tap[:, 12:13] * place2) * (1.0 / math.sqrt(seq)))
        kern[here, :] = filt
        source = outs[1] * outs[2]
        sig[here, :] = jnp.where(lane2 < lags, filt, 0.0).astype(bf16)
        sig[here1, :] = (source * half1).astype(bf16)
        sig[here2, :] = (source * half2).astype(bf16)
        return carry

    lax.fori_loop(0, own // tall, mix_rows, 0)
    g_line.send_own(first_two, middle, inward=False)
    piece_msg.wait_recv()
    bit_list = list(reversed(range(bits)))
    finish, held, slot = piece_step(bit_list[0], [group], ways)

    def freq_at(j):
        return (pl.ds(pl.multiple_of(j * lane_tile, lane_tile), lane_tile),
                pl.ds(pl.multiple_of(freq + j * lane_tile, lane_tile), lane_tile))

    def freq_tile(j, carry):
        re_at, im_at = freq_at(j)
        re = nn(sig[...], tab[:, re_at])
        im = nn(sig[...], tab[:, im_at])
        hat[:, re_at] = re.astype(bf16)
        hat[:, im_at] = im.astype(bf16)
        kr, ki = re[:own], im[:own]
        for h in range(2):
            sr, si = re[own * (h + 1) : own * (h + 2)], im[own * (h + 1) : own * (h + 2)]
            prod[own * h : own * (h + 1), re_at] = (kr * sr - ki * si).astype(bf16)
            prod[own * h : own * (h + 1), im_at] = (kr * si + ki * sr).astype(bf16)
        return carry

    lax.fori_loop(0, freq // lane_tile, freq_tile, 0)

    def time_tile(j, carry):
        at = token(j)
        both = nt(prod[0 : 2 * own, :], tab[at, :])
        total = (both[:own] * masks[0:1, at] + both[own:] * masks[1:2, at]) * (1.0 / freq)
        mixed[:, at] = total
        mixf[span, at] = (query[:, at] * total).astype(bf16)
        return carry

    def time_turn(index, carry):
        time_tile(side * (ways - 1 - index) + (1 - side) * index, 0)
        for early_index in first_two:
            @pl.when(index == early_index)
            def _():
                mix_line.send_own([early_index], True, inward=True)
        return carry

    lax.fori_loop(0, ways, time_turn, 0)
    mix_line.send_own([0], middle, inward=False)
    finish()
    finish, held, slot = piece_step(bit_list[1], held, slot)
    for index in first_two:
        g_line.long_way(index)
    mix_line.settle([0], first_two, outer)
    mix_line.send_own(last_two, outer)
    finish()
    finish, held, slot = piece_step(bit_list[2], held, slot)
    finish()
    for s in range(ways):
        for block_at in range(own * width // 128 // grain):
            piece, inside_at = divmod(block_at, per_piece)
            column, down = divmod(block_at, own // grain)
            outt[s * own + down * grain : s * own + (down + 1) * grain, 128 * column : 128 * column + 128] = pieces[
                piece, s, inside_at * grain : (inside_at + 1) * grain, :]
    for copy in weight_loads:
        copy.wait()

    def pass_set(index):
        for line in (g_line, mix_line):
            line.send_own([index], middle, inward=False)
            line.long_way(index)

    mix_line.long_way(0, next_hops)
    for index in first_two:
        mix_line.short_way(index)
    mix_line.long_way(0, last_hops)
    mix_line.send_own(last_two, middle, inward=True)
    for index in last_two:
        mix_line.short_way(index)

    half_block = block // 2

    def half_token(at, sub):
        return pl.ds(pl.multiple_of(at * block + sub * half_block, half_block), half_block)

    f_sum = LineSum(
        lambda dest, sub: tbuf.at[:, half_token(dest, sub)],
        lambda way, k, sub: tin.at[way, k, :, pl.ds(sub * half_block, half_block)],
        fs_send, fs_recv, z, ways, 2)
    e_sum = LineSum(
        lambda dest, sub: mbuf.at[own_rows(dest), token(sub)],
        lambda way, k, sub: ein.at[way, k, :, token(sub)],
        es_send, es_recv, z, ways, ways)

    def by_end(index):
        return (ways - 1 - index, index)

    halves_of = [(sub, sub) for sub in range(2)]
    plain_order = [(sub, sub) for sub in range(ways)]

    def tiles(count, fn):
        def run(j, carry):
            fn(pl.ds(pl.multiple_of(j * lane_tile, lane_tile), lane_tile))
            return carry
        lax.fori_loop(0, count // lane_tile, run, 0)

    def forward(q):
        at = token(q)
        def resid_tile(ds):
            rres[ds, :] = xf[ds, at].astype(f32) + nn(outt[ds, :], mixf[:, at])

        tiles(width, resid_tile)
        resown[:, at] = rres[span, :]
        centre, inverse = moments(rres[...])
        n2o[:, at] = ((rres[...] - centre) * inverse * gaincol[:, 1:2]).astype(bf16)

        @pl.when(q == z)
        def _():
            n2own[...] = (rres[...] - centre) * inverse
            inv2[0:1, :] = inverse

        def hidden_tile(fs):
            low = n2o[:, at]
            gate = tn(wg[:, fs], low)
            up = tn(wu[:, fs], low)
            bent = jax.nn.sigmoid(gate)
            act = gate * bent
            mid[fs, at] = (act * up).astype(bf16)
            gg[fs, at] = (up * bent * (1.0 + gate * (1.0 - bent))).astype(bf16)
            ug[fs, at] = act.astype(bf16)

        tiles(hidden, hidden_tile)

    def down(q):
        at = token(q)

        def mlp_tile(ds):
            mbuf[ds, at] = tn(wd[:, ds], mid[:, at]).astype(bf16)

        tiles(width, mlp_tile)

    def backward(q):
        at = token(q)

        def back_tile(fs):
            grad = nn(wd[fs, :], gf[:, at])
            gg[fs, at] = (grad * gg[fs, at].astype(f32)).astype(bf16)
            ug[fs, at] = (grad * ug[fs, at].astype(f32)).astype(bf16)

        tiles(hidden, back_tile)

        def term_tile(ds):
            tbuf[ds, at] = (nn(wg[ds, :], gg[:, at]) + nn(wu[ds, :], ug[:, at])).astype(bf16)

        tiles(width, term_tile)

    def turn_tokens(index):
        late = index // (ways - 2)
        return in_order(index + inner * late * (1 - 2 * (index - (ways - 2))))

    def weight_grads(turn, carry):
        at = token(turn_tokens(turn))
        for lhs, rhs, place_at in ((mid, gf, 0), (n2o, gg, hidden), (n2o, ug, hidden + width)):
            def run(j, carry):
                rows_at = pl.ds(pl.multiple_of(j * lane_tile, lane_tile), lane_tile)
                to = pl.ds(pl.multiple_of(place_at + j * lane_tile, lane_tile), lane_tile)
                gb[to, :] = (nt(lhs[rows_at, at], rhs[:, at]) + gb[to, :].astype(f32)).astype(bf16)
                return carry
            lax.fori_loop(0, lhs.shape[0] // lane_tile, run, 0)
        return carry

    big_rows = hidden + 2 * width

    def feed_forward_turn(index, carry):
        def at_turn(which):
            return pl.when(index == which)

        q = turn_tokens(index)
        mix_line.take(index)

        @at_turn(ways - 1)
        def _():
            for early_index in first_two:
                for k in range(ways - 2):
                    e_sum.first(k, by_end(early_index))

        forward(q)
        for which in every:
            @at_turn(which)
            def _():
                if which == 0:
                    mix_line.send_own([1], middle, inward=False)
                    mix_line.long_way(1)
                elif which + 1 < ways:
                    for line in (g_line, mix_line):
                        line.settle(range(ways - 1), range(which + 1))

                    @pl.when(jnp.logical_and(middle, r % 2 == 0))
                    def _():
                        pl.semaphore_signal(pace_sem, inc=1, device_id={"dp": flipped(r, 0)}, device_id_type=MESH)

                    @pl.when(jnp.logical_and(middle, r % 2 == 1))
                    def _():
                        pl.semaphore_wait(pace_sem, 1)

                    pass_set(which + 1)
                if which == ways - 3:
                    g_line.arrive(ways - 1)
                    mix_line.arrive(ways - 1)
                if which == ways - 2:
                    for sub in halves_of:
                        f_sum.near(0, sub)
        g_line.take(index)
        backward(q)
        for which in every:
            @at_turn(which)
            def _():
                if which < ways - 1:
                    for sub in halves_of:
                        f_sum.first(which, sub)
                if which == ways - 1:
                    for sub in halves_of:
                        f_sum.near(1, sub)
                    for sub in halves_of:
                        f_sum.far(0, sub)
        pl.when(index < ways - 1)(lambda: down(q))
        seen = (index + ways - 1) // ways
        behind = seen * (1 - (index + ways - 2) // ways)
        lax.fori_loop(index - behind * index, seen * (index + 1), weight_grads, 0)
        return carry

    lax.fori_loop(0, ways, feed_forward_turn, 0)

    first_rows = big_rows // 2
    big_parts = []
    for i, at in enumerate((0, first_rows)):
        def cut_rows(buf, at=at, size=first_rows):
            return buf.at[pl.ds(at, size)]
        big = RowSum(
            cut_rows(gb), cut_rows(weights), cut_rows(rb, at * 7 // 8, first_rows * 7 // 8),
            rbx.at[:, pl.ds(i * (rbx.shape[1] // 2), rbx.shape[1] // 2)], ar_send.at[i], ar_recv.at[i], r, all_bits)
        big.halve(0).start()
        big_parts.append(big)
    big_left = [[big.tasks()[1:] for big in big_parts] for _ in range(2)]

    def big_step(inside_line):
        steps = [left.pop(0) for left in big_left[inside_line]]

        @pl.when(inner == inside_line)
        def _():
            for step in steps:
                step()

    rres[...] = tbuf[:, token(z)].astype(f32)
    for sub in range(2):
        for way in (0, 1):
            f_sum.take(way, sub, rres.at[:, pl.ds(sub * half_block, half_block)])
    upstream = rres[...] * gaincol[:, 1:2]
    normed = n2own[...]
    plain = jnp.sum(upstream, axis=0, keepdims=True) * (1.0 / width)
    cross = jnp.sum(upstream * normed, axis=0, keepdims=True) * (1.0 / width)
    pgb[...] = (gf[:, token(z)].astype(f32) + inv2[0:1, :] * (upstream - plain - normed * cross)).astype(bf16)
    def mix_grad_tile(ds):
        mgb[ds, :] = tn(outt[:, ds], pgb[...]).astype(bf16)

    tiles(width, mix_grad_tile)
    swap_mix = Direct(lambda to: mgb.at[own_rows(to)], lambda at: mgf.at[:, token(at)], sw_send.at[0], sw_recv.at[0])
    swap_proj = Direct(lambda to: pgb.at[own_rows(to)], lambda at: pgo.at[:, token(at)], sw_send.at[1], sw_recv.at[1])
    swap_mix.start()
    down(turn_tokens(ways - 1))
    mgf[:, token(z)] = mgb[span, :]
    pgo[:, token(z)] = pgb[span, :]
    ones = jnp.ones((8, block), bf16)
    gsum[ways] = nt(ones, (rres[...] * normed).astype(bf16))

    big_step(0)
    big_step(1)
    swap_mix.wait_recv()
    swap_proj.start()
    for k in range(ways - 2):
        e_sum.first(k, by_end(2))
    for index in first_two:
        for k in range(ways - 2):
            e_sum.near(k, by_end(index))

    def grad_rows(i, carry):
        here = row_at(0, i)
        down = mgf[here, :].astype(f32) * query[here, :]
        sig[row_at(0, i), :] = (down * half1).astype(bf16)
        sig[row_at(1, i), :] = (down * half2).astype(bf16)
        return carry

    lax.fori_loop(0, own // row_tile, grad_rows, 0)

    def grad_freq(j, carry):
        re_at, im_at = freq_at(j)
        re = nn(sig[0 : 2 * own, :], tab[:, re_at])
        im = nn(sig[0 : 2 * own, :], tab[:, im_at])
        hr, hi = hat[:, re_at].astype(f32), hat[:, im_at].astype(f32)
        kr, ki = hr[:own], hi[:own]
        kg_re, kg_im = 0.0, 0.0
        for h in range(2):
            mr, mi = re[own * h : own * (h + 1)], im[own * h : own * (h + 1)]
            sr, si = hr[own * (h + 1) : own * (h + 2)], hi[own * (h + 1) : own * (h + 2)]
            prod[own * h : own * (h + 1), re_at] = (kr * mr + ki * mi).astype(bf16)
            prod[own * h : own * (h + 1), im_at] = (kr * mi - ki * mr).astype(bf16)
            kg_re = kg_re + sr * mr + si * mi
            kg_im = kg_im + sr * mi - si * mr
        prod[2 * own : 3 * own, re_at] = kg_re.astype(bf16)
        prod[2 * own : 3 * own, im_at] = kg_im.astype(bf16)
        return carry

    lax.fori_loop(0, freq // lane_tile, grad_freq, 0)
    big_step(1)

    def grad_time(j, carry):
        at = token(j)
        all3 = nt(prod[...], tab[at, :])
        sgr[:, at] = (all3[:own] * masks[0:1, at] + all3[own : 2 * own] * masks[1:2, at]) * (1.0 / freq)
        kgr[:, at] = all3[2 * own :] * (1.0 / freq)
        return carry

    lax.fori_loop(0, ways, grad_time, 0)

    def sum_slot(index, at, size):
        if index < seq // 128:
            return query.at[pl.ds(at, size), 128 * index : 128 * index + 128]
        index = index - seq // 128
        return n2own.at[pl.ds(own * (index % ways) + at, size), 128 * (index // ways) : 128 * (index // ways) + 128]

    def ahead2(values, steps):
        if steps == 0:
            return values
        return jnp.where(lane2 < seq - steps, pltpu.roll(values, seq - steps, 1), 0.0)

    def chain_rows(i, carry):
        at = pl.multiple_of(i * tall, tall)
        here, here1, here2 = (pl.ds(pl.multiple_of(j * own + i * tall, tall), tall) for j in range(3))
        tap = cols[here, :]

        def note(index, values):
            sum_slot(index, at, tall)[...] = sum(values[:, 128 * b : 128 * b + 128] for b in range(seq // 128))

        key, value = kv[here, :], kv[here1, :]
        kgrad = jnp.where(lane2 < lags, kgr[here, :], 0.0)
        base_grad = kgrad * (jnp.exp(-tap[:, 12:13] * place2) * (1.0 / math.sqrt(seq)))
        kgr[here, :] = base_grad
        note(12, -kgrad * kern[here, :] * place2)
        bent = squash[here, :]
        cond_grad = base_grad * (1.0 - bent * bent)
        sgrad = sgr[here, :]
        value_grad = sgrad * key
        for k in range(3):
            moved = ahead2(cond_grad, k)
            note(9 + k, moved * value)
            value_grad = value_grad + tap[:, 9 + k : 10 + k] * moved
        branch = (mgf[here, :].astype(f32) * mixed[here, :], sgrad * value, value_grad)
        for j, rows_at in enumerate((here, here1, here2)):
            part = proj[rows_at, :]
            total = 0.0
            for k in range(3):
                moved = ahead2(branch[j], k)
                note(3 * k + j, moved * part)
                total = total + tap[:, 3 * k + j : 3 * k + j + 1] * moved
            sig[rows_at, :] = total.astype(bf16)
        return carry

    lax.fori_loop(0, own // tall, chain_rows, 0)
    big_step(0)
    big_step(1)

    def finish_sums():
        ones_square = jnp.ones((128, 128), f32)

        def run(i, carry):
            at = pl.multiple_of(i * 64, 64)
            column = lax.broadcasted_iota(jnp.int32, (64, 128), 1)
            stat = jnp.zeros((64, 128), f32)
            for index in range(13):
                stat = jnp.where(column == index, nn(sum_slot(index, at, 64)[...], ones_square, highest), stat)
            sm[pl.ds(at, 64), :] = stat
            return carry

        lax.fori_loop(0, own // 64, run, 0)


    h_sum = LineSum(
        lambda dest, sub: tbuf.at[own_rows(dest), token(sub)],
        lambda way, k, sub: tin.at[way, k, own_rows(sub), :],
        hs_send, hs_recv, z, ways, ways)
    f_sum.drain()
    mom_msg = Direct(lambda to: mom.at[z], lambda at: mom.at[at], mom_send, mom_recv)

    def in_back(tile):
        at = token(tile)
        rres[...] = tn(in_t[...], sig[:, at])
        tbuf[:, at] = rres[...].astype(bf16)
        h_sum.first(0, (tile, tile), False)
        normed = (xf[:, at].astype(f32) - stat1[0:1, at]) * stat1[1:2, at]
        upstream = rres[...] * gaincol[:, 0:1]
        mom[z, 0:1, at] = jnp.sum(upstream, axis=0, keepdims=True)
        mom[z, 1:2, at] = jnp.sum(upstream * normed, axis=0, keepdims=True)
        gsum[tile] = nt(ones, (rres[...] * normed).astype(bf16))

    gb2 = gg.at[0 : 4 * own, 0:width]
    sum2 = mid.at[0 : 4 * own, 0:width]

    def proj_grad(lhs, rhs, place_at):
        def run(j, carry):
            gb2[pl.ds(pl.multiple_of(place_at + j * own, row_tile), own), :] = nt(
                lhs[pl.ds(pl.multiple_of(j * own, row_tile), own), :], rhs[...]).astype(bf16)
            return carry

        lax.fori_loop(0, lhs.shape[0] // own, run, 0)

    two = RowSum(gb2, sum2, rb2, rbx2, ar_send.at[2], ar_recv.at[2], r, all_bits)
    two_tasks = two.tasks()

    dp_rows, all_rows = pl.ds(0, own), pl.ds(own, 80)

    def small_copy(chain, b):
        at = (dp_rows, all_rows)[chain]
        return pltpu.make_async_remote_copy(
            src_ref=sm.at[at], dst_ref=smbox.at[b, at], send_sem=sm_send.at[chain, b], recv_sem=sm_recv.at[chain, b],
            device_id={"dp": flipped(r, b)}, device_id_type=MESH,
        )

    def small_step(chain, b):
        at = (dp_rows, all_rows)[chain]
        small_copy(chain, b).wait()
        sm[at, :] += smbox[b, at, :]
        if b + 1 < all_bits:
            small_copy(chain, b + 1).start()

    def near(summer, k, index):
        summer.near(k, by_end(index) if summer is e_sum else plain_order[index])

    def far(summer, k, index):
        summer.far(k, by_end(index) if summer is e_sum else plain_order[index])

    total = rres.at[0:own, :]

    def output_part(tile):
        at = token(tile)
        total[...] = mbuf[span, at].astype(f32)
        for way in (0, 1):
            e_sum.take(way, tile, total)
        resown[:, at] = (resown[:, at] + total[...]) * masks[2:3, at]

    def input_part(tile):
        at = token(tile)
        total[...] = tbuf[span, at].astype(f32)
        for way in (0, 1):
            h_sum.take(way, tile, total)
        sums = sum(mom[s, :, at] for s in range(ways)) * (1.0 / width)
        inverse = stat1[1:2, at]
        normed = (xf[span, at].astype(f32) - stat1[0:1, at]) * inverse
        upstream = total[...] * gaincol[span, 0:1]
        sgr[:, at] = pgo[:, at].astype(f32) + inverse * (upstream - sums[0:1, :] - normed * sums[1:2, :])
        save(sgr.at[:, at], igrad_hbm.at[:, at])

    def in_turn(tile, carry):
        in_back(tile)
        return carry

    lax.fori_loop(0, ways, in_turn, 0)
    big_step(0)
    for index in every:
        h_sum.note_first(0, plain_order[index])
    mom_msg.start()
    swap_proj.wait_recv()
    proj_grad(sig, n1o, 0)
    proj_grad(pgo, mixf, 3 * own)
    two_tasks.pop(0)()
    for index in every:
        h_sum.first(1, plain_order[index])
    for index in first_two:
        far(e_sum, 0, index)
    for k in range(ways - 2):
        near(e_sum, k, 2)

    wave_grad = tn(cols[:, 64:128], kgr[...], highest) * jnp.cos(arg[...])
    finish_sums()
    two_tasks.pop(0)()
    big_step(0)
    big_step(1)
    for index in every:
        near(h_sum, 0, index)
    sm[0:own, 64:128] = nt(kgr[...], jnp.sin(arg[...]), highest)
    sm[own : own + 64, 0:64] = nt(feat_ref[...], wave_grad, highest)
    sm[own : own + 64, 64:128] = jnp.zeros((64, 64), f32)
    sm[own + 64 :, :] = jnp.zeros((16, 128), f32)
    for b in range(width // 128):
        lanes = slice(128 * b, 128 * b + 128)
        sm[own + 64 + b : own + 65 + b, :] = sum(gsum[tile, 0:1, lanes] for tile in range(ways))
        sm[own + 72 + b : own + 73 + b, :] = gsum[ways, 0:1, lanes]
    small_copy(0, 0).start()
    z_msg = Direct(lambda to: zbox.at[z], lambda at: zbox.at[at], z_send, z_recv)
    zbox[z] = sm[own:, :]
    z_msg.start()
    two_tasks.pop(0)()
    small_step(0, 0)
    for k in range(ways - 2):
        e_sum.first(k, by_end(3))
    for index in every:
        far(h_sum, 0, index)
    two_tasks.pop(0)()
    for index in every:
        h_sum.first(2, plain_order[index])
    for index in every:
        near(h_sum, 1, index)
    for k in range(ways - 2):
        near(e_sum, k, 3)
    for index in every:
        e_sum.first(ways - 2, by_end(index))
    two_tasks.pop(0)()
    small_step(0, 1)
    z_msg.wait_recv()
    zsum = zbox[0]
    for other in range(1, ways):
        zsum = zsum + zbox[other]
    sm[own:, :] = zsum
    small_copy(1, 0).start()
    small_step(1, 0)
    far(e_sum, 0, 2)
    two_tasks.pop(0)()
    for b in range(2, all_bits):
        small_step(0, b)
    far(e_sum, 0, 3)
    big_step(1)
    small_step(1, 1)
    big_step(0)
    two_tasks.pop(0)()
    save(sum2, proj_hbm)
    for b in range(2, all_bits):
        small_step(1, b)
    save(sm, small_hbm)
    big_step(1)
    big_step(0)
    save(weights, big_hbm)
    mom_msg.wait_recv()
    input_part(0)
    input_part(1)
    input_part(2)
    input_part(3)
    def output_turn(tile, carry):
        output_part(tile)
        return carry

    lax.fori_loop(0, ways, output_turn, 0)
    save(resown, out_hbm)

    for line in (in_line, g_line, mix_line, e_sum, h_sum, gain_msg, piece_msg, swap_mix, swap_proj, mom_msg, z_msg, big_parts[0], big_parts[1], two):
        line.drain()
    for make, piece in piece_sends:
        make(piece).wait_send()
    for copy in saves:
        copy.wait()


def layer(cfg, x_own, g_own, out_t, in_t, table, w_gate, w_up, w_down, halves, gain1, gain2, short_taps, cond_taps, rates,
          filter_in, filter_bias, filter_out, feats):
    ways, seq, own, width, hidden, bits, all_bits = cfg
    period = 3 * seq // 2
    block = seq // ways
    big_rows = hidden + 2 * width
    assert hidden == width
    held = dict(
        xf=((width, seq), bf16), gf=((width, seq), bf16), outt=((width, width), bf16), proj=((3 * own, seq), f32),
        mixf=((width, seq), bf16), query=((own, seq), f32), kv=((2 * own, seq), f32), squash=((own, seq), f32), kern=((own, seq), f32),
        mixed=((own, seq), f32), hat=((3 * own, period), bf16), arg=((64, seq), f32), in_t=((3 * own, width), bf16),
        tab=((seq, period), bf16), n1o=((width, seq), bf16), masks=((8, seq), f32), cols=((own, 128), f32),
        prow=((128, 256), f32), frow=((64, 64), f32),
        pieces=((1 << bits, ways, own * width // 128 // (1 << bits), 128), bf16), gains=((ways, 8, 256), f32),
        gaincol=((width, 128), f32), stat1=((8, seq), f32), sig=((3 * own, seq), bf16), prod=((3 * own, period), bf16),
        weights=((big_rows, width), bf16), n2o=((width, seq), bf16),
        mid=((hidden, seq), bf16), gg=((hidden, seq), bf16), ug=((hidden, seq), bf16), tbuf=((width, seq), bf16),
        tin=((2, ways - 1, width, block), bf16), mbuf=((width, seq), bf16), ein=((2, ways - 1, own, seq), bf16),
        gb=((big_rows, width), bf16), rb=((big_rows * 7 // 8, width), bf16),
        rbx=((max(all_bits - 3, 1), big_rows // 8 if all_bits > 3 else 32, width), bf16),
        rb2=((4 * own * 7 // 8, width), bf16),
        rbx2=((max(all_bits - 3, 1), 4 * own // 8 if all_bits > 3 else 16, width), bf16),
        n2own=((width, block), f32), inv2=((8, block), f32), rres=((width, block), f32), resown=((own, seq), f32),
        pgb=((width, block), bf16), mgb=((width, block), bf16), mgf=((own, seq), bf16), pgo=((own, seq), bf16),
        sgr=((own, seq), f32), kgr=((own, seq), f32), sm=((own + 80, 128), f32),
        smbox=((all_bits, own + 80, 128), f32), zbox=((ways, 80, 128), f32),
        mom=((ways, 8, seq), f32), gsum=((ways + 1, 8, width), f32),
    )
    hops = (3, 2, ways - 1, ways)
    sems = dict(
        load_sem=(11,), line_send=hops, line_recv=hops, piece_send=(ways + (1 << bits),), piece_recv=(ways + (1 << bits),),
        gain_send=(ways,), gain_recv=(ways,), save_sem=(8,), fs_send=(2, ways - 1, 2), fs_recv=(2, ways - 1, 2),
        es_send=(2, ways - 1, ways), es_recv=(2, ways - 1, ways), hs_send=(2, ways - 1, ways), hs_recv=(2, ways - 1, ways),
        sw_send=(2, ways), sw_recv=(2, ways), pace_sem=None, ar_send=(3, 3 + max(all_bits, 3)), ar_recv=(3, 3 + max(all_bits, 3)),
        sm_send=(2, all_bits), sm_recv=(2, all_bits), z_send=(ways,), z_recv=(ways,), mom_send=(ways,), mom_recv=(ways,),
    )
    here = pl.BlockSpec(memory_space=pltpu.VMEM)
    there = pl.BlockSpec(memory_space=pl.ANY)
    outs = [
        ((own, seq), f32), ((own, seq), f32), ((big_rows, width), bf16), ((4 * own, width), bf16),
        ((own + 80, 128), f32),
    ]
    return pl.pallas_call(
        functools.partial(layer_kernel, cfg),
        out_shape=[jax.ShapeDtypeStruct(s, t) for s, t in outs],
        in_specs=[there] * 8 + [pl.BlockSpec(memory_space=pltpu.SMEM)] + [here] * 9,
        out_specs=[there] * len(outs),
        scratch_shapes=[pltpu.VMEM(s, t) for s, t in held.values()] + [
            pltpu.SemaphoreType.REGULAR if s is None else pltpu.SemaphoreType.DMA(s) for s in sems.values()],
        compiler_params=pltpu.CompilerParams(collective_id=0, has_side_effects=True, vmem_limit_bytes=64 << 20),
    )(x_own, g_own, out_t, in_t, table, w_gate, w_up, w_down, halves, gain1, gain2, short_taps, cond_taps, rates,
      filter_in, filter_bias, filter_out, feats)


def widen_kernel(
    cfg, count, out_in, igrad_in, big_in, two_in, small_ref,
    out_hbm, igrad_hbm, wd_hbm, wg_hbm, wu_hbm, in_hbm, outp_hbm, gain1_ref, gain2_ref, short_ref, cond_ref, rate_ref,
    fin_ref, fbias_ref, fout_ref, low, wide, through, in_sem, out_sem, copy_sem,
):
    ways, seq, own, width, hidden, bits, all_bits = cfg
    step = own
    sources = [(big_in, at) for at in range(0, hidden + 2 * width, step)] + [(two_in, at) for at in range(0, 4 * own, step)]
    targets = [
        (ref, at) for ref, size in ((wd_hbm, hidden), (wg_hbm, width), (wu_hbm, width), (in_hbm, 3 * own), (outp_hbm, own))
        for at in range(0, size, step)]
    loads = [
        pltpu.make_async_copy(src.at[pl.ds(at, step)], low.at[i], in_sem.at[i]) for i, (src, at) in enumerate(sources)]
    for copy in loads:
        copy.start()
    ins = [pltpu.make_async_copy(src, through.at[i], copy_sem.at[i]) for i, src in enumerate((out_in, igrad_in))]
    for copy in ins:
        copy.start()
    moves = []
    stats = small_ref[0:own, :].T
    for i in range(3):
        for j in range(3):
            short_ref[i, j : j + 1, :] = stats[3 * i + j : 3 * i + j + 1, :]
    cond_ref[...] = stats[9:12, :]
    rate_ref[...] = stats[12:13, :]
    fout_ref[...] = stats[64:128, :]
    fin_ref[...] = small_ref[own : own + count, 0:64]
    fbias_ref[...] = small_ref[own + count : own + count + 1, 0:64]
    shift = (width - own * lax.axis_index("chan")) % width
    for first, ref in ((64, gain1_ref), (72, gain2_ref)):
        row = jnp.concatenate([small_ref[own + first + b : own + first + b + 1, :] for b in range(width // 128)], axis=1)
        ref[...] = pltpu.roll(jnp.broadcast_to(row, (8, width)), shift, 1)[0:1, 0:own]
    for i, ref in enumerate((out_hbm, igrad_hbm)):
        ins[i].wait()
        copy = pltpu.make_async_copy(through.at[i], ref, copy_sem.at[2 + i])
        copy.start()
        moves.append(copy)
    for i, (ref, at) in enumerate(targets):
        loads[i].wait()
        wide[i] = low[i].astype(f32)
        copy = pltpu.make_async_copy(wide.at[i], ref.at[pl.ds(at, step)], out_sem.at[i])
        copy.start()
        moves.append(copy)
    for copy in moves:
        copy.wait()


def widen(cfg, count, output, input_grad, big, two, small):
    ways, seq, own, width, hidden, bits, all_bits = cfg
    here = pl.BlockSpec(memory_space=pltpu.VMEM)
    there = pl.BlockSpec(memory_space=pl.ANY)
    far = [(own, seq), (own, seq), (hidden, width), (width, hidden), (width, hidden), (3 * own, width), (own, width)]
    near = [(1, own), (1, own), (3, 3, own), (3, own), (1, own), (count, 64), (1, 64), (64, own)]
    steps = (hidden + 2 * width + 4 * own) // own
    dma = pltpu.SemaphoreType.DMA
    return pl.pallas_call(
        functools.partial(widen_kernel, cfg, count),
        out_shape=[jax.ShapeDtypeStruct(shape, f32) for shape in far + near],
        in_specs=[there] * 4 + [here],
        out_specs=[there] * len(far) + [here] * len(near),
        scratch_shapes=[
            pltpu.VMEM((steps, own, width), bf16), pltpu.VMEM((steps, own, width), f32),
            pltpu.VMEM((2, own, seq), f32), dma((steps,)), dma((steps,)), dma((4,))],
        compiler_params=pltpu.CompilerParams(vmem_limit_bytes=64 << 20),
    )(output, input_grad, big, two, small)


def local(
    hidden_in, halves, norm1_gain, in_proj, short_taps, cond_taps, filter_in, filter_bias,
    filter_out, decay_rate, out_proj, norm2_gain, w_gate, w_up, w_down, out_grad,
):
    seq, own = hidden_in.shape[1], hidden_in.shape[2]
    ways, rows = lax.axis_size("chan"), lax.axis_size("dp")
    width, hidden = own * ways, w_gate.shape[1]
    z = lax.axis_index("chan")
    all_bits = rows.bit_length() - 1
    cfg = (ways, seq, own, width, hidden, 3, all_bits)
    count = filter_in.shape[0]
    feat_np = np.concatenate([
        band_features(seq, count), np.ones((1, seq), np.float32), np.zeros((63 - count, seq), np.float32)])
    table = jnp.asarray(wave_matrix(seq).astype(np.float32)).astype(bf16)

    output, input_grad, big, two, small = layer(
        cfg, hidden_in[0].T, out_grad[0].T, out_proj.T, in_proj.transpose(1, 2, 0).reshape(3 * own, width), table,
        w_gate, w_up, w_down, halves, norm1_gain[None], norm2_gain[None], short_taps, cond_taps, decay_rate[None],
        filter_in, filter_bias[None], filter_out, jnp.asarray(feat_np))

    (output, input_grad, wd_sum, wg_sum, wu_sum, in_sum, out_sum, gain1, gain2, short, cond, rates, fin, fbias, fout) = widen(
        cfg, count, output, input_grad, big, two, small)
    return (
        output.T[None], input_grad.T[None], gain1[0], in_sum.reshape(3, own, width).transpose(2, 0, 1), short, cond, fin,
        fbias[0], fout, rates[0], out_sum.T, gain2[0], wg_sum, wu_sum, wd_sum,
    )


def solution(mesh):
    rows, cols = P("dp", None, "chan"), P(None, "chan")
    in_specs = (
        rows, P("dp", None), P("chan"), P(None, None, "chan"), P(None, None, "chan"), cols, P(), P(),
        cols, P("chan"), cols, P("chan"), cols, cols, P("chan", None), rows,
    )
    out_specs = (
        rows, rows, P("chan"), P(None, None, "chan"), P(None, None, "chan"), cols, P(), P(),
        cols, P("chan"), cols, P("chan"), cols, cols, P("chan", None),
    )
    return jax.shard_map(local, mesh=mesh, in_specs=in_specs, out_specs=out_specs, check_vma=False)
```

```python
import functools
import math

import jax
import jax.numpy as jnp
import numpy as np
from jax import lax
from jax.experimental import pallas as pl
from jax.experimental.pallas import tpu as pltpu
from jax.sharding import PartitionSpec as P

highest = lax.Precision.HIGHEST
norm_eps = 1e-05
f32 = jnp.float32
bf16 = jnp.bfloat16


def band_features(seq_len, feat_count):
    bands = (feat_count - 1) // 2
    positions = np.arange(seq_len)
    orders = np.arange(1, bands + 1)
    phases = (orders[:, None] * positions[None, :] % seq_len) * (2.0 * math.pi / seq_len)
    ramp = positions[None, :] / seq_len
    return np.concatenate([ramp, np.sin(phases), np.cos(phases)], axis=0).astype(np.float32)


def wave_matrix(seq_len):
    period = 3 * seq_len // 2
    freq = period // 2
    phase = (np.arange(seq_len)[:, None] * (2 * np.arange(freq)[None, :] + 1)) % (2 * period)
    angle = phase * (math.pi / period)
    return np.concatenate([np.cos(angle), np.sin(angle)], axis=1)


def nn(a, b, precision=None):
    return lax.dot_general(a, b, (((1,), (0,)), ((), ())), precision=precision, preferred_element_type=f32)


def nt(a, b, precision=None):
    return lax.dot_general(a, b, (((1,), (1,)), ((), ())), precision=precision, preferred_element_type=f32)


def tn(a, b, precision=None):
    return lax.dot_general(a, b, (((0,), (0,)), ((), ())), precision=precision, preferred_element_type=f32)


MESH = pl.DeviceIdType.MESH
lane_tile = 256
row_tile = 16


def flipped(index, bit):
    return index + (1 << bit) * (1 - 2 * ((index // (1 << bit)) % 2))


def both(first, second):
    if second is True:
        return first
    return second if first is True else jnp.logical_and(first, second)


class Line:
    def __init__(self, view, send_sem, recv_sem, at, ways):
        self.view, self.send_sem, self.recv_sem, self.at, self.ways = view, send_sem, recv_sem, at, ways
        self.pending, self.arrived = {}, set()

    def copy(self, way, hop, part, shard):
        ref = self.view(shard, part)
        step = 1 - 2 * way
        return pltpu.make_async_remote_copy(
            src_ref=ref, dst_ref=ref, send_sem=self.send_sem.at[way, hop, part],
            recv_sem=self.recv_sem.at[way, hop, part],
            device_id={"chan": (self.at + step + self.ways) % self.ways}, device_id_type=MESH,
        )

    def sends(self, way, hop):
        if way == 0:
            return jnp.logical_and(self.at >= hop, self.at < self.ways - 1)
        return jnp.logical_and(self.at + hop <= self.ways - 1, self.at > 0)

    def gets(self, way, hop):
        if way == 0:
            return self.at >= hop + 1
        return self.at + hop + 1 <= self.ways - 1

    def order(self, way, index):
        return index if way == 0 else self.ways - 1 - index

    def far_side(self):
        return (2 * self.at) // self.ways

    def launch(self, hop, way, index, wanted, wait_first):
        part, step = self.order(way, index), 1 - 2 * way

        @pl.when(both(self.sends(way, hop), wanted()))
        def _():
            if wait_first:
                self.copy(way, hop - 1, part, self.at - hop * step).wait_recv()
            self.copy(way, hop, part, self.at - hop * step).start()

        def left(also):
            @pl.when(both(both(self.sends(way, hop), wanted()), also))
            def _():
                self.copy(way, hop, part, self.at - hop * step).wait_send()

        self.pending.setdefault((hop, way, index), []).append(left)

    def settle(self, hops, indices, wanted=True):
        for key in [k for k in self.pending if k[0] in hops and k[2] in indices]:
            before = self.pending.pop(key)
            for left in before:
                left(wanted)
            if wanted is not True:
                self.pending[key] = [
                    lambda also, left=left: left(both(jnp.logical_not(wanted), also)) for left in before]

    def send_own(self, indices, wanted, inward=None):
        for index in indices:
            for way in (0, 1):
                def ok(way=way):
                    if inward is None:
                        return wanted
                    facing = self.far_side() == way
                    return both(wanted, facing if inward else jnp.logical_not(facing))
                self.launch(0, way, index, ok, False)

    def relay(self, way, index, wanted, hops=None, wait_first=True):
        for hop in range(1, self.ways - 1) if hops is None else hops:
            self.launch(hop, way, index, wanted, wait_first)

    def short_way(self, index):
        for way in (0, 1):
            self.relay(way, index, lambda way=way: self.far_side() == way)

    def long_way(self, index, hops=None):
        for way in (0, 1):
            self.relay(way, index, lambda way=way: self.far_side() != way, hops, index not in self.arrived)

    def arrive(self, index):
        self.arrived.add(index)
        for way in (0, 1):
            for hop in range(1, self.ways - 1):
                @pl.when(jnp.logical_and(self.sends(way, hop), self.far_side() != way))
                def _():
                    self.copy(way, hop - 1, self.order(way, index), self.at - hop * (1 - 2 * way)).wait_recv()

    def take(self, index):
        for way in (0, 1):
            for hop in range(self.ways - 1):
                last = self.gets(way, hop)
                if hop + 1 < self.ways - 1:
                    last = jnp.logical_and(last, jnp.logical_not(self.sends(way, hop + 1)))

                @pl.when(last)
                def _():
                    self.copy(way, hop, self.order(way, index), self.at - (hop + 1) * (1 - 2 * way)).wait_recv()

    def drain(self):
        self.settle(range(self.ways), range(self.ways))


class LineSum:
    def __init__(self, mine, inbox, send_sem, recv_sem, at, ways, subs):
        self.mine, self.inbox, self.send_sem, self.recv_sem = mine, inbox, send_sem, recv_sem
        self.at, self.ways, self.subs = at, ways, subs
        self.pending = {}

    def dest(self, way, k):
        return self.ways - 1 - k if way == 0 else k

    def sends(self, way, k):
        return self.dest(way, k) > self.at if way == 0 else self.dest(way, k) < self.at

    def gets(self, way, k):
        dest = self.dest(way, k)
        if way == 0:
            return jnp.logical_and(dest >= self.at, self.at > 0)
        return jnp.logical_and(dest <= self.at, self.at < self.ways - 1)

    def copy(self, way, k, sub):
        step = 1 - 2 * way
        return pltpu.make_async_remote_copy(
            src_ref=self.mine(self.dest(way, k), sub), dst_ref=self.inbox(way, k, sub),
            send_sem=self.send_sem.at[way, k, sub], recv_sem=self.recv_sem.at[way, k, sub],
            device_id={"chan": (self.at + step + self.ways) % self.ways}, device_id_type=MESH,
        )

    def first(self, k, sub, noted=True):
        for way in (0, 1):
            def starts(way=way):
                return jnp.logical_and(self.sends(way, k), jnp.logical_not(self.gets(way, k)))

            @pl.when(starts())
            def _():
                self.copy(way, k, sub[way]).start()
            if noted:
                self.note(way, k, sub[way], starts)

    def note_first(self, k, sub):
        for way in (0, 1):
            self.note(way, k, sub[way], lambda way=way: jnp.logical_and(
                self.sends(way, k), jnp.logical_not(self.gets(way, k))))

    def note(self, way, k, sub, going):
        def left(also):
            @pl.when(both(going(), also))
            def _():
                self.copy(way, k, sub).wait_send()
        self.pending.setdefault(k, []).append(left)

    def settle(self, k, wanted=True):
        before = self.pending.pop(k, [])
        for left in before:
            left(wanted)
        if wanted is not True:
            self.pending[k] = [
                lambda also, left=left: left(both(jnp.logical_not(wanted), also)) for left in before]

    def onward(self, way, k, sub, wanted):
        def going():
            return both(jnp.logical_and(self.sends(way, k), self.gets(way, k)), wanted())

        self.note(way, k, sub, going)

        @pl.when(going())
        def _():
            self.copy(way, k, sub).wait_recv()
            mine, inbox = self.mine(self.dest(way, k), sub), self.inbox(way, k, sub)
            mine[...] = (mine[...].astype(f32) + inbox[...].astype(f32)).astype(bf16)
            self.copy(way, k, sub).start()

    def near(self, k, sub):
        for way in (0, 1):
            self.onward(way, k, sub[way], lambda way=way: (2 * self.at) // self.ways == way)

    def far(self, k, sub):
        for way in (0, 1):
            self.onward(way, k, sub[way], lambda way=way: (2 * self.at) // self.ways != way)

    def take(self, way, sub, total):
        k = self.ways - 1 - self.at if way == 0 else self.at

        @pl.when(self.at > 0 if way == 0 else self.at < self.ways - 1)
        def _():
            self.copy(way, k, sub).wait_recv()
            total[...] += self.inbox(way, k, sub)[...].astype(f32)

    def drain(self):
        for k in list(self.pending):
            self.settle(k)


class RowSum:
    tile = 48

    def __init__(self, buf, result, box, extra_box, send_sem, recv_sem, r, total_bits):
        self.buf, self.result, self.box, self.extra_box = buf, result, box, extra_box
        self.send_sem, self.recv_sem = send_sem, recv_sem
        self.total_bits, self.r = total_bits, r
        height = buf.shape[0]
        core = r % 2
        steps = [1, 2 + 2 * core, 4 - 2 * core]
        self.levels = []
        base, size = 0, height
        inbox_at = 0
        for step in steps:
            size = size // 2
            bit = (r // step) % 2
            keep, give = base + bit * size, base + (1 - bit) * size
            self.levels.append((r + step * (1 - 2 * bit), keep, give, size, inbox_at))
            base = keep
            inbox_at += size

    def rows(self, at, size, buf=None):
        return (self.buf if buf is None else buf).at[pl.ds(pl.multiple_of(at, 16), size)]

    def halve(self, level):
        partner, keep, give, size, inbox_at = self.levels[level]
        return pltpu.make_async_remote_copy(
            src_ref=self.rows(give, size), dst_ref=self.box.at[pl.ds(inbox_at, size)],
            send_sem=self.send_sem.at[level], recv_sem=self.recv_sem.at[level],
            device_id={"dp": partner}, device_id_type=MESH,
        )

    def double(self, level, arriving=False):
        partner, keep, give, size, inbox_at = self.levels[level]
        part = self.rows(give if arriving else keep, size, self.result)
        return pltpu.make_async_remote_copy(
            src_ref=part, dst_ref=part, send_sem=self.send_sem.at[3 + level], recv_sem=self.recv_sem.at[3 + level],
            device_id={"dp": partner}, device_id_type=MESH,
        )

    def add(self, level, target=None):
        partner, keep, give, size, inbox_at = self.levels[level]
        target = self.buf if target is None else target
        self.halve(level).wait_recv()

        def run(i, carry):
            at = pl.ds(pl.multiple_of(keep + i * self.tile, 16), self.tile)
            there = pl.ds(pl.multiple_of(inbox_at + i * self.tile, 16), self.tile)
            target[at, :] = (self.buf[at, :].astype(f32) + self.box[there, :].astype(f32)).astype(bf16)
            return carry

        lax.fori_loop(0, size // self.tile, run, 0)

    def extra(self):
        partner, keep, give, size, inbox_at = self.levels[2]
        for bit in range(3, self.total_bits):
            copy = pltpu.make_async_remote_copy(
                src_ref=self.rows(keep, size, self.result), dst_ref=self.extra_box.at[bit - 3], send_sem=self.send_sem.at[3 + bit],
                recv_sem=self.recv_sem.at[3 + bit], device_id={"dp": flipped(self.r, bit)}, device_id_type=MESH,
            )
            copy.start()
            copy.wait()
            at = pl.ds(pl.multiple_of(keep, 16), size)
            self.result[at, :] = (self.result[at, :].astype(f32) + self.extra_box[bit - 3].astype(f32)).astype(bf16)

    def tasks(self):
        def second():
            self.add(0)
            self.halve(1).start()

        def third():
            self.add(1)
            self.halve(2).start()

        def turn():
            self.add(2, self.result)
            self.extra()
            self.double(2).start()

        def wider():
            self.double(2, True).wait_recv()
            self.double(1).start()

        def widest():
            self.double(1, True).wait_recv()
            self.double(0).start()

        def last():
            self.double(0, True).wait_recv()

        return [self.halve(0).start, second, third, turn, wider, widest, last]

    def drain(self):
        for level in range(3):
            self.halve(level).wait_send()
            self.double(level).wait_send()


def layer_kernel(
    cfg,
    x_hbm, g_hbm, outp_hbm, in_hbm, tab_hbm, wg_hbm, wu_hbm, wd_hbm, halves_ref, gain1_ref, gain2_ref, short_ref, cond_ref,
    rate_ref, fin_ref, fbias_ref, fout_ref, feat_ref,
    out_hbm, igrad_hbm, big_hbm, proj_hbm, small_hbm, *scratch,
):
    ways, seq, own, width, hidden, bits, all_bits = cfg
    (
        xf, gf, outt, proj, mixf, query, kv, squash, kern, mixed, hat, arg, in_t, tab, n1o, masks, cols, prow, frow,
        pieces, gains, gaincol, stat1, sig, prod, weights, n2o, mid, gg, ug, tbuf, tin, mbuf, ein,
        gb, rb, rbx, rb2, rbx2, n2own, inv2, rres, resown, pgb, mgb, mgf, pgo, sgr, kgr, sm, smbox, zbox, mom, gsum,
        load_sem, line_send, line_recv, piece_send, piece_recv, gain_send, gain_recv, save_sem,
        fs_send, fs_recv, es_send, es_recv, hs_send, hs_recv, sw_send, sw_recv,
        pace_sem, ar_send, ar_recv, sm_send, sm_recv, z_send, z_recv, mom_send, mom_recv,
    ) = scratch
    lags = 3 * seq // 4
    freq = lags
    block = seq // ways
    z = lax.axis_index("chan")
    r = lax.axis_index("dp")
    side = (2 * z) // ways
    inner = ((z + ways - 1) // ways) * ((2 * ways - 2 - z) // ways)
    group = r % (1 << bits)

    wd, wg, wu = (weights.at[pl.ds(at, size)] for at, size in ((0, hidden), (hidden, width), (hidden + width, width)))

    def own_rows(at):
        return pl.ds(pl.multiple_of(at * own, row_tile), own)

    def token(at):
        return pl.ds(pl.multiple_of(at * block, block), block)

    span = own_rows(z)
    saves = []

    def load(index, src, dst):
        copy = pltpu.make_async_copy(src, dst, load_sem.at[index])
        copy.start()
        return copy

    def save(src, dst):
        copy = pltpu.make_async_copy(src, dst, save_sem.at[len(saves)])
        copy.start()
        saves.append(copy)

    grain = 48
    per_piece = pieces.shape[2] // grain
    x_load = load(0, x_hbm, xf.at[span])
    g_load = load(1, g_hbm, gf.at[span])
    in_load = load(2, in_hbm, in_t)

    def piece_from(i):
        at = group * per_piece + i
        return outp_hbm.at[
            pl.ds(pl.multiple_of((at % (own // grain)) * grain, row_tile), grain),
            pl.ds(pl.multiple_of((at // (own // grain)) * 128, 128), 128)]

    piece_loads = [load(8 + i, piece_from(i), pieces.at[group, z, pl.ds(i * grain, grain)]) for i in range(per_piece)]
    tab_load = load(3, tab_hbm, tab)
    weight_loads = [load(4, wg_hbm, wg), load(5, wu_hbm, wu), load(6, wd_hbm, wd)]
    barrier = pltpu.get_barrier_semaphore()
    peers = [{"chan": (z + s) % ways} for s in range(1, ways)] + [{"dp": flipped(r, b)} for b in range(all_bits)]
    for peer in peers:
        pl.semaphore_signal(barrier, inc=1, device_id=peer, device_id_type=MESH)
    pl.semaphore_wait(barrier, len(peers))

    def cut(buf):
        return lambda shard, part: buf.at[own_rows(shard), token(part)]

    in_line, g_line, mix_line = (
        Line(cut(buf), line_send.at[i], line_recv.at[i], z, ways) for i, buf in enumerate((xf, gf, mixf)))

    class Direct:
        def __init__(self, view_src, view_dst, send, recv):
            self.view_src, self.view_dst, self.send, self.recv = view_src, view_dst, send, recv

        def copy(self, s, arriving):
            there = (z + s) % ways
            src = (z + ways - s) % ways
            dst = self.view_dst(src if arriving else z)
            return pltpu.make_async_remote_copy(
                src_ref=dst if arriving else self.view_src(there), dst_ref=dst, send_sem=self.send.at[s],
                recv_sem=self.recv.at[s], device_id={"chan": there}, device_id_type=MESH,
            )

        def start(self, wanted=None):
            for s in range(1, ways):
                if wanted is None:
                    self.copy(s, False).start()
                else:
                    @pl.when(wanted((z + s) % ways))
                    def _():
                        self.copy(s, False).start()

        def wait_recv(self):
            for s in range(1, ways):
                self.copy(s, True).wait_recv()

        def drain(self):
            for s in range(1, ways):
                self.copy(s, False).wait_send()

    gain_msg = Direct(lambda to: gains.at[z], lambda at: gains.at[at], gain_send, gain_recv)
    piece_msg = Direct(lambda to: pieces.at[group, z], lambda at: pieces.at[group, at], piece_send, piece_recv)

    gains[z] = jnp.zeros(gains.shape[1:], f32)
    gains[z, 0:1, 0:own] = gain1_ref[...]
    gains[z, 1:2, 0:own] = gain2_ref[...]
    gain_msg.start()
    x_load.wait()
    every, outer, middle = range(ways), inner == 0, inner == 1
    first_two, last_two = range(ways // 2), range(ways // 2, ways)
    next_hops, last_hops = range(1, 2), range(2, ways - 1)
    in_line.send_own(first_two, True)
    in_line.send_own(last_two, middle)

    def inside(at):
        return jnp.logical_and(at > 0, at < ways - 1)

    def early(there):
        return jnp.logical_or(inside(there), inner == 0)

    for copy in piece_loads:
        copy.wait()
    piece_msg.start(early)

    def clear(j, carry):
        gb[pl.ds(pl.multiple_of(j * 96, 96), 96), :] = jnp.zeros((96, width), bf16)
        return carry

    lax.fori_loop(0, gb.shape[0] // 96, clear, 0)

    line_at = lax.broadcasted_iota(jnp.int32, (1, seq), 1)
    split, valid = halves_ref[0, 0], halves_ref[0, 1]
    masks[0:1, :] = jnp.where(line_at < split, 1.0, 0.0)
    masks[1:2, :] = jnp.where(jnp.logical_and(line_at >= split, line_at < valid), 1.0, 0.0)
    masks[2:3, :] = masks[0:1, :] + masks[1:2, :]
    prow[...] = jnp.zeros(prow.shape, f32)
    for i in range(3):
        for j in range(3):
            prow[3 * i + j : 3 * i + j + 1, 0:own] = short_ref[i, j : j + 1, :]
    prow[9:12, 0:own] = cond_ref[...]
    prow[12:13, 0:own] = rate_ref[...]
    prow[64:128, 0:own] = fout_ref[...]
    cols[...] = prow[...].T[0:own, :]
    frow[...] = jnp.zeros(frow.shape, f32)
    frow[0 : fin_ref.shape[0], :] = fin_ref[...]
    frow[fin_ref.shape[0] : fin_ref.shape[0] + 1, :] = fbias_ref[...]
    g_load.wait()
    gf[span, :] = (gf[span, :].astype(f32) * masks[2:3, :]).astype(bf16)

    arg[...] = tn(frow[...], feat_ref[...], highest)
    kern[...] = nn(cols[:, 64:128], jnp.sin(arg[...]), highest)

    in_line.settle([0], first_two)
    in_line.send_own(last_two, outer)
    gain_msg.wait_recv()
    eye = lax.broadcasted_iota(jnp.int32, (own, gains.shape[2]), 0) == lax.broadcasted_iota(
        jnp.int32, (own, gains.shape[2]), 1)
    for s in range(ways):
        for which in range(2):
            row = gains[s, which : which + 1, :]
            gaincol[s * own : (s + 1) * own, which : which + 1] = jnp.sum(jnp.where(eye, row, 0.0), axis=1, keepdims=True)
    in_load.wait()

    def moments(values):
        centre = jnp.sum(values, axis=0, keepdims=True) * (1.0 / width)
        spread = jnp.sum(values * values, axis=0, keepdims=True) * (1.0 / width) - centre * centre
        return centre, lax.rsqrt(spread + norm_eps)

    def in_order(index):
        return side * index + (1 - side) * (ways - 1 - index)

    def norm1(q):
        at = token(q)
        values = xf[:, at].astype(f32)
        centre, inverse = moments(values)
        stat1[0:1, at] = centre
        stat1[1:2, at] = inverse
        low = ((values - centre) * inverse * gaincol[:, 0:1]).astype(bf16)
        n1o[:, at] = low
        proj[:, at] = nn(in_t[...], low)

    for index in first_two:
        in_line.short_way(index)
    for index in every:
        in_line.long_way(index, next_hops)
    for index in last_two:
        in_line.short_way(index)
    in_line.settle([0], last_two)
    g_line.send_own(every, outer)
    for index in first_two:
        in_line.long_way(index, last_hops)
    g_line.send_own(every, middle, inward=True)
    for index in last_two:
        in_line.long_way(index, last_hops)

    def norm_turn(index, carry):
        in_line.take(index)
        norm1(in_order(index))
        return carry

    lax.fori_loop(0, ways, norm_turn, 0)
    piece_msg.start(lambda there: jnp.logical_not(early(there)))
    for index in every:
        g_line.short_way(index)

    piece_sends = []

    def piece_step(bit, held, slot):
        batch = []
        for i, piece in enumerate(held):
            def make(which, slot=slot + i):
                return pltpu.make_async_remote_copy(
                    src_ref=pieces.at[which], dst_ref=pieces.at[which], send_sem=piece_send.at[slot],
                    recv_sem=piece_recv.at[slot], device_id={"dp": flipped(r, bit)}, device_id_type=MESH,
                )
            make(piece).start()
            batch.append((make, piece))
            piece_sends.append((make, piece))

        def finish():
            for make, piece in batch:
                make(flipped(piece, bit)).wait_recv()
        return finish, held + [flipped(piece, bit) for piece in held], slot + len(held)

    tab_load.wait()

    half1, half2 = masks[0:1, :], masks[1:2, :]

    def back(values, steps):
        if steps == 0:
            return values
        return jnp.where(lane2 >= steps, pltpu.roll(values, steps, 1), 0.0)

    def row_at(j, i):
        return pl.ds(pl.multiple_of(j * own + i * row_tile, row_tile), row_tile)

    tall = 2 * row_tile
    lane2 = lax.broadcasted_iota(jnp.int32, (tall, seq), 1)
    place2 = lane2.astype(f32)

    def mix_rows(i, carry):
        here, here1, here2 = (pl.ds(pl.multiple_of(j * own + i * tall, tall), tall) for j in range(3))
        tap = cols[here, :]
        outs = []
        for j in range(3):
            part = proj[(here, here1, here2)[j], :]
            outs.append(sum(tap[:, 3 * k + j : 3 * k + j + 1] * back(part, k) for k in range(3)))
        query[here, :] = outs[0]
        kv[here, :] = outs[1]
        kv[here1, :] = outs[2]
        cond = sum(tap[:, 9 + k : 10 + k] * back(outs[2], k) for k in range(3))
        bent = jnp.tanh(cond)
        squash[here, :] = bent
        filt = (kern[here, :] + bent) * (jnp.exp(-tap[:, 12:13] * place2) * (1.0 / math.sqrt(seq)))
        kern[here, :] = filt
        source = outs[1] * outs[2]
        sig[here, :] = jnp.where(lane2 < lags, filt, 0.0).astype(bf16)
        sig[here1, :] = (source * half1).astype(bf16)
        sig[here2, :] = (source * half2).astype(bf16)
        return carry

    lax.fori_loop(0, own // tall, mix_rows, 0)
    g_line.send_own(first_two, middle, inward=False)
    piece_msg.wait_recv()
    bit_list = list(reversed(range(bits)))
    finish, held, slot = piece_step(bit_list[0], [group], ways)

    def freq_at(j):
        return (pl.ds(pl.multiple_of(j * lane_tile, lane_tile), lane_tile),
                pl.ds(pl.multiple_of(freq + j * lane_tile, lane_tile), lane_tile))

    def freq_tile(j, carry):
        re_at, im_at = freq_at(j)
        re = nn(sig[...], tab[:, re_at])
        im = nn(sig[...], tab[:, im_at])
        hat[:, re_at] = re.astype(bf16)
        hat[:, im_at] = im.astype(bf16)
        kr, ki = re[:own], im[:own]
        for h in range(2):
            sr, si = re[own * (h + 1) : own * (h + 2)], im[own * (h + 1) : own * (h + 2)]
            prod[own * h : own * (h + 1), re_at] = (kr * sr - ki * si).astype(bf16)
            prod[own * h : own * (h + 1), im_at] = (kr * si + ki * sr).astype(bf16)
        return carry

    lax.fori_loop(0, freq // lane_tile, freq_tile, 0)

    def time_tile(j, carry):
        at = token(j)
        both = nt(prod[0 : 2 * own, :], tab[at, :])
        total = (both[:own] * masks[0:1, at] + both[own:] * masks[1:2, at]) * (1.0 / freq)
        mixed[:, at] = total
        mixf[span, at] = (query[:, at] * total).astype(bf16)
        return carry

    def time_turn(index, carry):
        time_tile(side * (ways - 1 - index) + (1 - side) * index, 0)
        for early_index in first_two:
            @pl.when(index == early_index)
            def _():
                mix_line.send_own([early_index], True, inward=True)
        return carry

    lax.fori_loop(0, ways, time_turn, 0)
    mix_line.send_own([0], middle, inward=False)
    finish()
    finish, held, slot = piece_step(bit_list[1], held, slot)
    for index in first_two:
        g_line.long_way(index)
    mix_line.settle([0], first_two, outer)
    mix_line.send_own(last_two, outer)
    finish()
    finish, held, slot = piece_step(bit_list[2], held, slot)
    finish()
    for s in range(ways):
        for block_at in range(own * width // 128 // grain):
            piece, inside_at = divmod(block_at, per_piece)
            column, down = divmod(block_at, own // grain)
            outt[s * own + down * grain : s * own + (down + 1) * grain, 128 * column : 128 * column + 128] = pieces[
                piece, s, inside_at * grain : (inside_at + 1) * grain, :]
    for copy in weight_loads:
        copy.wait()

    def pass_set(index):
        for line in (g_line, mix_line):
            line.long_way(index)

    mix_line.long_way(0, next_hops)
    for index in first_two:
        mix_line.short_way(index)
    mix_line.long_way(0, last_hops)
    mix_line.send_own(last_two, middle, inward=True)
    for index in last_two:
        mix_line.short_way(index)

    half_block = block // 2

    def half_token(at, sub):
        return pl.ds(pl.multiple_of(at * block + sub * half_block, half_block), half_block)

    f_sum = LineSum(
        lambda dest, sub: tbuf.at[:, half_token(dest, sub)],
        lambda way, k, sub: tin.at[way, k, :, pl.ds(sub * half_block, half_block)],
        fs_send, fs_recv, z, ways, 2)
    e_sum = LineSum(
        lambda dest, sub: mbuf.at[own_rows(dest), token(sub)],
        lambda way, k, sub: ein.at[way, k, :, token(sub)],
        es_send, es_recv, z, ways, ways)

    def by_end(index):
        return (ways - 1 - index, index)

    halves_of = [(sub, sub) for sub in range(2)]
    plain_order = [(sub, sub) for sub in range(ways)]

    def tiles(count, fn):
        def run(j, carry):
            fn(pl.ds(pl.multiple_of(j * lane_tile, lane_tile), lane_tile))
            return carry
        lax.fori_loop(0, count // lane_tile, run, 0)

    def forward(q):
        at = token(q)
        def resid_tile(ds):
            rres[ds, :] = xf[ds, at].astype(f32) + nn(outt[ds, :], mixf[:, at])

        tiles(width, resid_tile)
        resown[:, at] = rres[span, :]
        centre, inverse = moments(rres[...])
        n2o[:, at] = ((rres[...] - centre) * inverse * gaincol[:, 1:2]).astype(bf16)

        @pl.when(q == z)
        def _():
            n2own[...] = (rres[...] - centre) * inverse
            inv2[0:1, :] = inverse

        def hidden_tile(fs):
            low = n2o[:, at]
            gate = tn(wg[:, fs], low)
            up = tn(wu[:, fs], low)
            bent = jax.nn.sigmoid(gate)
            act = gate * bent
            mid[fs, at] = (act * up).astype(bf16)
            gg[fs, at] = (up * bent * (1.0 + gate * (1.0 - bent))).astype(bf16)
            ug[fs, at] = act.astype(bf16)

        tiles(hidden, hidden_tile)

    def down(q):
        at = token(q)

        def mlp_tile(ds):
            mbuf[ds, at] = tn(wd[:, ds], mid[:, at]).astype(bf16)

        tiles(width, mlp_tile)

    def backward(q):
        at = token(q)

        def back_tile(fs):
            grad = nn(wd[fs, :], gf[:, at])
            gg[fs, at] = (grad * gg[fs, at].astype(f32)).astype(bf16)
            ug[fs, at] = (grad * ug[fs, at].astype(f32)).astype(bf16)

        tiles(hidden, back_tile)

        def term_tile(ds):
            tbuf[ds, at] = (nn(wg[ds, :], gg[:, at]) + nn(wu[ds, :], ug[:, at])).astype(bf16)

        tiles(width, term_tile)

    def turn_tokens(index):
        late = index // (ways - 2)
        return in_order(index + inner * late * (1 - 2 * (index - (ways - 2))))

    def weight_grads(turn, carry):
        at = token(turn_tokens(turn))
        for lhs, rhs, place_at in ((mid, gf, 0), (n2o, gg, hidden), (n2o, ug, hidden + width)):
            def run(j, carry):
                rows_at = pl.ds(pl.multiple_of(j * lane_tile, lane_tile), lane_tile)
                to = pl.ds(pl.multiple_of(place_at + j * lane_tile, lane_tile), lane_tile)
                gb[to, :] = (nt(lhs[rows_at, at], rhs[:, at]) + gb[to, :].astype(f32)).astype(bf16)
                return carry
            lax.fori_loop(0, lhs.shape[0] // lane_tile, run, 0)
        return carry

    big_rows = hidden + 2 * width

    def feed_forward_turn(index, carry):
        def at_turn(which):
            return pl.when(index == which)

        q = turn_tokens(index)
        mix_line.take(index)

        @at_turn(ways - 1)
        def _():
            for early_index in first_two:
                for k in range(ways - 2):
                    e_sum.first(k, by_end(early_index))

        forward(q)
        for which in every:
            @at_turn(which)
            def _():
                if which == 0:
                    mix_line.send_own([1], middle, inward=False)
                    mix_line.long_way(1)
                elif which + 1 < ways:
                    for line in (g_line, mix_line):
                        line.send_own([which + 1], middle, inward=False)
                    for line in (g_line, mix_line):
                        line.settle(range(ways - 1), range(which + 1))

                    @pl.when(jnp.logical_and(middle, r % 2 == 0))
                    def _():
                        pl.semaphore_signal(pace_sem, inc=1, device_id={"dp": flipped(r, 0)}, device_id_type=MESH)

                    @pl.when(jnp.logical_and(middle, r % 2 == 1))
                    def _():
                        pl.semaphore_wait(pace_sem, 1)

                    pass_set(which + 1)
                if which == ways - 3:
                    g_line.arrive(ways - 1)
                    mix_line.arrive(ways - 1)
                if which == ways - 2:
                    for sub in halves_of:
                        f_sum.near(0, sub)
        g_line.take(index)
        backward(q)
        for which in every:
            @at_turn(which)
            def _():
                if which < ways - 1:
                    for sub in halves_of:
                        f_sum.first(which, sub)
                if which == ways - 1:
                    for sub in halves_of:
                        f_sum.near(1, sub)
                    for sub in halves_of:
                        f_sum.far(0, sub)
        pl.when(index < ways - 1)(lambda: down(q))
        seen = (index + ways - 1) // ways
        behind = seen * (1 - (index + ways - 2) // ways)
        lax.fori_loop(index - behind * index, seen * (index + 1), weight_grads, 0)
        return carry

    lax.fori_loop(0, ways, feed_forward_turn, 0)

    first_rows = big_rows // 2
    big_parts = []
    for i, at in enumerate((0, first_rows)):
        def cut_rows(buf, at=at, size=first_rows):
            return buf.at[pl.ds(at, size)]
        big = RowSum(
            cut_rows(gb), cut_rows(weights), cut_rows(rb, at * 7 // 8, first_rows * 7 // 8),
            rbx.at[:, pl.ds(i * (rbx.shape[1] // 2), rbx.shape[1] // 2)], ar_send.at[i], ar_recv.at[i], r, all_bits)
        big.halve(0).start()
        big_parts.append(big)
    big_left = [[big.tasks()[1:] for big in big_parts] for _ in range(2)]

    def big_step(inside_line):
        steps = [left.pop(0) for left in big_left[inside_line]]

        @pl.when(inner == inside_line)
        def _():
            for step in steps:
                step()

    rres[...] = tbuf[:, token(z)].astype(f32)
    for sub in range(2):
        for way in (0, 1):
            f_sum.take(way, sub, rres.at[:, pl.ds(sub * half_block, half_block)])
    upstream = rres[...] * gaincol[:, 1:2]
    normed = n2own[...]
    plain = jnp.sum(upstream, axis=0, keepdims=True) * (1.0 / width)
    cross = jnp.sum(upstream * normed, axis=0, keepdims=True) * (1.0 / width)
    pgb[...] = (gf[:, token(z)].astype(f32) + inv2[0:1, :] * (upstream - plain - normed * cross)).astype(bf16)
    def mix_grad_tile(ds):
        mgb[ds, :] = tn(outt[:, ds], pgb[...]).astype(bf16)

    tiles(width, mix_grad_tile)
    swap_mix = Direct(lambda to: mgb.at[own_rows(to)], lambda at: mgf.at[:, token(at)], sw_send.at[0], sw_recv.at[0])
    swap_proj = Direct(lambda to: pgb.at[own_rows(to)], lambda at: pgo.at[:, token(at)], sw_send.at[1], sw_recv.at[1])
    swap_mix.start()
    down(turn_tokens(ways - 1))
    mgf[:, token(z)] = mgb[span, :]
    pgo[:, token(z)] = pgb[span, :]
    ones = jnp.ones((8, block), bf16)
    gsum[ways] = nt(ones, (rres[...] * normed).astype(bf16))

    big_step(0)
    big_step(1)
    swap_mix.wait_recv()
    swap_proj.start()
    for k in range(ways - 2):
        e_sum.first(k, by_end(2))
    for index in first_two:
        for k in range(ways - 2):
            e_sum.near(k, by_end(index))

    def grad_rows(i, carry):
        here = row_at(0, i)
        down = mgf[here, :].astype(f32) * query[here, :]
        sig[row_at(0, i), :] = (down * half1).astype(bf16)
        sig[row_at(1, i), :] = (down * half2).astype(bf16)
        return carry

    lax.fori_loop(0, own // row_tile, grad_rows, 0)

    def grad_freq(j, carry):
        re_at, im_at = freq_at(j)
        re = nn(sig[0 : 2 * own, :], tab[:, re_at])
        im = nn(sig[0 : 2 * own, :], tab[:, im_at])
        hr, hi = hat[:, re_at].astype(f32), hat[:, im_at].astype(f32)
        kr, ki = hr[:own], hi[:own]
        kg_re, kg_im = 0.0, 0.0
        for h in range(2):
            mr, mi = re[own * h : own * (h + 1)], im[own * h : own * (h + 1)]
            sr, si = hr[own * (h + 1) : own * (h + 2)], hi[own * (h + 1) : own * (h + 2)]
            prod[own * h : own * (h + 1), re_at] = (kr * mr + ki * mi).astype(bf16)
            prod[own * h : own * (h + 1), im_at] = (kr * mi - ki * mr).astype(bf16)
            kg_re = kg_re + sr * mr + si * mi
            kg_im = kg_im + sr * mi - si * mr
        prod[2 * own : 3 * own, re_at] = kg_re.astype(bf16)
        prod[2 * own : 3 * own, im_at] = kg_im.astype(bf16)
        return carry

    lax.fori_loop(0, freq // lane_tile, grad_freq, 0)
    big_step(1)

    def grad_time(j, carry):
        at = token(j)
        all3 = nt(prod[...], tab[at, :])
        sgr[:, at] = (all3[:own] * masks[0:1, at] + all3[own : 2 * own] * masks[1:2, at]) * (1.0 / freq)
        kgr[:, at] = all3[2 * own :] * (1.0 / freq)
        return carry

    lax.fori_loop(0, ways, grad_time, 0)
    big_step(0)

    def sum_slot(index, at, size):
        if index < seq // 128:
            return query.at[pl.ds(at, size), 128 * index : 128 * index + 128]
        index = index - seq // 128
        return n2own.at[pl.ds(own * (index % ways) + at, size), 128 * (index // ways) : 128 * (index // ways) + 128]

    def ahead2(values, steps):
        if steps == 0:
            return values
        return jnp.where(lane2 < seq - steps, pltpu.roll(values, seq - steps, 1), 0.0)

    def chain_rows(i, carry):
        at = pl.multiple_of(i * tall, tall)
        here, here1, here2 = (pl.ds(pl.multiple_of(j * own + i * tall, tall), tall) for j in range(3))
        tap = cols[here, :]

        def note(index, values):
            sum_slot(index, at, tall)[...] = sum(values[:, 128 * b : 128 * b + 128] for b in range(seq // 128))

        key, value = kv[here, :], kv[here1, :]
        kgrad = jnp.where(lane2 < lags, kgr[here, :], 0.0)
        base_grad = kgrad * (jnp.exp(-tap[:, 12:13] * place2) * (1.0 / math.sqrt(seq)))
        kgr[here, :] = base_grad
        note(12, -kgrad * kern[here, :] * place2)
        bent = squash[here, :]
        cond_grad = base_grad * (1.0 - bent * bent)
        sgrad = sgr[here, :]
        value_grad = sgrad * key
        for k in range(3):
            moved = ahead2(cond_grad, k)
            note(9 + k, moved * value)
            value_grad = value_grad + tap[:, 9 + k : 10 + k] * moved
        branch = (mgf[here, :].astype(f32) * mixed[here, :], sgrad * value, value_grad)
        for j, rows_at in enumerate((here, here1, here2)):
            part = proj[rows_at, :]
            total = 0.0
            for k in range(3):
                moved = ahead2(branch[j], k)
                note(3 * k + j, moved * part)
                total = total + tap[:, 3 * k + j : 3 * k + j + 1] * moved
            sig[rows_at, :] = total.astype(bf16)
        return carry

    lax.fori_loop(0, own // tall, chain_rows, 0)
    big_step(1)

    def finish_sums():
        ones_square = jnp.ones((128, 128), f32)

        def run(i, carry):
            at = pl.multiple_of(i * 64, 64)
            column = lax.broadcasted_iota(jnp.int32, (64, 128), 1)
            stat = jnp.zeros((64, 128), f32)
            for index in range(13):
                stat = jnp.where(column == index, nn(sum_slot(index, at, 64)[...], ones_square, highest), stat)
            sm[pl.ds(at, 64), :] = stat
            return carry

        lax.fori_loop(0, own // 64, run, 0)


    h_sum = LineSum(
        lambda dest, sub: tbuf.at[own_rows(dest), token(sub)],
        lambda way, k, sub: tin.at[way, k, own_rows(sub), :],
        hs_send, hs_recv, z, ways, ways)
    f_sum.drain()
    mom_msg = Direct(lambda to: mom.at[z], lambda at: mom.at[at], mom_send, mom_recv)

    def in_back(tile):
        at = token(tile)
        rres[...] = tn(in_t[...], sig[:, at])
        tbuf[:, at] = rres[...].astype(bf16)
        h_sum.first(0, (tile, tile), False)
        normed = (xf[:, at].astype(f32) - stat1[0:1, at]) * stat1[1:2, at]
        upstream = rres[...] * gaincol[:, 0:1]
        mom[z, 0:1, at] = jnp.sum(upstream, axis=0, keepdims=True)
        mom[z, 1:2, at] = jnp.sum(upstream * normed, axis=0, keepdims=True)
        gsum[tile] = nt(ones, (rres[...] * normed).astype(bf16))

    gb2 = gg.at[0 : 4 * own, 0:width]
    sum2 = mid.at[0 : 4 * own, 0:width]

    def proj_grad(lhs, rhs, place_at):
        def run(j, carry):
            gb2[pl.ds(pl.multiple_of(place_at + j * own, row_tile), own), :] = nt(
                lhs[pl.ds(pl.multiple_of(j * own, row_tile), own), :], rhs[...]).astype(bf16)
            return carry

        lax.fori_loop(0, lhs.shape[0] // own, run, 0)

    two = RowSum(gb2, sum2, rb2, rbx2, ar_send.at[2], ar_recv.at[2], r, all_bits)
    two_tasks = two.tasks()

    dp_rows, all_rows = pl.ds(0, own), pl.ds(own, 80)

    def small_copy(chain, b):
        at = (dp_rows, all_rows)[chain]
        return pltpu.make_async_remote_copy(
            src_ref=sm.at[at], dst_ref=smbox.at[b, at], send_sem=sm_send.at[chain, b], recv_sem=sm_recv.at[chain, b],
            device_id={"dp": flipped(r, b)}, device_id_type=MESH,
        )

    def small_step(chain, b):
        at = (dp_rows, all_rows)[chain]
        small_copy(chain, b).wait()
        sm[at, :] += smbox[b, at, :]
        if b + 1 < all_bits:
            small_copy(chain, b + 1).start()

    def near(summer, k, index):
        summer.near(k, by_end(index) if summer is e_sum else plain_order[index])

    def far(summer, k, index):
        summer.far(k, by_end(index) if summer is e_sum else plain_order[index])

    total = rres.at[0:own, :]

    def output_part(tile):
        at = token(tile)
        total[...] = mbuf[span, at].astype(f32)
        for way in (0, 1):
            e_sum.take(way, tile, total)
        resown[:, at] = (resown[:, at] + total[...]) * masks[2:3, at]

    def input_part(tile):
        at = token(tile)
        total[...] = tbuf[span, at].astype(f32)
        for way in (0, 1):
            h_sum.take(way, tile, total)
        sums = sum(mom[s, :, at] for s in range(ways)) * (1.0 / width)
        inverse = stat1[1:2, at]
        normed = (xf[span, at].astype(f32) - stat1[0:1, at]) * inverse
        upstream = total[...] * gaincol[span, 0:1]
        sgr[:, at] = pgo[:, at].astype(f32) + inverse * (upstream - sums[0:1, :] - normed * sums[1:2, :])
        save(sgr.at[:, at], igrad_hbm.at[:, at])

    def in_turn(tile, carry):
        in_back(tile)
        return carry

    lax.fori_loop(0, ways, in_turn, 0)
    big_step(0)
    for index in every:
        h_sum.note_first(0, plain_order[index])
    mom_msg.start()
    swap_proj.wait_recv()
    proj_grad(sig, n1o, 0)
    proj_grad(pgo, mixf, 3 * own)
    two_tasks.pop(0)()
    for index in every:
        h_sum.first(1, plain_order[index])
    for index in first_two:
        far(e_sum, 0, index)
    for k in range(ways - 2):
        near(e_sum, k, 2)

    wave_grad = tn(cols[:, 64:128], kgr[...], highest) * jnp.cos(arg[...])
    finish_sums()
    two_tasks.pop(0)()
    for index in every:
        near(h_sum, 0, index)
    sm[0:own, 64:128] = nt(kgr[...], jnp.sin(arg[...]), highest)
    sm[own : own + 64, 0:64] = nt(feat_ref[...], wave_grad, highest)
    sm[own : own + 64, 64:128] = jnp.zeros((64, 64), f32)
    sm[own + 64 :, :] = jnp.zeros((16, 128), f32)
    for b in range(width // 128):
        lanes = slice(128 * b, 128 * b + 128)
        sm[own + 64 + b : own + 65 + b, :] = sum(gsum[tile, 0:1, lanes] for tile in range(ways))
        sm[own + 72 + b : own + 73 + b, :] = gsum[ways, 0:1, lanes]
    small_copy(0, 0).start()
    z_msg = Direct(lambda to: zbox.at[z], lambda at: zbox.at[at], z_send, z_recv)
    zbox[z] = sm[own:, :]
    z_msg.start()
    two_tasks.pop(0)()
    big_step(0)
    big_step(1)
    small_step(0, 0)
    for k in range(ways - 2):
        e_sum.first(k, by_end(3))
    two_tasks.pop(0)()
    for index in every:
        h_sum.first(2, plain_order[index])
    for index in every:
        e_sum.first(ways - 2, by_end(index))
    two_tasks.pop(0)()
    for index in every:
        near(h_sum, 1, index)
    for index in every:
        far(h_sum, 0, index)
    for k in range(ways - 2):
        near(e_sum, k, 3)
    small_step(0, 1)
    z_msg.wait_recv()
    zsum = zbox[0]
    for other in range(1, ways):
        zsum = zsum + zbox[other]
    sm[own:, :] = zsum
    small_copy(1, 0).start()
    small_step(1, 0)
    far(e_sum, 0, 2)
    two_tasks.pop(0)()
    for b in range(2, all_bits):
        small_step(0, b)
    far(e_sum, 0, 3)
    big_step(1)
    small_step(1, 1)
    big_step(0)
    two_tasks.pop(0)()
    save(sum2, proj_hbm)
    for b in range(2, all_bits):
        small_step(1, b)
    save(sm, small_hbm)
    big_step(1)
    big_step(0)
    save(weights, big_hbm)
    mom_msg.wait_recv()
    input_part(0)
    input_part(1)
    input_part(2)
    input_part(3)
    def output_turn(tile, carry):
        output_part(tile)
        return carry

    lax.fori_loop(0, ways, output_turn, 0)
    save(resown, out_hbm)

    for line in (in_line, g_line, mix_line, e_sum, h_sum, gain_msg, piece_msg, swap_mix, swap_proj, mom_msg, z_msg, big_parts[0], big_parts[1], two):
        line.drain()
    for make, piece in piece_sends:
        make(piece).wait_send()
    for copy in saves:
        copy.wait()


def layer(cfg, x_own, g_own, out_t, in_t, table, w_gate, w_up, w_down, halves, gain1, gain2, short_taps, cond_taps, rates,
          filter_in, filter_bias, filter_out, feats):
    ways, seq, own, width, hidden, bits, all_bits = cfg
    period = 3 * seq // 2
    block = seq // ways
    big_rows = hidden + 2 * width
    assert hidden == width
    held = dict(
        xf=((width, seq), bf16), gf=((width, seq), bf16), outt=((width, width), bf16), proj=((3 * own, seq), f32),
        mixf=((width, seq), bf16), query=((own, seq), f32), kv=((2 * own, seq), f32), squash=((own, seq), f32), kern=((own, seq), f32),
        mixed=((own, seq), f32), hat=((3 * own, period), bf16), arg=((64, seq), f32), in_t=((3 * own, width), bf16),
        tab=((seq, period), bf16), n1o=((width, seq), bf16), masks=((8, seq), f32), cols=((own, 128), f32),
        prow=((128, 256), f32), frow=((64, 64), f32),
        pieces=((1 << bits, ways, own * width // 128 // (1 << bits), 128), bf16), gains=((ways, 8, 256), f32),
        gaincol=((width, 128), f32), stat1=((8, seq), f32), sig=((3 * own, seq), bf16), prod=((3 * own, period), bf16),
        weights=((big_rows, width), bf16), n2o=((width, seq), bf16),
        mid=((hidden, seq), bf16), gg=((hidden, seq), bf16), ug=((hidden, seq), bf16), tbuf=((width, seq), bf16),
        tin=((2, ways - 1, width, block), bf16), mbuf=((width, seq), bf16), ein=((2, ways - 1, own, seq), bf16),
        gb=((big_rows, width), bf16), rb=((big_rows * 7 // 8, width), bf16),
        rbx=((max(all_bits - 3, 1), big_rows // 8 if all_bits > 3 else 32, width), bf16),
        rb2=((4 * own * 7 // 8, width), bf16),
        rbx2=((max(all_bits - 3, 1), 4 * own // 8 if all_bits > 3 else 16, width), bf16),
        n2own=((width, block), f32), inv2=((8, block), f32), rres=((width, block), f32), resown=((own, seq), f32),
        pgb=((width, block), bf16), mgb=((width, block), bf16), mgf=((own, seq), bf16), pgo=((own, seq), bf16),
        sgr=((own, seq), f32), kgr=((own, seq), f32), sm=((own + 80, 128), f32),
        smbox=((all_bits, own + 80, 128), f32), zbox=((ways, 80, 128), f32),
        mom=((ways, 8, seq), f32), gsum=((ways + 1, 8, width), f32),
    )
    hops = (3, 2, ways - 1, ways)
    sems = dict(
        load_sem=(11,), line_send=hops, line_recv=hops, piece_send=(ways + (1 << bits),), piece_recv=(ways + (1 << bits),),
        gain_send=(ways,), gain_recv=(ways,), save_sem=(8,), fs_send=(2, ways - 1, 2), fs_recv=(2, ways - 1, 2),
        es_send=(2, ways - 1, ways), es_recv=(2, ways - 1, ways), hs_send=(2, ways - 1, ways), hs_recv=(2, ways - 1, ways),
        sw_send=(2, ways), sw_recv=(2, ways), pace_sem=None, ar_send=(3, 3 + max(all_bits, 3)), ar_recv=(3, 3 + max(all_bits, 3)),
        sm_send=(2, all_bits), sm_recv=(2, all_bits), z_send=(ways,), z_recv=(ways,), mom_send=(ways,), mom_recv=(ways,),
    )
    here = pl.BlockSpec(memory_space=pltpu.VMEM)
    there = pl.BlockSpec(memory_space=pl.ANY)
    outs = [
        ((own, seq), f32), ((own, seq), f32), ((big_rows, width), bf16), ((4 * own, width), bf16),
        ((own + 80, 128), f32),
    ]
    return pl.pallas_call(
        functools.partial(layer_kernel, cfg),
        out_shape=[jax.ShapeDtypeStruct(s, t) for s, t in outs],
        in_specs=[there] * 8 + [pl.BlockSpec(memory_space=pltpu.SMEM)] + [here] * 9,
        out_specs=[there] * len(outs),
        scratch_shapes=[pltpu.VMEM(s, t) for s, t in held.values()] + [
            pltpu.SemaphoreType.REGULAR if s is None else pltpu.SemaphoreType.DMA(s) for s in sems.values()],
        compiler_params=pltpu.CompilerParams(collective_id=0, has_side_effects=True, vmem_limit_bytes=64 << 20),
    )(x_own, g_own, out_t, in_t, table, w_gate, w_up, w_down, halves, gain1, gain2, short_taps, cond_taps, rates,
      filter_in, filter_bias, filter_out, feats)


def widen_kernel(
    cfg, count, out_in, igrad_in, big_in, two_in, small_ref,
    out_hbm, igrad_hbm, wd_hbm, wg_hbm, wu_hbm, in_hbm, outp_hbm, gain1_ref, gain2_ref, short_ref, cond_ref, rate_ref,
    fin_ref, fbias_ref, fout_ref, low, wide, through, in_sem, out_sem, copy_sem,
):
    ways, seq, own, width, hidden, bits, all_bits = cfg
    step = own
    sources = [(big_in, at) for at in range(0, hidden + 2 * width, step)] + [(two_in, at) for at in range(0, 4 * own, step)]
    targets = [
        (ref, at) for ref, size in ((wd_hbm, hidden), (wg_hbm, width), (wu_hbm, width), (in_hbm, 3 * own), (outp_hbm, own))
        for at in range(0, size, step)]
    loads = [
        pltpu.make_async_copy(src.at[pl.ds(at, step)], low.at[i], in_sem.at[i]) for i, (src, at) in enumerate(sources)]
    for copy in loads:
        copy.start()
    ins = [pltpu.make_async_copy(src, through.at[i], copy_sem.at[i]) for i, src in enumerate((out_in, igrad_in))]
    for copy in ins:
        copy.start()
    moves = []
    stats = small_ref[0:own, :].T
    for i in range(3):
        for j in range(3):
            short_ref[i, j : j + 1, :] = stats[3 * i + j : 3 * i + j + 1, :]
    cond_ref[...] = stats[9:12, :]
    rate_ref[...] = stats[12:13, :]
    fout_ref[...] = stats[64:128, :]
    fin_ref[...] = small_ref[own : own + count, 0:64]
    fbias_ref[...] = small_ref[own + count : own + count + 1, 0:64]
    shift = (width - own * lax.axis_index("chan")) % width
    for first, ref in ((64, gain1_ref), (72, gain2_ref)):
        row = jnp.concatenate([small_ref[own + first + b : own + first + b + 1, :] for b in range(width // 128)], axis=1)
        ref[...] = pltpu.roll(jnp.broadcast_to(row, (8, width)), shift, 1)[0:1, 0:own]
    for i, ref in enumerate((out_hbm, igrad_hbm)):
        ins[i].wait()
        copy = pltpu.make_async_copy(through.at[i], ref, copy_sem.at[2 + i])
        copy.start()
        moves.append(copy)
    for i, (ref, at) in enumerate(targets):
        loads[i].wait()
        wide[i] = low[i].astype(f32)
        copy = pltpu.make_async_copy(wide.at[i], ref.at[pl.ds(at, step)], out_sem.at[i])
        copy.start()
        moves.append(copy)
    for copy in moves:
        copy.wait()


def widen(cfg, count, output, input_grad, big, two, small):
    ways, seq, own, width, hidden, bits, all_bits = cfg
    here = pl.BlockSpec(memory_space=pltpu.VMEM)
    there = pl.BlockSpec(memory_space=pl.ANY)
    far = [(own, seq), (own, seq), (hidden, width), (width, hidden), (width, hidden), (3 * own, width), (own, width)]
    near = [(1, own), (1, own), (3, 3, own), (3, own), (1, own), (count, 64), (1, 64), (64, own)]
    steps = (hidden + 2 * width + 4 * own) // own
    dma = pltpu.SemaphoreType.DMA
    return pl.pallas_call(
        functools.partial(widen_kernel, cfg, count),
        out_shape=[jax.ShapeDtypeStruct(shape, f32) for shape in far + near],
        in_specs=[there] * 4 + [here],
        out_specs=[there] * len(far) + [here] * len(near),
        scratch_shapes=[
            pltpu.VMEM((steps, own, width), bf16), pltpu.VMEM((steps, own, width), f32),
            pltpu.VMEM((2, own, seq), f32), dma((steps,)), dma((steps,)), dma((4,))],
        compiler_params=pltpu.CompilerParams(vmem_limit_bytes=64 << 20),
    )(output, input_grad, big, two, small)


def local(
    hidden_in, halves, norm1_gain, in_proj, short_taps, cond_taps, filter_in, filter_bias,
    filter_out, decay_rate, out_proj, norm2_gain, w_gate, w_up, w_down, out_grad,
):
    seq, own = hidden_in.shape[1], hidden_in.shape[2]
    ways, rows = lax.axis_size("chan"), lax.axis_size("dp")
    width, hidden = own * ways, w_gate.shape[1]
    z = lax.axis_index("chan")
    all_bits = rows.bit_length() - 1
    cfg = (ways, seq, own, width, hidden, 3, all_bits)
    count = filter_in.shape[0]
    feat_np = np.concatenate([
        band_features(seq, count), np.ones((1, seq), np.float32), np.zeros((63 - count, seq), np.float32)])
    table = jnp.asarray(wave_matrix(seq).astype(np.float32)).astype(bf16)

    output, input_grad, big, two, small = layer(
        cfg, hidden_in[0].T, out_grad[0].T, out_proj.T, in_proj.transpose(1, 2, 0).reshape(3 * own, width), table,
        w_gate, w_up, w_down, halves, norm1_gain[None], norm2_gain[None], short_taps, cond_taps, decay_rate[None],
        filter_in, filter_bias[None], filter_out, jnp.asarray(feat_np))

    (output, input_grad, wd_sum, wg_sum, wu_sum, in_sum, out_sum, gain1, gain2, short, cond, rates, fin, fbias, fout) = widen(
        cfg, count, output, input_grad, big, two, small)
    return (
        output.T[None], input_grad.T[None], gain1[0], in_sum.reshape(3, own, width).transpose(2, 0, 1), short, cond, fin,
        fbias[0], fout, rates[0], out_sum.T, gain2[0], wg_sum, wu_sum, wd_sum,
    )


def solution(mesh):
    rows, cols = P("dp", None, "chan"), P(None, "chan")
    in_specs = (
        rows, P("dp", None), P("chan"), P(None, None, "chan"), P(None, None, "chan"), cols, P(), P(),
        cols, P("chan"), cols, P("chan"), cols, cols, P("chan", None), rows,
    )
    out_specs = (
        rows, rows, P("chan"), P(None, None, "chan"), P(None, None, "chan"), cols, P(), P(),
        cols, P("chan"), cols, P("chan"), cols, cols, P("chan", None),
    )
    return jax.shard_map(local, mesh=mesh, in_specs=in_specs, out_specs=out_specs, check_vma=False)
```

```python
import functools
import math

import jax
import jax.numpy as jnp
import numpy as np
from jax import lax
from jax.experimental import pallas as pl
from jax.experimental.pallas import tpu as pltpu
from jax.sharding import PartitionSpec as P

highest = lax.Precision.HIGHEST
norm_eps = 1e-05
f32 = jnp.float32
bf16 = jnp.bfloat16


def band_features(seq_len, feat_count):
    bands = (feat_count - 1) // 2
    positions = np.arange(seq_len)
    orders = np.arange(1, bands + 1)
    phases = (orders[:, None] * positions[None, :] % seq_len) * (2.0 * math.pi / seq_len)
    ramp = positions[None, :] / seq_len
    return np.concatenate([ramp, np.sin(phases), np.cos(phases)], axis=0).astype(np.float32)


def wave_matrix(seq_len):
    period = 3 * seq_len // 2
    freq = period // 2
    phase = (np.arange(seq_len)[:, None] * (2 * np.arange(freq)[None, :] + 1)) % (2 * period)
    angle = phase * (math.pi / period)
    return np.concatenate([np.cos(angle), np.sin(angle)], axis=1)


def nn(a, b, precision=None):
    return lax.dot_general(a, b, (((1,), (0,)), ((), ())), precision=precision, preferred_element_type=f32)


def nt(a, b, precision=None):
    return lax.dot_general(a, b, (((1,), (1,)), ((), ())), precision=precision, preferred_element_type=f32)


def tn(a, b, precision=None):
    return lax.dot_general(a, b, (((0,), (0,)), ((), ())), precision=precision, preferred_element_type=f32)


MESH = pl.DeviceIdType.MESH
lane_tile = 256
row_tile = 16


def flipped(index, bit):
    return index + (1 << bit) * (1 - 2 * ((index // (1 << bit)) % 2))


def both(first, second):
    if second is True:
        return first
    return second if first is True else jnp.logical_and(first, second)


class Line:
    def __init__(self, view, send_sem, recv_sem, at, ways):
        self.view, self.send_sem, self.recv_sem, self.at, self.ways = view, send_sem, recv_sem, at, ways
        self.pending, self.arrived = {}, set()

    def copy(self, way, hop, part, shard):
        ref = self.view(shard, part)
        step = 1 - 2 * way
        return pltpu.make_async_remote_copy(
            src_ref=ref, dst_ref=ref, send_sem=self.send_sem.at[way, hop, part],
            recv_sem=self.recv_sem.at[way, hop, part],
            device_id={"chan": (self.at + step + self.ways) % self.ways}, device_id_type=MESH,
        )

    def sends(self, way, hop):
        if way == 0:
            return jnp.logical_and(self.at >= hop, self.at < self.ways - 1)
        return jnp.logical_and(self.at + hop <= self.ways - 1, self.at > 0)

    def gets(self, way, hop):
        if way == 0:
            return self.at >= hop + 1
        return self.at + hop + 1 <= self.ways - 1

    def order(self, way, index):
        return index if way == 0 else self.ways - 1 - index

    def far_side(self):
        return (2 * self.at) // self.ways

    def launch(self, hop, way, index, wanted, wait_first):
        part, step = self.order(way, index), 1 - 2 * way

        @pl.when(both(self.sends(way, hop), wanted()))
        def _():
            if wait_first:
                self.copy(way, hop - 1, part, self.at - hop * step).wait_recv()
            self.copy(way, hop, part, self.at - hop * step).start()

        def left(also):
            @pl.when(both(both(self.sends(way, hop), wanted()), also))
            def _():
                self.copy(way, hop, part, self.at - hop * step).wait_send()

        self.pending.setdefault((hop, way, index), []).append(left)

    def settle(self, hops, indices, wanted=True):
        for key in [k for k in self.pending if k[0] in hops and k[2] in indices]:
            before = self.pending.pop(key)
            for left in before:
                left(wanted)
            if wanted is not True:
                self.pending[key] = [
                    lambda also, left=left: left(both(jnp.logical_not(wanted), also)) for left in before]

    def send_own(self, indices, wanted, inward=None):
        for index in indices:
            for way in (0, 1):
                def ok(way=way):
                    if inward is None:
                        return wanted
                    facing = self.far_side() == way
                    return both(wanted, facing if inward else jnp.logical_not(facing))
                self.launch(0, way, index, ok, False)

    def relay(self, way, index, wanted, hops=None, wait_first=True):
        for hop in range(1, self.ways - 1) if hops is None else hops:
            self.launch(hop, way, index, wanted, wait_first)

    def short_way(self, index):
        for way in (0, 1):
            self.relay(way, index, lambda way=way: self.far_side() == way)

    def long_way(self, index, hops=None):
        for way in (0, 1):
            self.relay(way, index, lambda way=way: self.far_side() != way, hops, index not in self.arrived)

    def arrive(self, index):
        self.arrived.add(index)
        for way in (0, 1):
            for hop in range(1, self.ways - 1):
                @pl.when(jnp.logical_and(self.sends(way, hop), self.far_side() != way))
                def _():
                    self.copy(way, hop - 1, self.order(way, index), self.at - hop * (1 - 2 * way)).wait_recv()

    def take(self, index):
        for way in (0, 1):
            for hop in range(self.ways - 1):
                last = self.gets(way, hop)
                if hop + 1 < self.ways - 1:
                    last = jnp.logical_and(last, jnp.logical_not(self.sends(way, hop + 1)))

                @pl.when(last)
                def _():
                    self.copy(way, hop, self.order(way, index), self.at - (hop + 1) * (1 - 2 * way)).wait_recv()

    def drain(self):
        self.settle(range(self.ways), range(self.ways))


class LineSum:
    def __init__(self, mine, inbox, send_sem, recv_sem, at, ways, subs):
        self.mine, self.inbox, self.send_sem, self.recv_sem = mine, inbox, send_sem, recv_sem
        self.at, self.ways, self.subs = at, ways, subs
        self.pending = {}

    def dest(self, way, k):
        return self.ways - 1 - k if way == 0 else k

    def sends(self, way, k):
        return self.dest(way, k) > self.at if way == 0 else self.dest(way, k) < self.at

    def gets(self, way, k):
        dest = self.dest(way, k)
        if way == 0:
            return jnp.logical_and(dest >= self.at, self.at > 0)
        return jnp.logical_and(dest <= self.at, self.at < self.ways - 1)

    def copy(self, way, k, sub):
        step = 1 - 2 * way
        return pltpu.make_async_remote_copy(
            src_ref=self.mine(self.dest(way, k), sub), dst_ref=self.inbox(way, k, sub),
            send_sem=self.send_sem.at[way, k, sub], recv_sem=self.recv_sem.at[way, k, sub],
            device_id={"chan": (self.at + step + self.ways) % self.ways}, device_id_type=MESH,
        )

    def first(self, k, sub, noted=True):
        for way in (0, 1):
            def starts(way=way):
                return jnp.logical_and(self.sends(way, k), jnp.logical_not(self.gets(way, k)))

            @pl.when(starts())
            def _():
                self.copy(way, k, sub[way]).start()
            if noted:
                self.note(way, k, sub[way], starts)

    def note_first(self, k, sub):
        for way in (0, 1):
            self.note(way, k, sub[way], lambda way=way: jnp.logical_and(
                self.sends(way, k), jnp.logical_not(self.gets(way, k))))

    def note(self, way, k, sub, going):
        def left(also):
            @pl.when(both(going(), also))
            def _():
                self.copy(way, k, sub).wait_send()
        self.pending.setdefault(k, []).append(left)

    def settle(self, k, wanted=True):
        before = self.pending.pop(k, [])
        for left in before:
            left(wanted)
        if wanted is not True:
            self.pending[k] = [
                lambda also, left=left: left(both(jnp.logical_not(wanted), also)) for left in before]

    def onward(self, way, k, sub, wanted):
        def going():
            return both(jnp.logical_and(self.sends(way, k), self.gets(way, k)), wanted())

        self.note(way, k, sub, going)

        @pl.when(going())
        def _():
            self.copy(way, k, sub).wait_recv()
            mine, inbox = self.mine(self.dest(way, k), sub), self.inbox(way, k, sub)
            mine[...] = (mine[...].astype(f32) + inbox[...].astype(f32)).astype(bf16)
            self.copy(way, k, sub).start()

    def near(self, k, sub):
        for way in (0, 1):
            self.onward(way, k, sub[way], lambda way=way: (2 * self.at) // self.ways == way)

    def far(self, k, sub):
        for way in (0, 1):
            self.onward(way, k, sub[way], lambda way=way: (2 * self.at) // self.ways != way)

    def take(self, way, sub, total):
        k = self.ways - 1 - self.at if way == 0 else self.at

        @pl.when(self.at > 0 if way == 0 else self.at < self.ways - 1)
        def _():
            self.copy(way, k, sub).wait_recv()
            total[...] += self.inbox(way, k, sub)[...].astype(f32)

    def drain(self):
        for k in list(self.pending):
            self.settle(k)


class RowSum:
    tile = 48

    def __init__(self, buf, result, box, extra_box, send_sem, recv_sem, r, total_bits):
        self.buf, self.result, self.box, self.extra_box = buf, result, box, extra_box
        self.send_sem, self.recv_sem = send_sem, recv_sem
        self.total_bits, self.r = total_bits, r
        height = buf.shape[0]
        core = r % 2
        steps = [1, 2 + 2 * core, 4 - 2 * core]
        self.levels = []
        base, size = 0, height
        inbox_at = 0
        for step in steps:
            size = size // 2
            bit = (r // step) % 2
            keep, give = base + bit * size, base + (1 - bit) * size
            self.levels.append((r + step * (1 - 2 * bit), keep, give, size, inbox_at))
            base = keep
            inbox_at += size

    def rows(self, at, size, buf=None):
        return (self.buf if buf is None else buf).at[pl.ds(pl.multiple_of(at, 16), size)]

    def halve(self, level):
        partner, keep, give, size, inbox_at = self.levels[level]
        return pltpu.make_async_remote_copy(
            src_ref=self.rows(give, size), dst_ref=self.box.at[pl.ds(inbox_at, size)],
            send_sem=self.send_sem.at[level], recv_sem=self.recv_sem.at[level],
            device_id={"dp": partner}, device_id_type=MESH,
        )

    def double(self, level, arriving=False):
        partner, keep, give, size, inbox_at = self.levels[level]
        part = self.rows(give if arriving else keep, size, self.result)
        return pltpu.make_async_remote_copy(
            src_ref=part, dst_ref=part, send_sem=self.send_sem.at[3 + level], recv_sem=self.recv_sem.at[3 + level],
            device_id={"dp": partner}, device_id_type=MESH,
        )

    def add(self, level, target=None):
        partner, keep, give, size, inbox_at = self.levels[level]
        target = self.buf if target is None else target
        self.halve(level).wait_recv()

        def run(i, carry):
            at = pl.ds(pl.multiple_of(keep + i * self.tile, 16), self.tile)
            there = pl.ds(pl.multiple_of(inbox_at + i * self.tile, 16), self.tile)
            target[at, :] = (self.buf[at, :].astype(f32) + self.box[there, :].astype(f32)).astype(bf16)
            return carry

        lax.fori_loop(0, size // self.tile, run, 0)

    def extra(self):
        partner, keep, give, size, inbox_at = self.levels[2]
        for bit in range(3, self.total_bits):
            copy = pltpu.make_async_remote_copy(
                src_ref=self.rows(keep, size, self.result), dst_ref=self.extra_box.at[bit - 3], send_sem=self.send_sem.at[3 + bit],
                recv_sem=self.recv_sem.at[3 + bit], device_id={"dp": flipped(self.r, bit)}, device_id_type=MESH,
            )
            copy.start()
            copy.wait()
            at = pl.ds(pl.multiple_of(keep, 16), size)
            self.result[at, :] = (self.result[at, :].astype(f32) + self.extra_box[bit - 3].astype(f32)).astype(bf16)

    def tasks(self):
        def second():
            self.add(0)
            self.halve(1).start()

        def third():
            self.add(1)
            self.halve(2).start()

        def turn():
            self.add(2, self.result)
            self.extra()
            self.double(2).start()

        def wider():
            self.double(2, True).wait_recv()
            self.double(1).start()

        def widest():
            self.double(1, True).wait_recv()
            self.double(0).start()

        def last():
            self.double(0, True).wait_recv()

        return [self.halve(0).start, second, third, turn, wider, widest, last]

    def drain(self):
        for level in range(3):
            self.halve(level).wait_send()
            self.double(level).wait_send()


def layer_kernel(
    cfg,
    x_hbm, g_hbm, outp_hbm, in_hbm, tab_hbm, wg_hbm, wu_hbm, wd_hbm, halves_ref, gain1_ref, gain2_ref, short_ref, cond_ref,
    rate_ref, fin_ref, fbias_ref, fout_ref, feat_ref,
    out_hbm, igrad_hbm, big_hbm, proj_hbm, small_hbm, *scratch,
):
    ways, seq, own, width, hidden, bits, all_bits = cfg
    (
        xf, gf, outt, proj, mixf, query, kv, squash, kern, mixed, hat, arg, in_t, tab, n1o, masks, cols, prow, frow,
        pieces, gains, gaincol, stat1, sig, prod, weights, n2o, mid, gg, ug, tbuf, tin, mbuf, ein,
        gb, rb, rbx, rb2, rbx2, n2own, inv2, rres, resown, pgb, mgb, mgf, pgo, sgr, kgr, sm, smbox, zbox, mom, gsum,
        load_sem, line_send, line_recv, piece_send, piece_recv, gain_send, gain_recv, save_sem,
        fs_send, fs_recv, es_send, es_recv, hs_send, hs_recv, sw_send, sw_recv,
        pace_sem, ar_send, ar_recv, sm_send, sm_recv, z_send, z_recv, mom_send, mom_recv,
    ) = scratch
    lags = 3 * seq // 4
    freq = lags
    block = seq // ways
    z = lax.axis_index("chan")
    r = lax.axis_index("dp")
    side = (2 * z) // ways
    inner = ((z + ways - 1) // ways) * ((2 * ways - 2 - z) // ways)
    group = r % (1 << bits)

    wd, wg, wu = (weights.at[pl.ds(at, size)] for at, size in ((0, hidden), (hidden, width), (hidden + width, width)))

    def own_rows(at):
        return pl.ds(pl.multiple_of(at * own, row_tile), own)

    def token(at):
        return pl.ds(pl.multiple_of(at * block, block), block)

    span = own_rows(z)
    saves = []

    def load(index, src, dst):
        copy = pltpu.make_async_copy(src, dst, load_sem.at[index])
        copy.start()
        return copy

    def save(src, dst):
        copy = pltpu.make_async_copy(src, dst, save_sem.at[len(saves)])
        copy.start()
        saves.append(copy)

    grain = 48
    per_piece = pieces.shape[2] // grain
    x_load = load(0, x_hbm, xf.at[span])
    g_load = load(1, g_hbm, gf.at[span])
    in_load = load(2, in_hbm, in_t)

    def piece_from(i):
        at = group * per_piece + i
        return outp_hbm.at[
            pl.ds(pl.multiple_of((at % (own // grain)) * grain, row_tile), grain),
            pl.ds(pl.multiple_of((at // (own // grain)) * 128, 128), 128)]

    piece_loads = [load(8 + i, piece_from(i), pieces.at[group, z, pl.ds(i * grain, grain)]) for i in range(per_piece)]
    tab_load = load(3, tab_hbm, tab)
    weight_loads = [load(4, wg_hbm, wg), load(5, wu_hbm, wu), load(6, wd_hbm, wd)]
    barrier = pltpu.get_barrier_semaphore()
    peers = [{"chan": (z + s) % ways} for s in range(1, ways)] + [{"dp": flipped(r, b)} for b in range(all_bits)]
    for peer in peers:
        pl.semaphore_signal(barrier, inc=1, device_id=peer, device_id_type=MESH)
    pl.semaphore_wait(barrier, len(peers))

    def cut(buf):
        return lambda shard, part: buf.at[own_rows(shard), token(part)]

    in_line, g_line, mix_line = (
        Line(cut(buf), line_send.at[i], line_recv.at[i], z, ways) for i, buf in enumerate((xf, gf, mixf)))

    class Direct:
        def __init__(self, view_src, view_dst, send, recv):
            self.view_src, self.view_dst, self.send, self.recv = view_src, view_dst, send, recv

        def copy(self, s, arriving):
            there = (z + s) % ways
            src = (z + ways - s) % ways
            dst = self.view_dst(src if arriving else z)
            return pltpu.make_async_remote_copy(
                src_ref=dst if arriving else self.view_src(there), dst_ref=dst, send_sem=self.send.at[s],
                recv_sem=self.recv.at[s], device_id={"chan": there}, device_id_type=MESH,
            )

        def start(self, wanted=None):
            for s in range(1, ways):
                if wanted is None:
                    self.copy(s, False).start()
                else:
                    @pl.when(wanted((z + s) % ways))
                    def _():
                        self.copy(s, False).start()

        def wait_recv(self):
            for s in range(1, ways):
                self.copy(s, True).wait_recv()

        def drain(self):
            for s in range(1, ways):
                self.copy(s, False).wait_send()

    gain_msg = Direct(lambda to: gains.at[z], lambda at: gains.at[at], gain_send, gain_recv)
    piece_msg = Direct(lambda to: pieces.at[group, z], lambda at: pieces.at[group, at], piece_send, piece_recv)

    gains[z] = jnp.zeros(gains.shape[1:], f32)
    gains[z, 0:1, 0:own] = gain1_ref[...]
    gains[z, 1:2, 0:own] = gain2_ref[...]
    gain_msg.start()
    x_load.wait()
    every, outer, middle = range(ways), inner == 0, inner == 1
    first_two, last_two = range(ways // 2), range(ways // 2, ways)
    next_hops, last_hops = range(1, 2), range(2, ways - 1)
    in_line.send_own(first_two, True)
    in_line.send_own(last_two, middle)

    def inside(at):
        return jnp.logical_and(at > 0, at < ways - 1)

    def early(there):
        return jnp.logical_or(inside(there), inner == 0)

    for copy in piece_loads:
        copy.wait()
    piece_msg.start(early)

    def clear(j, carry):
        gb[pl.ds(pl.multiple_of(j * 96, 96), 96), :] = jnp.zeros((96, width), bf16)
        return carry

    lax.fori_loop(0, gb.shape[0] // 96, clear, 0)

    line_at = lax.broadcasted_iota(jnp.int32, (1, seq), 1)
    split, valid = halves_ref[0, 0], halves_ref[0, 1]
    masks[0:1, :] = jnp.where(line_at < split, 1.0, 0.0)
    masks[1:2, :] = jnp.where(jnp.logical_and(line_at >= split, line_at < valid), 1.0, 0.0)
    masks[2:3, :] = masks[0:1, :] + masks[1:2, :]
    prow[...] = jnp.zeros(prow.shape, f32)
    for i in range(3):
        for j in range(3):
            prow[3 * i + j : 3 * i + j + 1, 0:own] = short_ref[i, j : j + 1, :]
    prow[9:12, 0:own] = cond_ref[...]
    prow[12:13, 0:own] = rate_ref[...]
    prow[64:128, 0:own] = fout_ref[...]
    cols[...] = prow[...].T[0:own, :]
    frow[...] = jnp.zeros(frow.shape, f32)
    frow[0 : fin_ref.shape[0], :] = fin_ref[...]
    frow[fin_ref.shape[0] : fin_ref.shape[0] + 1, :] = fbias_ref[...]
    g_load.wait()
    gf[span, :] = (gf[span, :].astype(f32) * masks[2:3, :]).astype(bf16)

    arg[...] = tn(frow[...], feat_ref[...], highest)
    kern[...] = nn(cols[:, 64:128], jnp.sin(arg[...]), highest)

    in_line.settle([0], first_two)
    in_line.send_own(last_two, outer)
    gain_msg.wait_recv()
    eye = lax.broadcasted_iota(jnp.int32, (own, gains.shape[2]), 0) == lax.broadcasted_iota(
        jnp.int32, (own, gains.shape[2]), 1)
    for s in range(ways):
        for which in range(2):
            row = gains[s, which : which + 1, :]
            gaincol[s * own : (s + 1) * own, which : which + 1] = jnp.sum(jnp.where(eye, row, 0.0), axis=1, keepdims=True)
    in_load.wait()

    def moments(values):
        centre = jnp.sum(values, axis=0, keepdims=True) * (1.0 / width)
        spread = jnp.sum(values * values, axis=0, keepdims=True) * (1.0 / width) - centre * centre
        return centre, lax.rsqrt(spread + norm_eps)

    def in_order(index):
        return side * index + (1 - side) * (ways - 1 - index)

    def norm1(q):
        at = token(q)
        values = xf[:, at].astype(f32)
        centre, inverse = moments(values)
        stat1[0:1, at] = centre
        stat1[1:2, at] = inverse
        low = ((values - centre) * inverse * gaincol[:, 0:1]).astype(bf16)
        n1o[:, at] = low
        proj[:, at] = nn(in_t[...], low)

    for index in first_two:
        in_line.short_way(index)
    for index in every:
        in_line.long_way(index, next_hops)
    for index in last_two:
        in_line.short_way(index)
    in_line.settle([0], last_two)
    g_line.send_own(every, outer)
    for index in first_two:
        in_line.long_way(index, last_hops)
    g_line.send_own(every, middle, inward=True)
    for index in last_two:
        in_line.long_way(index, last_hops)

    def norm_turn(index, carry):
        in_line.take(index)
        norm1(in_order(index))
        return carry

    lax.fori_loop(0, ways, norm_turn, 0)
    piece_msg.start(lambda there: jnp.logical_not(early(there)))
    for index in every:
        g_line.short_way(index)

    piece_sends = []

    def piece_step(bit, held, slot):
        batch = []
        for i, piece in enumerate(held):
            def make(which, slot=slot + i):
                return pltpu.make_async_remote_copy(
                    src_ref=pieces.at[which], dst_ref=pieces.at[which], send_sem=piece_send.at[slot],
                    recv_sem=piece_recv.at[slot], device_id={"dp": flipped(r, bit)}, device_id_type=MESH,
                )
            make(piece).start()
            batch.append((make, piece))
            piece_sends.append((make, piece))

        def finish():
            for make, piece in batch:
                make(flipped(piece, bit)).wait_recv()
        return finish, held + [flipped(piece, bit) for piece in held], slot + len(held)

    tab_load.wait()

    half1, half2 = masks[0:1, :], masks[1:2, :]

    def back(values, steps):
        if steps == 0:
            return values
        return jnp.where(lane2 >= steps, pltpu.roll(values, steps, 1), 0.0)

    def row_at(j, i):
        return pl.ds(pl.multiple_of(j * own + i * row_tile, row_tile), row_tile)

    tall = 2 * row_tile
    lane2 = lax.broadcasted_iota(jnp.int32, (tall, seq), 1)
    place2 = lane2.astype(f32)

    def mix_rows(i, carry):
        here, here1, here2 = (pl.ds(pl.multiple_of(j * own + i * tall, tall), tall) for j in range(3))
        tap = cols[here, :]
        outs = []
        for j in range(3):
            part = proj[(here, here1, here2)[j], :]
            outs.append(sum(tap[:, 3 * k + j : 3 * k + j + 1] * back(part, k) for k in range(3)))
        query[here, :] = outs[0]
        kv[here, :] = outs[1]
        kv[here1, :] = outs[2]
        cond = sum(tap[:, 9 + k : 10 + k] * back(outs[2], k) for k in range(3))
        bent = jnp.tanh(cond)
        squash[here, :] = bent
        filt = (kern[here, :] + bent) * (jnp.exp(-tap[:, 12:13] * place2) * (1.0 / math.sqrt(seq)))
        kern[here, :] = filt
        source = outs[1] * outs[2]
        sig[here, :] = jnp.where(lane2 < lags, filt, 0.0).astype(bf16)
        sig[here1, :] = (source * half1).astype(bf16)
        sig[here2, :] = (source * half2).astype(bf16)
        return carry

    lax.fori_loop(0, own // tall, mix_rows, 0)
    g_line.send_own(first_two, middle, inward=False)
    piece_msg.wait_recv()
    bit_list = list(reversed(range(bits)))
    finish, held, slot = piece_step(bit_list[0], [group], ways)

    def freq_at(j):
        return (pl.ds(pl.multiple_of(j * lane_tile, lane_tile), lane_tile),
                pl.ds(pl.multiple_of(freq + j * lane_tile, lane_tile), lane_tile))

    def freq_tile(j, carry):
        re_at, im_at = freq_at(j)
        re = nn(sig[...], tab[:, re_at])
        im = nn(sig[...], tab[:, im_at])
        hat[:, re_at] = re.astype(bf16)
        hat[:, im_at] = im.astype(bf16)
        kr, ki = re[:own], im[:own]
        for h in range(2):
            sr, si = re[own * (h + 1) : own * (h + 2)], im[own * (h + 1) : own * (h + 2)]
            prod[own * h : own * (h + 1), re_at] = (kr * sr - ki * si).astype(bf16)
            prod[own * h : own * (h + 1), im_at] = (kr * si + ki * sr).astype(bf16)
        return carry

    lax.fori_loop(0, freq // lane_tile, freq_tile, 0)

    def time_tile(j, carry):
        at = token(j)
        both = nt(prod[0 : 2 * own, :], tab[at, :])
        total = (both[:own] * masks[0:1, at] + both[own:] * masks[1:2, at]) * (1.0 / freq)
        mixed[:, at] = total
        mixf[span, at] = (query[:, at] * total).astype(bf16)
        return carry

    def time_turn(index, carry):
        time_tile(side * (ways - 1 - index) + (1 - side) * index, 0)
        for early_index in first_two:
            @pl.when(index == early_index)
            def _():
                mix_line.send_own([early_index], True, inward=True)
        return carry

    lax.fori_loop(0, ways, time_turn, 0)
    mix_line.send_own([0], middle, inward=False)
    finish()
    finish, held, slot = piece_step(bit_list[1], held, slot)
    for index in first_two:
        g_line.long_way(index)
    mix_line.settle([0], first_two, outer)
    mix_line.send_own(last_two, outer)
    finish()
    finish, held, slot = piece_step(bit_list[2], held, slot)
    finish()
    for s in range(ways):
        for block_at in range(own * width // 128 // grain):
            piece, inside_at = divmod(block_at, per_piece)
            column, down = divmod(block_at, own // grain)
            outt[s * own + down * grain : s * own + (down + 1) * grain, 128 * column : 128 * column + 128] = pieces[
                piece, s, inside_at * grain : (inside_at + 1) * grain, :]
    for copy in weight_loads:
        copy.wait()

    def pass_set(index):
        for line in (g_line, mix_line):
            line.long_way(index)

    mix_line.long_way(0, next_hops)
    for index in first_two:
        mix_line.short_way(index)
    mix_line.long_way(0, last_hops)
    mix_line.send_own(last_two, middle, inward=True)
    for index in last_two:
        mix_line.short_way(index)

    half_block = block // 2

    def half_token(at, sub):
        return pl.ds(pl.multiple_of(at * block + sub * half_block, half_block), half_block)

    f_sum = LineSum(
        lambda dest, sub: tbuf.at[:, half_token(dest, sub)],
        lambda way, k, sub: tin.at[way, k, :, pl.ds(sub * half_block, half_block)],
        fs_send, fs_recv, z, ways, 2)
    e_sum = LineSum(
        lambda dest, sub: mbuf.at[own_rows(dest), token(sub)],
        lambda way, k, sub: ein.at[way, k, :, token(sub)],
        es_send, es_recv, z, ways, ways)

    def by_end(index):
        return (ways - 1 - index, index)

    halves_of = [(sub, sub) for sub in range(2)]
    plain_order = [(sub, sub) for sub in range(ways)]

    def tiles(count, fn):
        def run(j, carry):
            fn(pl.ds(pl.multiple_of(j * lane_tile, lane_tile), lane_tile))
            return carry
        lax.fori_loop(0, count // lane_tile, run, 0)

    def forward(q):
        at = token(q)
        def resid_tile(ds):
            rres[ds, :] = xf[ds, at].astype(f32) + nn(outt[ds, :], mixf[:, at])

        tiles(width, resid_tile)
        resown[:, at] = rres[span, :]
        centre, inverse = moments(rres[...])
        n2o[:, at] = ((rres[...] - centre) * inverse * gaincol[:, 1:2]).astype(bf16)

        @pl.when(q == z)
        def _():
            n2own[...] = (rres[...] - centre) * inverse
            inv2[0:1, :] = inverse

        def hidden_tile(fs):
            low = n2o[:, at]
            gate = tn(wg[:, fs], low)
            up = tn(wu[:, fs], low)
            bent = jax.nn.sigmoid(gate)
            act = gate * bent
            mid[fs, at] = (act * up).astype(bf16)
            gg[fs, at] = (up * bent * (1.0 + gate * (1.0 - bent))).astype(bf16)
            ug[fs, at] = act.astype(bf16)

        tiles(hidden, hidden_tile)

    def down(q):
        at = token(q)

        def mlp_tile(ds):
            mbuf[ds, at] = tn(wd[:, ds], mid[:, at]).astype(bf16)

        tiles(width, mlp_tile)

    def backward(q):
        at = token(q)

        def back_tile(fs):
            grad = nn(wd[fs, :], gf[:, at])
            gg[fs, at] = (grad * gg[fs, at].astype(f32)).astype(bf16)
            ug[fs, at] = (grad * ug[fs, at].astype(f32)).astype(bf16)

        tiles(hidden, back_tile)

        def term_tile(ds):
            tbuf[ds, at] = (nn(wg[ds, :], gg[:, at]) + nn(wu[ds, :], ug[:, at])).astype(bf16)

        tiles(width, term_tile)

    def turn_tokens(index):
        late = index // (ways - 2)
        return in_order(index + inner * late * (1 - 2 * (index - (ways - 2))))

    def weight_grads(turn, carry):
        at = token(turn_tokens(turn))
        for lhs, rhs, place_at in ((mid, gf, 0), (n2o, gg, hidden), (n2o, ug, hidden + width)):
            def run(j, carry):
                rows_at = pl.ds(pl.multiple_of(j * lane_tile, lane_tile), lane_tile)
                to = pl.ds(pl.multiple_of(place_at + j * lane_tile, lane_tile), lane_tile)
                gb[to, :] = (nt(lhs[rows_at, at], rhs[:, at]) + gb[to, :].astype(f32)).astype(bf16)
                return carry
            lax.fori_loop(0, lhs.shape[0] // lane_tile, run, 0)
        return carry

    big_rows = hidden + 2 * width

    def feed_forward_turn(index, carry):
        def at_turn(which):
            return pl.when(index == which)

        q = turn_tokens(index)
        mix_line.take(index)

        @at_turn(2)
        def _():
            for k in range(ways - 1):
                e_sum.first(k, by_end(0))

        @at_turn(ways - 1)
        def _():
            for early_index in (1, 2):
                for k in range(ways - 2):
                    e_sum.first(k, by_end(early_index))

        forward(q)
        for which in every:
            @at_turn(which)
            def _():
                if which == 0:
                    mix_line.send_own([1], middle, inward=False)
                    mix_line.long_way(1)
                elif which + 1 < ways:
                    for line in (g_line, mix_line):
                        line.send_own([which + 1], middle, inward=False)
                    for line in (g_line, mix_line):
                        line.settle(range(ways - 1), range(which + 1))

                    @pl.when(jnp.logical_and(middle, r % 2 == 0))
                    def _():
                        pl.semaphore_signal(pace_sem, inc=1, device_id={"dp": flipped(r, 0)}, device_id_type=MESH)

                    @pl.when(jnp.logical_and(middle, r % 2 == 1))
                    def _():
                        pl.semaphore_wait(pace_sem, 1)

                    pass_set(which + 1)
                if which == ways - 3:
                    g_line.arrive(ways - 1)
                    mix_line.arrive(ways - 1)
                if which == ways - 2:
                    for sub in halves_of:
                        f_sum.near(0, sub)
        g_line.take(index)
        backward(q)
        for which in every:
            @at_turn(which)
            def _():
                if which < ways - 1:
                    for sub in halves_of:
                        f_sum.first(which, sub)
                if which == ways - 1:
                    for sub in halves_of:
                        f_sum.near(1, sub)
                    for sub in halves_of:
                        f_sum.far(0, sub)
        pl.when(index < ways - 1)(lambda: down(q))
        seen = (index + ways - 1) // ways
        behind = seen * (1 - (index + ways - 2) // ways)
        lax.fori_loop(index - behind * index, seen * (index + 1), weight_grads, 0)
        return carry

    lax.fori_loop(0, ways, feed_forward_turn, 0)

    first_rows = big_rows // 2
    big_parts = []
    for i, at in enumerate((0, first_rows)):
        def cut_rows(buf, at=at, size=first_rows):
            return buf.at[pl.ds(at, size)]
        big = RowSum(
            cut_rows(gb), cut_rows(weights), cut_rows(rb, at * 7 // 8, first_rows * 7 // 8),
            rbx.at[:, pl.ds(i * (rbx.shape[1] // 2), rbx.shape[1] // 2)], ar_send.at[i], ar_recv.at[i], r, all_bits)
        big.halve(0).start()
        big_parts.append(big)
    big_left = [[big.tasks()[1:] for big in big_parts] for _ in range(2)]

    def big_step(inside_line):
        steps = [left.pop(0) for left in big_left[inside_line]]

        @pl.when(inner == inside_line)
        def _():
            for step in steps:
                step()

    rres[...] = tbuf[:, token(z)].astype(f32)
    for sub in range(2):
        for way in (0, 1):
            f_sum.take(way, sub, rres.at[:, pl.ds(sub * half_block, half_block)])
    upstream = rres[...] * gaincol[:, 1:2]
    normed = n2own[...]
    plain = jnp.sum(upstream, axis=0, keepdims=True) * (1.0 / width)
    cross = jnp.sum(upstream * normed, axis=0, keepdims=True) * (1.0 / width)
    pgb[...] = (gf[:, token(z)].astype(f32) + inv2[0:1, :] * (upstream - plain - normed * cross)).astype(bf16)
    def mix_grad_tile(ds):
        mgb[ds, :] = tn(outt[:, ds], pgb[...]).astype(bf16)

    tiles(width, mix_grad_tile)
    swap_mix = Direct(lambda to: mgb.at[own_rows(to)], lambda at: mgf.at[:, token(at)], sw_send.at[0], sw_recv.at[0])
    swap_proj = Direct(lambda to: pgb.at[own_rows(to)], lambda at: pgo.at[:, token(at)], sw_send.at[1], sw_recv.at[1])
    swap_mix.start()
    down(turn_tokens(ways - 1))
    mgf[:, token(z)] = mgb[span, :]
    pgo[:, token(z)] = pgb[span, :]
    ones = jnp.ones((8, block), bf16)
    gsum[ways] = nt(ones, (rres[...] * normed).astype(bf16))

    big_step(0)
    big_step(1)
    swap_mix.wait_recv()
    swap_proj.start()
    for index in first_two:
        for k in range(ways - 2):
            e_sum.near(k, by_end(index))

    def grad_rows(i, carry):
        here = row_at(0, i)
        down = mgf[here, :].astype(f32) * query[here, :]
        sig[row_at(0, i), :] = (down * half1).astype(bf16)
        sig[row_at(1, i), :] = (down * half2).astype(bf16)
        return carry

    lax.fori_loop(0, own // row_tile, grad_rows, 0)

    def grad_freq(j, carry):
        re_at, im_at = freq_at(j)
        re = nn(sig[0 : 2 * own, :], tab[:, re_at])
        im = nn(sig[0 : 2 * own, :], tab[:, im_at])
        hr, hi = hat[:, re_at].astype(f32), hat[:, im_at].astype(f32)
        kr, ki = hr[:own], hi[:own]
        kg_re, kg_im = 0.0, 0.0
        for h in range(2):
            mr, mi = re[own * h : own * (h + 1)], im[own * h : own * (h + 1)]
            sr, si = hr[own * (h + 1) : own * (h + 2)], hi[own * (h + 1) : own * (h + 2)]
            prod[own * h : own * (h + 1), re_at] = (kr * mr + ki * mi).astype(bf16)
            prod[own * h : own * (h + 1), im_at] = (kr * mi - ki * mr).astype(bf16)
            kg_re = kg_re + sr * mr + si * mi
            kg_im = kg_im + sr * mi - si * mr
        prod[2 * own : 3 * own, re_at] = kg_re.astype(bf16)
        prod[2 * own : 3 * own, im_at] = kg_im.astype(bf16)
        return carry

    lax.fori_loop(0, freq // lane_tile, grad_freq, 0)
    big_step(1)

    def grad_time(j, carry):
        at = token(j)
        all3 = nt(prod[...], tab[at, :])
        sgr[:, at] = (all3[:own] * masks[0:1, at] + all3[own : 2 * own] * masks[1:2, at]) * (1.0 / freq)
        kgr[:, at] = all3[2 * own :] * (1.0 / freq)
        return carry

    lax.fori_loop(0, ways, grad_time, 0)
    big_step(0)

    def sum_slot(index, at, size):
        if index < seq // 128:
            return query.at[pl.ds(at, size), 128 * index : 128 * index + 128]
        index = index - seq // 128
        return n2own.at[pl.ds(own * (index % ways) + at, size), 128 * (index // ways) : 128 * (index // ways) + 128]

    def ahead2(values, steps):
        if steps == 0:
            return values
        return jnp.where(lane2 < seq - steps, pltpu.roll(values, seq - steps, 1), 0.0)

    def chain_rows(i, carry):
        at = pl.multiple_of(i * tall, tall)
        here, here1, here2 = (pl.ds(pl.multiple_of(j * own + i * tall, tall), tall) for j in range(3))
        tap = cols[here, :]

        def note(index, values):
            sum_slot(index, at, tall)[...] = sum(values[:, 128 * b : 128 * b + 128] for b in range(seq // 128))

        key, value = kv[here, :], kv[here1, :]
        kgrad = jnp.where(lane2 < lags, kgr[here, :], 0.0)
        base_grad = kgrad * (jnp.exp(-tap[:, 12:13] * place2) * (1.0 / math.sqrt(seq)))
        kgr[here, :] = base_grad
        note(12, -kgrad * kern[here, :] * place2)
        bent = squash[here, :]
        cond_grad = base_grad * (1.0 - bent * bent)
        sgrad = sgr[here, :]
        value_grad = sgrad * key
        for k in range(3):
            moved = ahead2(cond_grad, k)
            note(9 + k, moved * value)
            value_grad = value_grad + tap[:, 9 + k : 10 + k] * moved
        branch = (mgf[here, :].astype(f32) * mixed[here, :], sgrad * value, value_grad)
        for j, rows_at in enumerate((here, here1, here2)):
            part = proj[rows_at, :]
            total = 0.0
            for k in range(3):
                moved = ahead2(branch[j], k)
                note(3 * k + j, moved * part)
                total = total + tap[:, 3 * k + j : 3 * k + j + 1] * moved
            sig[rows_at, :] = total.astype(bf16)
        return carry

    lax.fori_loop(0, own // tall, chain_rows, 0)
    big_step(1)

    def finish_sums():
        ones_square = jnp.ones((128, 128), f32)

        def run(i, carry):
            at = pl.multiple_of(i * 64, 64)
            column = lax.broadcasted_iota(jnp.int32, (64, 128), 1)
            stat = jnp.zeros((64, 128), f32)
            for index in range(13):
                stat = jnp.where(column == index, nn(sum_slot(index, at, 64)[...], ones_square, highest), stat)
            sm[pl.ds(at, 64), :] = stat
            return carry

        lax.fori_loop(0, own // 64, run, 0)


    h_sum = LineSum(
        lambda dest, sub: tbuf.at[own_rows(dest), token(sub)],
        lambda way, k, sub: tin.at[way, k, own_rows(sub), :],
        hs_send, hs_recv, z, ways, ways)
    f_sum.drain()
    mom_msg = Direct(lambda to: mom.at[z], lambda at: mom.at[at], mom_send, mom_recv)

    def in_back(tile):
        at = token(tile)
        rres[...] = tn(in_t[...], sig[:, at])
        tbuf[:, at] = rres[...].astype(bf16)
        h_sum.first(0, (tile, tile), False)
        normed = (xf[:, at].astype(f32) - stat1[0:1, at]) * stat1[1:2, at]
        upstream = rres[...] * gaincol[:, 0:1]
        mom[z, 0:1, at] = jnp.sum(upstream, axis=0, keepdims=True)
        mom[z, 1:2, at] = jnp.sum(upstream * normed, axis=0, keepdims=True)
        gsum[tile] = nt(ones, (rres[...] * normed).astype(bf16))

    gb2 = gg.at[0 : 4 * own, 0:width]
    sum2 = mid.at[0 : 4 * own, 0:width]

    def proj_grad(lhs, rhs, place_at):
        def run(j, carry):
            gb2[pl.ds(pl.multiple_of(place_at + j * own, row_tile), own), :] = nt(
                lhs[pl.ds(pl.multiple_of(j * own, row_tile), own), :], rhs[...]).astype(bf16)
            return carry

        lax.fori_loop(0, lhs.shape[0] // own, run, 0)

    two = RowSum(gb2, sum2, rb2, rbx2, ar_send.at[2], ar_recv.at[2], r, all_bits)
    two_tasks = two.tasks()

    dp_rows, all_rows = pl.ds(0, own), pl.ds(own, 80)

    def small_copy(chain, b):
        at = (dp_rows, all_rows)[chain]
        return pltpu.make_async_remote_copy(
            src_ref=sm.at[at], dst_ref=smbox.at[b, at], send_sem=sm_send.at[chain, b], recv_sem=sm_recv.at[chain, b],
            device_id={"dp": flipped(r, b)}, device_id_type=MESH,
        )

    def small_step(chain, b):
        at = (dp_rows, all_rows)[chain]
        small_copy(chain, b).wait()
        sm[at, :] += smbox[b, at, :]
        if b + 1 < all_bits:
            small_copy(chain, b + 1).start()

    def near(summer, k, index):
        summer.near(k, by_end(index) if summer is e_sum else plain_order[index])

    def far(summer, k, index):
        summer.far(k, by_end(index) if summer is e_sum else plain_order[index])

    total = rres.at[0:own, :]

    def output_part(tile):
        at = token(tile)
        total[...] = mbuf[span, at].astype(f32)
        for way in (0, 1):
            e_sum.take(way, tile, total)
        resown[:, at] = (resown[:, at] + total[...]) * masks[2:3, at]

    def input_part(tile):
        at = token(tile)
        total[...] = tbuf[span, at].astype(f32)
        for way in (0, 1):
            h_sum.take(way, tile, total)
        sums = sum(mom[s, :, at] for s in range(ways)) * (1.0 / width)
        inverse = stat1[1:2, at]
        normed = (xf[span, at].astype(f32) - stat1[0:1, at]) * inverse
        upstream = total[...] * gaincol[span, 0:1]
        sgr[:, at] = pgo[:, at].astype(f32) + inverse * (upstream - sums[0:1, :] - normed * sums[1:2, :])
        save(sgr.at[:, at], igrad_hbm.at[:, at])

    def in_turn(tile, carry):
        in_back(tile)
        return carry

    lax.fori_loop(0, ways, in_turn, 0)
    big_step(0)
    for index in every:
        h_sum.note_first(0, plain_order[index])
    mom_msg.start()
    swap_proj.wait_recv()
    proj_grad(sig, n1o, 0)
    proj_grad(pgo, mixf, 3 * own)
    two_tasks.pop(0)()
    for index in every:
        h_sum.first(1, plain_order[index])
    for index in first_two:
        far(e_sum, 0, index)
    for k in range(ways - 2):
        near(e_sum, k, 2)

    wave_grad = tn(cols[:, 64:128], kgr[...], highest) * jnp.cos(arg[...])
    finish_sums()
    two_tasks.pop(0)()
    for index in every:
        near(h_sum, 0, index)
    sm[0:own, 64:128] = nt(kgr[...], jnp.sin(arg[...]), highest)
    sm[own : own + 64, 0:64] = nt(feat_ref[...], wave_grad, highest)
    sm[own : own + 64, 64:128] = jnp.zeros((64, 64), f32)
    sm[own + 64 :, :] = jnp.zeros((16, 128), f32)
    for b in range(width // 128):
        lanes = slice(128 * b, 128 * b + 128)
        sm[own + 64 + b : own + 65 + b, :] = sum(gsum[tile, 0:1, lanes] for tile in range(ways))
        sm[own + 72 + b : own + 73 + b, :] = gsum[ways, 0:1, lanes]
    small_copy(0, 0).start()
    z_msg = Direct(lambda to: zbox.at[z], lambda at: zbox.at[at], z_send, z_recv)
    zbox[z] = sm[own:, :]
    z_msg.start()
    two_tasks.pop(0)()
    big_step(0)
    big_step(1)
    small_step(0, 0)
    for k in range(ways - 2):
        e_sum.first(k, by_end(3))
    two_tasks.pop(0)()
    for index in every:
        h_sum.first(2, plain_order[index])
    for index in range(1, ways):
        e_sum.first(ways - 2, by_end(index))
    two_tasks.pop(0)()
    for index in every:
        near(h_sum, 1, index)
    for index in every:
        far(h_sum, 0, index)
    for k in range(ways - 2):
        near(e_sum, k, 3)
    z_msg.wait_recv()
    zsum = zbox[0]
    for other in range(1, ways):
        zsum = zsum + zbox[other]
    sm[own:, :] = zsum
    small_copy(1, 0).start()
    small_step(0, 1)
    small_step(1, 0)
    far(e_sum, 0, 2)
    two_tasks.pop(0)()
    for b in range(2, all_bits):
        small_step(0, b)
    far(e_sum, 0, 3)
    big_step(1)
    small_step(1, 1)
    big_step(0)
    two_tasks.pop(0)()
    save(sum2, proj_hbm)
    for b in range(2, all_bits):
        small_step(1, b)
    save(sm, small_hbm)
    big_step(1)
    big_step(0)
    save(weights, big_hbm)
    mom_msg.wait_recv()
    input_part(0)
    input_part(1)
    input_part(2)
    input_part(3)
    def output_turn(tile, carry):
        output_part(tile)
        return carry

    lax.fori_loop(0, ways, output_turn, 0)
    save(resown, out_hbm)

    for line in (in_line, g_line, mix_line, e_sum, h_sum, gain_msg, piece_msg, swap_mix, swap_proj, mom_msg, z_msg, big_parts[0], big_parts[1], two):
        line.drain()
    for make, piece in piece_sends:
        make(piece).wait_send()
    for copy in saves:
        copy.wait()


def layer(cfg, x_own, g_own, out_t, in_t, table, w_gate, w_up, w_down, halves, gain1, gain2, short_taps, cond_taps, rates,
          filter_in, filter_bias, filter_out, feats):
    ways, seq, own, width, hidden, bits, all_bits = cfg
    period = 3 * seq // 2
    block = seq // ways
    big_rows = hidden + 2 * width
    assert hidden == width
    held = dict(
        xf=((width, seq), bf16), gf=((width, seq), bf16), outt=((width, width), bf16), proj=((3 * own, seq), f32),
        mixf=((width, seq), bf16), query=((own, seq), f32), kv=((2 * own, seq), f32), squash=((own, seq), f32), kern=((own, seq), f32),
        mixed=((own, seq), f32), hat=((3 * own, period), bf16), arg=((64, seq), f32), in_t=((3 * own, width), bf16),
        tab=((seq, period), bf16), n1o=((width, seq), bf16), masks=((8, seq), f32), cols=((own, 128), f32),
        prow=((128, 256), f32), frow=((64, 64), f32),
        pieces=((1 << bits, ways, own * width // 128 // (1 << bits), 128), bf16), gains=((ways, 8, 256), f32),
        gaincol=((width, 128), f32), stat1=((8, seq), f32), sig=((3 * own, seq), bf16), prod=((3 * own, period), bf16),
        weights=((big_rows, width), bf16), n2o=((width, seq), bf16),
        mid=((hidden, seq), bf16), gg=((hidden, seq), bf16), ug=((hidden, seq), bf16), tbuf=((width, seq), bf16),
        tin=((2, ways - 1, width, block), bf16), mbuf=((width, seq), bf16), ein=((2, ways - 1, own, seq), bf16),
        gb=((big_rows, width), bf16), rb=((big_rows * 7 // 8, width), bf16),
        rbx=((max(all_bits - 3, 1), big_rows // 8 if all_bits > 3 else 32, width), bf16),
        rb2=((4 * own * 7 // 8, width), bf16),
        rbx2=((max(all_bits - 3, 1), 4 * own // 8 if all_bits > 3 else 16, width), bf16),
        n2own=((width, block), f32), inv2=((8, block), f32), rres=((width, block), f32), resown=((own, seq), f32),
        pgb=((width, block), bf16), mgb=((width, block), bf16), mgf=((own, seq), bf16), pgo=((own, seq), bf16),
        sgr=((own, seq), f32), kgr=((own, seq), f32), sm=((own + 80, 128), f32),
        smbox=((all_bits, own + 80, 128), f32), zbox=((ways, 80, 128), f32),
        mom=((ways, 8, seq), f32), gsum=((ways + 1, 8, width), f32),
    )
    hops = (3, 2, ways - 1, ways)
    sems = dict(
        load_sem=(11,), line_send=hops, line_recv=hops, piece_send=(ways + (1 << bits),), piece_recv=(ways + (1 << bits),),
        gain_send=(ways,), gain_recv=(ways,), save_sem=(8,), fs_send=(2, ways - 1, 2), fs_recv=(2, ways - 1, 2),
        es_send=(2, ways - 1, ways), es_recv=(2, ways - 1, ways), hs_send=(2, ways - 1, ways), hs_recv=(2, ways - 1, ways),
        sw_send=(2, ways), sw_recv=(2, ways), pace_sem=None, ar_send=(3, 3 + max(all_bits, 3)), ar_recv=(3, 3 + max(all_bits, 3)),
        sm_send=(2, all_bits), sm_recv=(2, all_bits), z_send=(ways,), z_recv=(ways,), mom_send=(ways,), mom_recv=(ways,),
    )
    here = pl.BlockSpec(memory_space=pltpu.VMEM)
    there = pl.BlockSpec(memory_space=pl.ANY)
    outs = [
        ((own, seq), f32), ((own, seq), f32), ((big_rows, width), bf16), ((4 * own, width), bf16),
        ((own + 80, 128), f32),
    ]
    return pl.pallas_call(
        functools.partial(layer_kernel, cfg),
        out_shape=[jax.ShapeDtypeStruct(s, t) for s, t in outs],
        in_specs=[there] * 8 + [pl.BlockSpec(memory_space=pltpu.SMEM)] + [here] * 9,
        out_specs=[there] * len(outs),
        scratch_shapes=[pltpu.VMEM(s, t) for s, t in held.values()] + [
            pltpu.SemaphoreType.REGULAR if s is None else pltpu.SemaphoreType.DMA(s) for s in sems.values()],
        compiler_params=pltpu.CompilerParams(collective_id=0, has_side_effects=True, vmem_limit_bytes=64 << 20),
    )(x_own, g_own, out_t, in_t, table, w_gate, w_up, w_down, halves, gain1, gain2, short_taps, cond_taps, rates,
      filter_in, filter_bias, filter_out, feats)


def widen_kernel(
    cfg, count, out_in, igrad_in, big_in, two_in, small_ref,
    out_hbm, igrad_hbm, wd_hbm, wg_hbm, wu_hbm, in_hbm, outp_hbm, gain1_ref, gain2_ref, short_ref, cond_ref, rate_ref,
    fin_ref, fbias_ref, fout_ref, low, wide, through, in_sem, out_sem, copy_sem,
):
    ways, seq, own, width, hidden, bits, all_bits = cfg
    step = own
    sources = [(big_in, at) for at in range(0, hidden + 2 * width, step)] + [(two_in, at) for at in range(0, 4 * own, step)]
    targets = [
        (ref, at) for ref, size in ((wd_hbm, hidden), (wg_hbm, width), (wu_hbm, width), (in_hbm, 3 * own), (outp_hbm, own))
        for at in range(0, size, step)]
    loads = [
        pltpu.make_async_copy(src.at[pl.ds(at, step)], low.at[i], in_sem.at[i]) for i, (src, at) in enumerate(sources)]
    for copy in loads:
        copy.start()
    ins = [pltpu.make_async_copy(src, through.at[i], copy_sem.at[i]) for i, src in enumerate((out_in, igrad_in))]
    for copy in ins:
        copy.start()
    moves = []
    stats = small_ref[0:own, :].T
    for i in range(3):
        for j in range(3):
            short_ref[i, j : j + 1, :] = stats[3 * i + j : 3 * i + j + 1, :]
    cond_ref[...] = stats[9:12, :]
    rate_ref[...] = stats[12:13, :]
    fout_ref[...] = stats[64:128, :]
    fin_ref[...] = small_ref[own : own + count, 0:64]
    fbias_ref[...] = small_ref[own + count : own + count + 1, 0:64]
    shift = (width - own * lax.axis_index("chan")) % width
    for first, ref in ((64, gain1_ref), (72, gain2_ref)):
        row = jnp.concatenate([small_ref[own + first + b : own + first + b + 1, :] for b in range(width // 128)], axis=1)
        ref[...] = pltpu.roll(jnp.broadcast_to(row, (8, width)), shift, 1)[0:1, 0:own]
    for i, ref in enumerate((out_hbm, igrad_hbm)):
        ins[i].wait()
        copy = pltpu.make_async_copy(through.at[i], ref, copy_sem.at[2 + i])
        copy.start()
        moves.append(copy)
    for i, (ref, at) in enumerate(targets):
        loads[i].wait()
        wide[i] = low[i].astype(f32)
        copy = pltpu.make_async_copy(wide.at[i], ref.at[pl.ds(at, step)], out_sem.at[i])
        copy.start()
        moves.append(copy)
    for copy in moves:
        copy.wait()


def widen(cfg, count, output, input_grad, big, two, small):
    ways, seq, own, width, hidden, bits, all_bits = cfg
    here = pl.BlockSpec(memory_space=pltpu.VMEM)
    there = pl.BlockSpec(memory_space=pl.ANY)
    far = [(own, seq), (own, seq), (hidden, width), (width, hidden), (width, hidden), (3 * own, width), (own, width)]
    near = [(1, own), (1, own), (3, 3, own), (3, own), (1, own), (count, 64), (1, 64), (64, own)]
    steps = (hidden + 2 * width + 4 * own) // own
    dma = pltpu.SemaphoreType.DMA
    return pl.pallas_call(
        functools.partial(widen_kernel, cfg, count),
        out_shape=[jax.ShapeDtypeStruct(shape, f32) for shape in far + near],
        in_specs=[there] * 4 + [here],
        out_specs=[there] * len(far) + [here] * len(near),
        scratch_shapes=[
            pltpu.VMEM((steps, own, width), bf16), pltpu.VMEM((steps, own, width), f32),
            pltpu.VMEM((2, own, seq), f32), dma((steps,)), dma((steps,)), dma((4,))],
        compiler_params=pltpu.CompilerParams(vmem_limit_bytes=64 << 20),
    )(output, input_grad, big, two, small)


def local(
    hidden_in, halves, norm1_gain, in_proj, short_taps, cond_taps, filter_in, filter_bias,
    filter_out, decay_rate, out_proj, norm2_gain, w_gate, w_up, w_down, out_grad,
):
    seq, own = hidden_in.shape[1], hidden_in.shape[2]
    ways, rows = lax.axis_size("chan"), lax.axis_size("dp")
    width, hidden = own * ways, w_gate.shape[1]
    z = lax.axis_index("chan")
    all_bits = rows.bit_length() - 1
    cfg = (ways, seq, own, width, hidden, 3, all_bits)
    count = filter_in.shape[0]
    feat_np = np.concatenate([
        band_features(seq, count), np.ones((1, seq), np.float32), np.zeros((63 - count, seq), np.float32)])
    table = jnp.asarray(wave_matrix(seq).astype(np.float32)).astype(bf16)

    output, input_grad, big, two, small = layer(
        cfg, hidden_in[0].T, out_grad[0].T, out_proj.T, in_proj.transpose(1, 2, 0).reshape(3 * own, width), table,
        w_gate, w_up, w_down, halves, norm1_gain[None], norm2_gain[None], short_taps, cond_taps, decay_rate[None],
        filter_in, filter_bias[None], filter_out, jnp.asarray(feat_np))

    (output, input_grad, wd_sum, wg_sum, wu_sum, in_sum, out_sum, gain1, gain2, short, cond, rates, fin, fbias, fout) = widen(
        cfg, count, output, input_grad, big, two, small)
    return (
        output.T[None], input_grad.T[None], gain1[0], in_sum.reshape(3, own, width).transpose(2, 0, 1), short, cond, fin,
        fbias[0], fout, rates[0], out_sum.T, gain2[0], wg_sum, wu_sum, wd_sum,
    )


def solution(mesh):
    rows, cols = P("dp", None, "chan"), P(None, "chan")
    in_specs = (
        rows, P("dp", None), P("chan"), P(None, None, "chan"), P(None, None, "chan"), cols, P(), P(),
        cols, P("chan"), cols, P("chan"), cols, cols, P("chan", None), rows,
    )
    out_specs = (
        rows, rows, P("chan"), P(None, None, "chan"), P(None, None, "chan"), cols, P(), P(),
        cols, P("chan"), cols, P("chan"), cols, cols, P("chan", None),
    )
    return jax.shard_map(local, mesh=mesh, in_specs=in_specs, out_specs=out_specs, check_vma=False)
```
